32 devices in a mesh: expert: 4 (over z), tensor: 8 (over y, x, core).
Axes of the slice: x: 2, y: 2, z: 4, core: 2. Of those that a mesh axis runs over, the one named last changes fastest.
Arguments:
- tokens: bfloat16 [12288, 1024], P(('expert', 'tensor')), may hold values from -6 to 6
- cotangent: bfloat16 [12288, 1024], P(('expert', 'tensor')), may hold values from -6 to 6
- doc_lengths: int32 [4, 5], P('expert'), may hold values from 1 to 1024, 3072 in all within a row
- expert_choices: int32 [12288, 8], P(('expert', 'tensor')), may hold values from 0 to 31, all different within a row; in each aligned block of 384 rows (0 to 383, 384 to 767, ...) at most 192 rows name the same one
- gains: float32 [2, 1024], replicated, may hold values from 0.5 to 1.5
- gain_moment: float32 [2, 1024], replicated, may hold values from -112 to 112
- gain_square: float32 [2, 1024], replicated, may hold values from 1474.56 to 5775.36
- router: float32 [1024, 32], replicated, may hold values from -0.09375 to 0.09375
- router_moment: float32 [1024, 32], replicated, may hold values from -320 to 320
- router_square: float32 [1024, 32], replicated, may hold values from 10444.8 to 41164.8
- w_attention: float32 [1024, 8, 256], P(None, 'tensor'), may hold values from -0.1875 to 0.1875
- attention_moment: float32 [1024, 8, 256], P(None, 'tensor'), may hold values from -64 to 64
- attention_square: float32 [1024, 8, 256], P(None, 'tensor'), may hold values from 651.264 to 2580.48
- w_out: float32 [8, 128, 1024], P('tensor'), may hold values from -1.5 to 1.5
- out_moment: float32 [8, 128, 1024], P('tensor'), may hold values from -6 to 6
- out_square: float32 [8, 128, 1024], P('tensor'), may hold values from 14.7456 to 57.7536
- w_gate_up: float32 [32, 2, 1024, 512], P('expert', None, None, 'tensor'), may hold values from -0.1875 to 0.1875
- gate_up_moment: float32 [32, 2, 1024, 512], P('expert', None, None, 'tensor'), may hold values from -6 to 6
- gate_up_square: float32 [32, 2, 1024, 512], P('expert', None, None, 'tensor'), may hold values from 14.4384 to 58.368
- w_down: float32 [32, 512, 1024], P('expert', 'tensor'), may hold values from -1 to 1
- down_moment: float32 [32, 512, 1024], P('expert', 'tensor'), may hold values from -6 to 6
- down_square: float32 [32, 512, 1024], P('expert', 'tensor'), may hold values from 1.04448 to 3.9936
Outputs:
- mixed: float32 [12288, 1024], P(('expert', 'tensor'))
- input_grad: float32 [12288, 1024], P(('expert', 'tensor'))
- gain_first: float32 [2, 1024], replicated
- gain_second: float32 [2, 1024], replicated
- gain_new: float32 [2, 1024], replicated
- router_first: float32 [1024, 32], replicated
- router_second: float32 [1024, 32], replicated
- router_new: float32 [1024, 32], replicated
- attention_first: float32 [1024, 8, 256], P(None, 'tensor')
- attention_second: float32 [1024, 8, 256], P(None, 'tensor')
- attention_new: float32 [1024, 8, 256], P(None, 'tensor')
- out_first: float32 [8, 128, 1024], P('tensor')
- out_second: float32 [8, 128, 1024], P('tensor')
- out_new: float32 [8, 128, 1024], P('tensor')
- gate_up_first: float32 [32, 2, 1024, 512], P('expert', None, None, 'tensor')
- gate_up_second: float32 [32, 2, 1024, 512], P('expert', None, None, 'tensor')
- gate_up_new: float32 [32, 2, 1024, 512], P('expert', None, None, 'tensor')
- down_first: float32 [32, 512, 1024], P('expert', 'tensor')
- down_second: float32 [32, 512, 1024], P('expert', 'tensor')
- down_new: float32 [32, 512, 1024], P('expert', 'tensor')
The draws below stay inside these ranges and needn't reach their ends.
Inputs may be any that keep to these rules, and one draw needn't show every extreme that they name: `expert_choices`: in the rows of one device no expert is named by more than 192 rows, a bound that some block reaches. `doc_lengths`: each row sums to 3072; the largest entry of each row is 1024.
All inputs are finite; a program needn't handle non-finite values.
Results may differ from the reference program's by a relative error of at most 0.025.
Values may be sent and summed in bfloat16 or wider, within the bound.
No kernel may reach another device: no remote copies, remote signals or barrier semaphores. Data moves between devices by JAX's collectives and lax.ppermute only.
A program may use at most 256 MiB of HBM per device.

```python
import math
from functools import partial
import jax
import jax.numpy as jnp
import numpy as np
from jax import lax

D = 1024
H = 16
KV = 8
HD = 64
FF = 512
EXPERTS = 32
TOPK = 8
G = 2
TOK_DEV = 384
QBLOCK = 512
STEP = 10
TOK_GRP = 3072
GROUPS = 4
TOKENS = 12288
DOC_MOST = 1024
DOCS = 5
CAP = 192


def steps_of(stream_key, dims, split, least, top_value):
    level = 1.0
    for axis_at, blocks in split:
        steps = jax.random.uniform(jax.random.fold_in(jax.random.fold_in(stream_key, 6), axis_at), (blocks,), jnp.float32, least / len(split), top_value / len(split))
        level = level * jnp.repeat(jnp.exp(steps), dims[axis_at] // blocks).reshape((-1,) + (1,) * (len(dims) - 1 - axis_at))
    return level


def length_profile(number_of, total, reach, lean):
    portions = [(1 << 20) // math.isqrt(rank ** lean) + 1 for rank in range(2, number_of + 1)]
    rest, holding = total - reach - (number_of - 1), [1] * (number_of - 1)
    while rest > 0:
        candidates = [i for i in range(number_of - 1) if holding[i] < reach]
        whole, budget = sum([portions[i] for i in candidates]), rest
        for i in candidates:
            more = min(reach - holding[i], max(1, budget * portions[i] // whole), rest)
            holding[i] = holding[i] + more
            rest = rest - more
    return np.array([reach] + holding)


def ragged(rng, number_of, total, reach, skew):
    if number_of == 2:
        one = jax.random.randint(rng, (), max(1, total - reach), min(reach, total - 1) + 1)
        return jnp.stack([one, total - one])
    sizes = jnp.asarray(length_profile(number_of, total, reach, skew), jnp.int32)
    twos = (number_of - 1) // 2
    giver, taker = sizes[1:1 + 2 * twos:2], sizes[2:2 + 2 * twos:2]
    room = jnp.minimum(giver - 1, reach - taker)
    moved = jax.random.randint(jax.random.fold_in(rng, 1), (twos,), 0, 1 << 20) % (room + 1)
    sizes = sizes.at[1:1 + 2 * twos:2].set(giver - moved).at[2:2 + 2 * twos:2].set(taker + moved)
    return sizes[jax.random.permutation(jax.random.fold_in(rng, 2), number_of)]


def routed_block(key, own, number, rows, count, top, most, lean):
    sequence = jax.random.permutation(key, count)
    packed, ordinary = load_shares(count, rows * top, most, lean, True), load_shares(count, rows * top, most, lean, False)
    places = jnp.arange(count)

    def named(tallies, turn):
        used = int((tallies > 0).sum())
        fixed = max(1, used // 4)
        moved = fixed + (places - fixed + turn * (used - fixed)) % max(1, count - fixed)
        return jnp.zeros((count,), jnp.int32).at[sequence[jnp.where(places < fixed, places, moved)]].set(jnp.asarray(tallies, jnp.int32))

    tallies = jnp.where(number % 4 == 0, named(packed, number // 4), named(ordinary, number - number // 4 - 1))
    mixed = jax.random.permutation(jax.random.fold_in(own, 3), count)
    donor, sink = mixed[0:count // 2 * 2:2], mixed[1:count // 2 * 2:2]
    margin = jnp.minimum(tallies[donor] - 1, most - tallies[sink]) // 2
    margin = jnp.where((donor == sequence[0]) | (sink == sequence[0]) | (tallies[sink] == 0), 0, jnp.maximum(margin, 0))
    moved = jax.random.randint(jax.random.fold_in(own, 4), (count // 2,), 0, 1 << 20) % (margin + 1)
    tallies = tallies.at[donor].add(-moved).at[sink].add(moved)
    members = jnp.searchsorted(jnp.cumsum(tallies), jnp.arange(rows * top), side="right").astype(jnp.int32)
    listing = members.reshape(top, rows).T
    listing = listing[jax.random.permutation(jax.random.fold_in(own, 1), rows)]
    turn = jax.random.randint(jax.random.fold_in(own, 2), (rows, 1), 0, top)
    return jnp.take_along_axis(listing, (jnp.arange(top)[None, :] + turn) % top, axis=1)


def load_shares(amount, total, bound, skew, full):
    loads = [(1 << 20) // math.isqrt(standing ** skew) + 1 for standing in range(1, amount + 1)]
    largest = bound if full else min(bound, max(-(-total // amount), total * loads[0] // sum(loads)))
    least = 1 if total - largest >= amount - 1 else 0
    holding, spare = [largest] + [least] * (amount - 1), total - largest - least * (amount - 1)
    while spare > 0:
        free = [i for i in range(1, amount) if holding[i] < largest] or [i for i in range(1, amount) if holding[i] < bound]
        whole, left = sum([loads[i] for i in free]), spare
        for i in free:
            addition = min(bound - holding[i], max(1, left * loads[i] // whole), spare)
            holding[i] = holding[i] + addition
            spare = spare - addition
    return np.array(holding)


def noise(own_key, extent, deviation, reach, shards=(), held_as=jnp.bfloat16):
    drawn = jax.random.normal(own_key, extent, jnp.float32) * deviation
    if len(shards) > 0:
        drawn = steps_of(own_key, extent, shards, -0.22, 0.18) * drawn
    return jnp.clip(drawn, min=-reach, max=reach).astype(held_as)


def setup_inputs(seed: int = 0) -> dict:
    seeds = jax.random.split(jax.random.key(seed), 23)
    tokens = noise(seeds[0], (TOKENS, D), 1.0, 6.0, ((0, 32),))
    cotangent = noise(seeds[1], (TOKENS, D), 1.0, 6.0, ((0, 32),))
    doc_lengths = jax.vmap(lambda own: ragged(own, DOCS, TOK_GRP, DOC_MOST, 2))(jax.random.split(seeds[2], GROUPS)).reshape((GROUPS, DOCS)).astype(jnp.int32)
    expert_choices_keys = jax.random.split(jax.random.fold_in(seeds[3], 1), TOKENS // TOK_DEV)
    expert_choices_turns = jax.random.permutation(jax.random.fold_in(seeds[3], 3), TOKENS // TOK_DEV)
    expert_choices = jax.vmap(lambda own, number: routed_block(jax.random.fold_in(seeds[3], 2), own, number, TOK_DEV, EXPERTS, TOPK, CAP, 2))(expert_choices_keys, expert_choices_turns).reshape((TOKENS, TOPK))
    gains = jnp.clip(1.0 + 0.1 * jax.random.normal(seeds[4], (2, D), jnp.float32), 0.5, 1.5)
    gain_moment = noise(seeds[5], (2, D), (0.16 * TOKENS ** 0.5), 112.0, (), jnp.float32)
    gain_square = jnp.clip(jnp.exp(jax.random.uniform(seeds[6], (2, D), jnp.float32, math.log(1474.56), math.log(5775.36))), 1474.56, 5775.36)
    router = noise(seeds[7], (D, EXPERTS), (4 * D) ** -0.5, 0.09375, (), jnp.float32)
    router_moment = noise(seeds[8], (D, EXPERTS), (0.9 * (TOKENS * TOPK // EXPERTS) ** 0.5), 320.0, (), jnp.float32)
    router_square = jnp.clip(jnp.exp(jax.random.uniform(seeds[9], (D, EXPERTS), jnp.float32, math.log(10444.8), math.log(41164.8))), 10444.8, 41164.8)
    w_attention = noise(seeds[10], (D, KV, (G + 2) * HD), D ** -0.5, 0.1875, ((1, 8),), jnp.float32)
    attention_moment = noise(seeds[11], (D, KV, (G + 2) * HD), (0.11 * TOKENS ** 0.5), 64.0, ((1, 8),), jnp.float32)
    attention_square = jnp.clip(jnp.exp(math.log(2580.48) - 1.37681564 * jax.random.uniform(seeds[12], (D, KV, (G + 2) * HD), jnp.float32) ** steps_of(seeds[12], (D, KV, (G + 2) * HD), ((1, 8),), -0.2, 0.2)), 651.264, 2580.48)
    w_out = noise(seeds[13], (KV, G * HD, D), (H * HD // 64) ** -0.5, 1.5, ((0, 8),), jnp.float32)
    out_moment = noise(seeds[14], (KV, G * HD, D), (0.017 * TOKENS ** 0.5), 6.0, ((0, 8),), jnp.float32)
    out_square = jnp.clip(jnp.exp(math.log(57.7536) - 1.36524099 * jax.random.uniform(seeds[15], (KV, G * HD, D), jnp.float32) ** steps_of(seeds[15], (KV, G * HD, D), ((0, 8),), -0.2, 0.2)), 14.7456, 57.7536)
    w_gate_up = noise(seeds[16], (EXPERTS, 2, D, FF), D ** -0.5, 0.1875, ((0, 4), (3, 8)), jnp.float32)
    gate_up_moment = noise(seeds[17], (EXPERTS, 2, D, FF), (0.033 * (TOKENS * TOPK // EXPERTS) ** 0.5), 6.0, ((0, 4), (3, 8)), jnp.float32)
    gate_up_square = jnp.clip(jnp.exp(math.log(58.368) - 1.3968765 * jax.random.uniform(seeds[18], (EXPERTS, 2, D, FF), jnp.float32) ** steps_of(seeds[18], (EXPERTS, 2, D, FF), ((0, 4), (3, 8)), -0.2, 0.2)), 14.4384, 58.368)
    w_down = noise(seeds[19], (EXPERTS, FF, D), (FF // 16) ** -0.5, 1.0, ((0, 4), (1, 8)), jnp.float32)
    down_moment = noise(seeds[20], (EXPERTS, FF, D), (0.009 * (TOKENS * TOPK // EXPERTS) ** 0.5), 6.0, ((0, 4), (1, 8)), jnp.float32)
    down_square = jnp.clip(jnp.exp(math.log(3.9936) - 1.3411739 * jax.random.uniform(seeds[21], (EXPERTS, FF, D), jnp.float32) ** steps_of(seeds[21], (EXPERTS, FF, D), ((0, 4), (1, 8)), -0.2, 0.2)), 1.04448, 3.9936)
    return {"tokens": tokens, "cotangent": cotangent, "doc_lengths": doc_lengths, "expert_choices": expert_choices, "gains": gains, "gain_moment": gain_moment, "gain_square": gain_square, "router": router, "router_moment": router_moment, "router_square": router_square, "w_attention": w_attention, "attention_moment": attention_moment, "attention_square": attention_square, "w_out": w_out, "out_moment": out_moment, "out_square": out_square, "w_gate_up": w_gate_up, "gate_up_moment": gate_up_moment, "gate_up_square": gate_up_square, "w_down": w_down, "down_moment": down_moment, "down_square": down_square}


@jax.custom_vjp
def low(v):
    return lax.optimization_barrier(v.astype(jnp.bfloat16)).astype(jnp.float32)

@jax.custom_vjp
def low_back(v):
    return v

def low_keep(v):
    return (low(v), None)

def low_pass(kept, grad):
    return (grad,)

def back_keep(v):
    return (v, None)

def back_low(kept, grad):
    return (low(grad),)
low.defvjp(low_keep, low_pass)
low_back.defvjp(back_keep, back_low)
norm_eps = 1e-06
rope_base = 10000.0
masked_score = -1e+30
beta_one = 0.9
beta_two = 0.95
adam_eps = 1e-08
decay_rate = 0.1
highest = lax.Precision.HIGHEST

def rms_norm(values, gain):
    return values * lax.rsqrt(lax.optimization_barrier(jnp.mean(values * values, axis=-1, keepdims=True)) + norm_eps) * gain

def rotate(values, position, sign):
    half = values.shape[-1] // 2
    frequency = rope_base ** (-jnp.arange(half, dtype=jnp.float32) * 2.0 / values.shape[-1])
    angles = sign * position.astype(jnp.float32)[:, None] * frequency[None, :]
    cosine = jnp.cos(angles)[:, None, :]
    sine = jnp.sin(angles)[:, None, :]
    first = values[..., :half]
    second = values[..., half:]
    return jnp.concatenate([first * cosine - second * sine, second * cosine + first * sine], axis=-1)

def doc_table(lengths, count):
    lengths = lengths.astype(jnp.int32)
    ends = jnp.cumsum(lengths).astype(jnp.int32)
    places = jnp.arange(count, dtype=jnp.int32)
    after = (places[:, None] >= ends[None, :]).astype(jnp.int32)
    document = lax.optimization_barrier(jnp.sum(after, axis=1)).astype(jnp.int32)
    starts = lax.optimization_barrier(jnp.sum(after * lengths[None, :], axis=1)).astype(jnp.int32)
    return (document, places - starts)

def slot_table(choices):
    experts = jnp.arange(EXPERTS, dtype=jnp.int32)
    hits = lax.optimization_barrier(jnp.sum((choices[:, :, None] == experts[None, None, :]).astype(jnp.int32), axis=1)).astype(jnp.int32)
    before = (jnp.cumsum(hits, axis=0) - hits).astype(jnp.int32)
    return jnp.take_along_axis(before, choices, axis=1).astype(jnp.int32)

def slot_owners(choices, capacity):
    entries = choices.shape[0] * choices.shape[1]
    target = (choices * capacity + slot_table(choices)).reshape(-1).astype(jnp.int32)
    owners = jnp.full((EXPERTS * capacity,), entries, jnp.int32).at[target].set(jnp.arange(entries, dtype=jnp.int32))
    return (target, owners)

def block_mask(start, document):
    rows = start + jnp.arange(QBLOCK, dtype=jnp.int32)
    columns = jnp.arange(document.shape[0], dtype=jnp.int32)
    same = lax.dynamic_slice_in_dim(document, start, QBLOCK, 0)[:, None] == document[None, :]
    return same & (columns[None, :] <= rows[:, None])

def attend_block(start, queries, keys, values, document):
    kv_heads = keys.shape[1]
    block_query = lax.dynamic_slice_in_dim(queries, start, QBLOCK, 0).reshape(QBLOCK, kv_heads, -1, HD)
    raw = jnp.einsum('qkgh,tkh->kgqt', block_query, keys, precision=highest)
    scores = low_back(raw) * HD ** (-0.5)
    scores = jnp.where(block_mask(start, document), scores, masked_score)
    top = lax.optimization_barrier(jnp.max(scores, axis=-1, keepdims=True))
    exponent = jnp.exp(scores - top)
    weights = low(exponent / lax.optimization_barrier(jnp.sum(exponent, axis=-1, keepdims=True)))
    mixed = jnp.einsum('kgqt,tkh->qkgh', weights, values, precision=highest)
    return low(low_back(mixed)).reshape(QBLOCK, -1)

def group_attention(item, w_attention):
    normed, lengths = item
    count = normed.shape[0]
    document, position = doc_table(lengths, count)
    projected = low_back(jnp.einsum('td,dkc->tkc', normed, w_attention, precision=highest))
    queries = projected[:, :, :G * HD].reshape(count, -1, HD)
    keys = projected[:, :, G * HD:(G + 1) * HD]
    values = low(projected[:, :, (G + 1) * HD:])
    queries = low(rotate(queries, position, 1.0))
    keys = low(rotate(keys, position, 1.0))
    starts = jnp.arange(0, count, QBLOCK, dtype=jnp.int32)
    blocks = lax.map(jax.checkpoint(partial(attend_block, queries=queries, keys=keys, values=values, document=document)), starts)
    return blocks.reshape(count, -1)

def expert_block(item, w_gate_up, w_down):
    moved, gates, target, owners = item
    rows = moved.shape[0]
    padded = jnp.concatenate([moved, jnp.zeros((1, D), jnp.float32)], axis=0)
    sent = low_back(padded[owners // TOPK].reshape(EXPERTS, -1, D))
    projections = low_back(jnp.einsum('ecd,eidf->iecf', sent, w_gate_up, precision=highest))
    hidden = low(jax.nn.silu(projections[0]) * projections[1])
    result = jnp.einsum('ecf,efd->ecd', hidden, w_down, precision=highest)
    returned = low(low_back(result)).reshape(-1, D)
    picked = returned[target].reshape(rows, TOPK, D)
    return lax.optimization_barrier(jnp.sum(picked * gates[:, :, None], axis=1))

def forward(inputs, gains, router, w_attention, w_out, w_gate_up, w_down, lengths, choices, targets, owners):
    blocks_count = TOKENS // TOK_DEV
    normed = low(rms_norm(inputs, gains[0]))
    grouped = normed.reshape(GROUPS, TOK_GRP, D)
    heads = lax.map(jax.checkpoint(partial(group_attention, w_attention=low(w_attention))), (grouped, lengths))
    attended = low_back(jnp.dot(heads.reshape(TOKENS, -1), low(w_out).reshape(-1, D), precision=highest, preferred_element_type=jnp.float32))
    state = inputs + attended
    normed_two = rms_norm(state, gains[1])
    logits = jnp.dot(normed_two, router, precision=highest)
    gates = jax.nn.softmax(jnp.take_along_axis(logits, choices, axis=1), axis=-1)
    moved = low(normed_two).reshape(blocks_count, TOK_DEV, D)
    expert_out = lax.map(jax.checkpoint(partial(expert_block, w_gate_up=low(w_gate_up), w_down=low(w_down))), (moved, gates.reshape(blocks_count, TOK_DEV, TOPK), targets, owners))
    return state + expert_out.reshape(TOKENS, D)

def adamw(weight, grad, first, second, rate, decay):
    first = beta_one * first + (1.0 - beta_one) * grad
    second = beta_two * second + (1.0 - beta_two) * grad * grad
    step = first / (1.0 - beta_one ** STEP) / (jnp.sqrt(second / (1.0 - beta_two ** STEP)) + adam_eps)
    return (first, second, weight - rate * (step + decay * weight))

def reference(tokens, cotangent, doc_lengths, expert_choices, gains, gain_moment, gain_square, router, router_moment, router_square, w_attention, attention_moment, attention_square, w_out, out_moment, out_square, w_gate_up, gate_up_moment, gate_up_square, w_down, down_moment, down_square):
    blocks_count = TOKENS // TOK_DEV
    block_choices = expert_choices.reshape(blocks_count, TOK_DEV, TOPK)
    targets, owners = jax.vmap(partial(slot_owners, capacity=CAP))(block_choices)
    program = partial(forward, lengths=doc_lengths, choices=expert_choices, targets=targets, owners=owners)
    mixed, pull = jax.vjp(program, tokens.astype(jnp.float32), gains, router, w_attention, w_out, w_gate_up, w_down)
    grads = pull(cotangent.astype(jnp.float32))
    gain_first, gain_second, gain_new = adamw(gains, grads[1], gain_moment, gain_square, 1.0, 0.0)
    router_first, router_second, router_new = adamw(router, grads[2], router_moment, router_square, D ** (-0.5), decay_rate)
    attention_first, attention_second, attention_new = adamw(w_attention, grads[3], attention_moment, attention_square, 2.0 * D ** (-0.5), decay_rate)
    out_first, out_second, out_new = adamw(w_out, grads[4], out_moment, out_square, 16.0 * (H * HD) ** (-0.5), decay_rate)
    gate_up_first, gate_up_second, gate_up_new = adamw(w_gate_up, grads[5], gate_up_moment, gate_up_square, 2.0 * D ** (-0.5), decay_rate)
    down_first, down_second, down_new = adamw(w_down, grads[6], down_moment, down_square, 8.0 * FF ** (-0.5), decay_rate)
    return (mixed, grads[0], gain_first, gain_second, gain_new, router_first, router_second, router_new, attention_first, attention_second, attention_new, out_first, out_second, out_new, gate_up_first, gate_up_second, gate_up_new, down_first, down_second, down_new)
```

```python
from functools import partial

import jax
import jax.numpy as jnp
from jax import lax
from jax.experimental import pallas as pl
from jax.experimental.pallas import tpu as pltpu
from jax.sharding import PartitionSpec as P

D = 1024
H = 16
HD = 64
FF = 512
EXPERTS = 32
TOPK = 8
G = 2
STEP = 10

norm_eps = 1e-06
rope_base = 10000.0
masked_score = -1e30
beta_one = 0.9
beta_two = 0.95
adam_eps = 1e-08
decay_rate = 0.1
highest = lax.Precision.HIGHEST

QT = 256
KT = 256
RT = 256

f32 = jnp.float32
bf16 = jnp.bfloat16

NN = (((1,), (0,)), ((), ()))
NT = (((1,), (1,)), ((), ()))
TN = (((0,), (0,)), ((), ()))


def mm(a, b, dims):
    return lax.dot_general(a, b, dims, preferred_element_type=f32)


def attention_tile(j, i, start, k_ref):
    keys = k_ref[pl.ds(pl.multiple_of(j * KT, KT), KT), :]
    key_id = j * KT + lax.broadcasted_iota(jnp.int32, (KT, QT), 0)
    row_id = i * QT + lax.broadcasted_iota(jnp.int32, (KT, QT), 1)
    return keys, (key_id >= start) & (key_id <= row_id)


def attention_forward_kernel(low_ref, start_ref, q_ref, k_ref, v_ref, o_ref, sum_ref):
    i = pl.program_id(0)
    start = start_ref[...]

    def step(j, carry):
        keys, mask = attention_tile(j, i, start, k_ref)
        values = v_ref[:, pl.ds(pl.multiple_of(j * KT, KT), KT)]
        out = []
        for g in range(G):
            top, total, acc = carry[g]
            scores = mm(keys, q_ref[g * HD : (g + 1) * HD, :], NN)
            scores = jnp.where(mask, scores, masked_score)
            new_top = jnp.maximum(top, jnp.max(scores, axis=0, keepdims=True))
            probs = jnp.exp(scores - new_top)
            shrink = jnp.exp(top - new_top)
            total = total * shrink + jnp.sum(probs, axis=0, keepdims=True)
            acc = acc * shrink + mm(values, probs.astype(bf16), NN)
            out.append((new_top, total, acc))
        return tuple(out)

    zero = (
        jnp.full((1, QT), masked_score, f32),
        jnp.zeros((1, QT), f32),
        jnp.zeros((HD, QT), f32),
    )
    done = lax.fori_loop(low_ref[i], i + 1, step, (zero,) * G)
    for g in range(G):
        top, total, acc = done[g]
        o_ref[g * HD : (g + 1) * HD, :] = (acc / total).astype(bf16)
        sum_ref[g : g + 1, :] = top + jnp.log(total)


def attention_backward_kernel(
    low_ref, start_ref, q_ref, o_ref, d_ref, sum_ref, k_ref, kt_ref, v_ref, dq_ref, dk_ref, dv_ref
):
    i = pl.program_id(0)
    start = start_ref[...]

    @pl.when(i == 0)
    def _():
        dk_ref[...] = jnp.zeros_like(dk_ref)
        dv_ref[...] = jnp.zeros_like(dv_ref)

    grads, inner = [], []
    for g in range(G):
        part = slice(g * HD, (g + 1) * HD)
        grads.append(d_ref[part, :])
        inner.append(
            jnp.sum(d_ref[part, :].astype(f32) * o_ref[part, :].astype(f32), axis=0, keepdims=True)
        )

    def step(j, carry):
        keys, mask = attention_tile(j, i, start, k_ref)
        columns = pl.ds(pl.multiple_of(j * KT, KT), KT)
        values = v_ref[columns, :]
        keys_t = kt_ref[:, columns]
        dk = jnp.zeros((HD, KT), f32)
        dv = jnp.zeros((HD, KT), f32)
        out = []
        for g in range(G):
            query = q_ref[g * HD : (g + 1) * HD, :]
            scores = mm(keys, query, NN)
            probs = jnp.where(mask, jnp.exp(scores - sum_ref[g : g + 1, :]), 0.0)
            probs_grad = mm(values, grads[g], NN)
            score_grad = (probs * (probs_grad - inner[g])).astype(bf16)
            dv += mm(grads[g], probs.astype(bf16), NT)
            dk += mm(query, score_grad, NT)
            out.append(carry[g] + mm(keys_t, score_grad, NN))
        dk_ref[:, columns] += dk
        dv_ref[:, columns] += dv
        return tuple(out)

    done = lax.fori_loop(low_ref[i], i + 1, step, (jnp.zeros((HD, QT), f32),) * G)
    for g in range(G):
        dq_ref[g * HD : (g + 1) * HD, :] = done[g] * HD ** (-0.5)


def attention_forward(low, start, q, k, vt):
    rows = q.shape[1]
    tile = lambda height: pl.BlockSpec((height, QT), lambda i, s: (0, i))
    whole = lambda a: pl.BlockSpec(a.shape, lambda i, s: (0, 0))
    return pl.pallas_call(
        attention_forward_kernel,
        out_shape=(
            jax.ShapeDtypeStruct((G * HD, rows), bf16),
            jax.ShapeDtypeStruct((G, rows), f32),
        ),
        grid_spec=pltpu.PrefetchScalarGridSpec(
            num_scalar_prefetch=1,
            grid=(rows // QT,),
            in_specs=[tile(1), tile(G * HD), whole(k), whole(vt)],
            out_specs=[tile(G * HD), tile(G)],
        ),
        compiler_params=pltpu.CompilerParams(vmem_limit_bytes=24 << 20),
        cost_estimate=pl.CostEstimate(flops=1 << 20, bytes_accessed=1 << 20, transcendentals=0),
        name="attention_forward",
    )(low, start, q, k, vt)


def attention_backward(low, start, q, o, d, sums, k, kt, v):
    rows = q.shape[1]
    tile = lambda height: pl.BlockSpec((height, QT), lambda i, s: (0, i))
    whole = lambda a: pl.BlockSpec(a.shape, lambda i, s: (0, 0))
    return pl.pallas_call(
        attention_backward_kernel,
        out_shape=(
            jax.ShapeDtypeStruct((G * HD, rows), f32),
            jax.ShapeDtypeStruct((HD, rows), f32),
            jax.ShapeDtypeStruct((HD, rows), f32),
        ),
        grid_spec=pltpu.PrefetchScalarGridSpec(
            num_scalar_prefetch=1,
            grid=(rows // QT,),
            in_specs=[tile(1), tile(G * HD), tile(G * HD), tile(G * HD), tile(G)]
            + [whole(k), whole(kt), whole(v)],
            out_specs=[tile(G * HD), whole(kt), whole(kt)],
        ),
        compiler_params=pltpu.CompilerParams(vmem_limit_bytes=24 << 20),
        cost_estimate=pl.CostEstimate(flops=1 << 20, bytes_accessed=1 << 20, transcendentals=0),
        name="attention_backward",
    )(low, start, q, o, d, sums, k, kt, v)


def expert_kernel(blocks, rows, offset_ref, count_ref, rank_ref, gate_ref, *refs):
    x_refs, cot_refs, refs = refs[:blocks], refs[blocks : 2 * blocks], refs[2 * blocks :]
    w_ref, refs = refs[0], refs[1:]
    mixed_refs, slot_refs, refs = refs[:blocks], refs[blocks : 2 * blocks], refs[2 * blocks :]
    gate_grad_ref, w_grad_ref, mixed_acc, slot_acc, w_acc, xs, cs, gates, gate_grads = refs
    seg = rows // 2
    chunk, expert = pl.program_id(0), pl.program_id(1)
    step = chunk * pl.num_programs(1) + expert

    @pl.when(step == 0)
    def _():
        xs[...] = jnp.zeros_like(xs)
        cs[...] = jnp.zeros_like(cs)

    @pl.when(expert == 0)
    def _():
        mixed_acc[...] = jnp.zeros_like(mixed_acc)
        slot_acc[...] = jnp.zeros_like(slot_acc)

    @pl.when((chunk == 0) | (pl.num_programs(1) > 1))
    def _():
        w_acc[...] = jnp.zeros_like(w_acc)

    gates[...] = jnp.zeros_like(gates)

    def picks(block):
        rank = rank_ref[0, :, block * rows : (block + 1) * rows]
        return lax.broadcasted_iota(jnp.int32, (seg, rows), 0) == rank

    for block in range(blocks):
        first = offset_ref[step * (blocks + 1) + block]
        count = count_ref[step * blocks + block]

        @pl.when(count > 0)
        def _():
            hit = picks(block)
            one = jnp.where(hit, 1.0, 0.0).astype(bf16)
            place = pl.ds(pl.multiple_of(first, 16), seg)
            part = slice(block * rows, (block + 1) * rows)
            xs[place, :] = mm(one, x_refs[block][...], NN).astype(bf16)
            cs[place, :] = mm(one, cot_refs[block][...], NN).astype(bf16)
            gates[place, :] = jnp.sum(
                jnp.where(hit, gate_ref[0, :, part], 0.0), axis=1, keepdims=True
            )

    used = offset_ref[step * (blocks + 1) + blocks]

    def tile(t, carry):
        place = pl.ds(pl.multiple_of(t * RT, RT), RT)
        x, c, gate = xs[place, :], cs[place, :], gates[place, :]
        gate_pre = mm(x, w_ref[0, 0], NT)
        up_pre = mm(x, w_ref[0, 1], NT)
        sigmoid = jax.nn.sigmoid(gate_pre)
        active = gate_pre * sigmoid
        inner = active * up_pre
        plain = mm(c, w_ref[0, 2], NT)
        gate_grads[place, :] = jnp.sum(plain * inner, axis=1, keepdims=True)
        inner_grad = plain * gate
        gate_pre_grad = inner_grad * up_pre * sigmoid * (1.0 + gate_pre * (1.0 - sigmoid))
        gate_pre_grad = gate_pre_grad.astype(bf16)
        up_pre_grad = (inner_grad * active).astype(bf16)
        scaled = (inner * gate).astype(bf16)
        w_acc[0] += mm(gate_pre_grad, x, TN)
        w_acc[1] += mm(up_pre_grad, x, TN)
        w_acc[2] += mm(scaled, c, TN)
        cs[place, :] = mm(scaled, w_ref[0, 2], NN).astype(bf16)
        xs[place, :] = (
            mm(gate_pre_grad, w_ref[0, 0], NN) + mm(up_pre_grad, w_ref[0, 1], NN)
        ).astype(bf16)
        return carry

    lax.fori_loop(0, (used + RT - 1) // RT, tile, 0)

    for block in range(blocks):
        first = offset_ref[step * (blocks + 1) + block]
        count = count_ref[step * blocks + block]
        part = slice(block * rows, (block + 1) * rows)

        @pl.when(count > 0)
        def _():
            hit = picks(block)
            one = jnp.where(hit, 1.0, 0.0).astype(bf16)
            place = pl.ds(pl.multiple_of(first, 16), seg)
            mixed_acc[part, :] += mm(one, cs[place, :], TN)
            slot_acc[part, :] += mm(one, xs[place, :], TN)
            gate_grad_ref[0, :, part] = jnp.sum(
                jnp.where(hit, gate_grads[place, :], 0.0), axis=0, keepdims=True
            )

        @pl.when(count == 0)
        def _():
            gate_grad_ref[0, :, part] = jnp.zeros((1, rows), f32)

    w_grad_ref[0] = w_acc[...].astype(bf16)

    @pl.when(expert == pl.num_programs(1) - 1)
    def _():
        for block in range(blocks):
            part = slice(block * rows, (block + 1) * rows)
            mixed_refs[block][...] = mixed_acc[part, :].astype(bf16)
            slot_refs[block][...] = slot_acc[part, :].astype(bf16)


def expert_layer(rank, gate, counts, x, cot, weights, rows):
    experts, blocks = weights.shape[0], len(x)
    height = blocks * rows
    chunks = rank.shape[0] // experts
    padded = -(-counts // 16) * 16
    offsets = jnp.concatenate(
        [jnp.zeros((chunks * experts, 1), jnp.int32), jnp.cumsum(padded, axis=1)], axis=1
    )
    room = -(-blocks * (rows // 2) // RT) * RT
    tokens = lambda: pl.BlockSpec((rows, D), lambda c, e, a, b: (c, 0))
    held = lambda: pl.BlockSpec((rows, D), lambda c, e, a, b: (c, 0), pipeline_mode=pl.Buffered(1))
    line = lambda: pl.BlockSpec((1, 1, height), lambda c, e, a, b: (c * experts + e, 0, 0))
    weight = lambda: pl.BlockSpec((1, 3, FF, D), lambda c, e, a, b: (e, 0, 0, 0))
    rows_out = [jax.ShapeDtypeStruct((chunks * rows, D), bf16)] * blocks
    out = pl.pallas_call(
        partial(expert_kernel, blocks, rows),
        out_shape=rows_out
        + rows_out
        + [
            jax.ShapeDtypeStruct((chunks * experts, 1, height), f32),
            jax.ShapeDtypeStruct(weights.shape, bf16),
        ],
        grid_spec=pltpu.PrefetchScalarGridSpec(
            num_scalar_prefetch=2,
            grid=(chunks, experts),
            in_specs=[line(), line()] + [held() for _ in range(2 * blocks)] + [weight()],
            out_specs=[tokens() for _ in range(2 * blocks)] + [line(), weight()],
            scratch_shapes=[
                pltpu.VMEM((height, D), f32),
                pltpu.VMEM((height, D), f32),
                pltpu.VMEM((3, FF, D), f32),
                pltpu.VMEM((room, D), bf16),
                pltpu.VMEM((room, D), bf16),
                pltpu.VMEM((room, 1), f32),
                pltpu.VMEM((room, 1), f32),
            ],
        ),
        compiler_params=pltpu.CompilerParams(vmem_limit_bytes=58 << 20),
        cost_estimate=pl.CostEstimate(flops=1 << 20, bytes_accessed=1 << 20, transcendentals=0),
        name="experts",
    )(offsets.reshape(-1), counts.reshape(-1), rank, gate, *x, *cot, weights)
    return out[:blocks], out[blocks : 2 * blocks], out[-2], out[-1]


def angles(position):
    half = HD // 2
    frequency = rope_base ** (-jnp.arange(half, dtype=f32) * 2.0 / HD)
    angle = frequency[:, None] * position.astype(f32)[None, :]
    return jnp.cos(angle), jnp.sin(angle)


def rotate(values, cosine, sine):
    half = HD // 2
    parts = values.reshape(-1, HD, values.shape[1])
    first, second = parts[:, :half], parts[:, half:]
    return jnp.concatenate(
        [first * cosine - second * sine, second * cosine + first * sine], axis=1
    ).reshape(values.shape)


def doc_table(lengths, count):
    ends = jnp.cumsum(lengths)
    places = jnp.arange(count, dtype=jnp.int32)
    after = (places[None, :] >= ends[:, None]).astype(jnp.int32)
    starts = jnp.sum(after * lengths[:, None], axis=0)
    return (starts, places - starts)


def rank_table(choices, first, experts):
    named = (first + jnp.arange(experts, dtype=jnp.int32))[None, :, None, None]
    hits = jnp.any(choices[:, None, :, :] == named, axis=2)
    order = jnp.arange(choices.shape[2])
    before = (order[:, None] < order[None, :]).astype(bf16)
    rank = jnp.einsum("ber,rs->bes", hits.astype(bf16), before, preferred_element_type=f32)
    rank = jnp.where(hits, rank.astype(jnp.int32), -1)
    return rank, jnp.sum(hits.astype(jnp.int32), axis=2)


def after(value, other):
    return lax.optimization_barrier((value, other))[0]


def shift(value, axis, step):
    size = lax.axis_size(axis)
    return lax.ppermute(value, axis, [(i, (i + step) % size) for i in range(size)])


def pack(values, rows, parts):
    terms, rest = [], values.astype(f32)
    for _ in range(parts):
        term = rest.astype(bf16)
        terms.append(term)
        rest = rest - term.astype(f32)
    terms = jnp.stack(terms).reshape(-1)
    terms = jnp.pad(terms, (0, -terms.size % (16 * D))).reshape(-1, D)
    return jnp.concatenate([rows, terms], axis=0)


def unpack(message, rows, shape, parts):
    size = shape[0] * shape[1]
    terms = message[rows:].reshape(-1)[: parts * size].reshape((parts,) + shape)
    return jnp.sum(terms.astype(f32), axis=0)


def total(values, axis):
    size = lax.axis_size(axis)
    distance = 1
    while distance < size:
        pairs = [(i, i ^ distance) for i in range(size)]
        other = [lax.ppermute(v, axis, pairs) for v in values]
        values = [(v.astype(f32) + o.astype(f32)).astype(v.dtype) for v, o in zip(values, other)]
        distance *= 2
    return values


def spread(values, axis):
    return lax.all_to_all(values, axis, split_axis=0, concat_axis=0, tiled=True)


def to_rows(values, ranks):
    width = values.shape[0]
    parts = values.reshape(width, ranks, -1).swapaxes(0, 1)
    return spread(parts, "tensor").reshape(ranks * width, -1)


def to_heads(values, ranks):
    parts = spread(values.reshape(ranks, -1, values.shape[1]), "tensor")
    return parts.swapaxes(0, 1).reshape(parts.shape[1], -1)


def adamw(weight, grad, first, second, rate, decay):
    first = beta_one * first + (1.0 - beta_one) * grad
    second = beta_two * second + (1.0 - beta_two) * grad * grad
    step = first / (1.0 - beta_one**STEP) / (jnp.sqrt(second / (1.0 - beta_two**STEP)) + adam_eps)
    return (first, second, weight - rate * (step + decay * weight))


def on_device(
    tokens,
    cotangent,
    doc_lengths,
    expert_choices,
    gains,
    gain_moment,
    gain_square,
    router,
    router_moment,
    router_square,
    w_attention,
    attention_moment,
    attention_square,
    w_out,
    out_moment,
    out_square,
    w_gate_up,
    gate_up_moment,
    gate_up_square,
    w_down,
    down_moment,
    down_square,
):
    ranks = lax.axis_size("tensor")
    peers = lax.axis_size("expert")
    rows = tokens.shape[0]
    group_rows = rows * ranks
    experts = w_gate_up.shape[0]
    blocks = min(peers, 4)
    halves = 2 if experts % 2 == 0 else 1
    half = experts // halves
    hidden = w_down.shape[1]

    inputs = tokens.astype(f32)
    scale_one = lax.rsqrt(jnp.mean(inputs * inputs, axis=-1, keepdims=True) + norm_eps)
    normed = (inputs * scale_one * gains[0]).astype(bf16)
    gathered = lax.all_gather(normed, "tensor", axis=0, tiled=True)

    attention_low = w_attention.reshape(D, -1).astype(bf16)
    out_low = w_out.reshape(-1, D).astype(bf16)
    expert_low = jnp.concatenate(
        [w_gate_up.swapaxes(2, 3).astype(bf16), w_down.astype(bf16)[:, None]], axis=1
    )
    width = out_low.shape[0]
    both_all = lax.all_gather(
        jnp.concatenate([out_low, attention_low.T], axis=0), "tensor", axis=0, tiled=False
    )
    out_all = both_all[:, :width].reshape(-1, D)
    attention_all = both_all[:, width:].reshape(-1, D)
    expert_all = [
        lax.all_gather(expert_low[part * half : (part + 1) * half], "tensor", axis=2, tiled=True)
        for part in range(halves)
    ]

    message = pack(expert_choices.T, cotangent, 1)
    messages = [shift(message, "expert", d) for d in range(1, peers)]
    cot_in = [cotangent] + messages
    choices_in = [expert_choices.T] + [
        unpack(m, rows, (TOPK, rows), 1).astype(jnp.int32) for m in messages
    ]

    start, position = doc_table(doc_lengths[0], group_rows)
    cosine, sine = angles(position)
    lowest = start[::QT] // KT
    start = start[None, :]
    projected = jnp.einsum("dc,td->ct", attention_low, gathered, preferred_element_type=f32)
    turned = rotate(projected[: (G + 1) * HD], cosine, sine).astype(bf16)
    queries = turned[: G * HD] * bf16(HD ** (-0.5))
    keys_t = turned[G * HD :]
    values_t = projected[(G + 1) * HD :].astype(bf16)
    keys, values = keys_t.T, values_t.T
    heads, log_sums = attention_forward(lowest, start, queries, keys, values_t)

    heads_rows = to_rows(heads, ranks)
    attended = jnp.einsum("ct,cd->td", heads_rows, out_all, preferred_element_type=f32)
    state = inputs + attended
    scale_two = lax.rsqrt(jnp.mean(state * state, axis=-1, keepdims=True) + norm_eps)
    unit = state * scale_two
    normed_two = unit * gains[1]

    logits = lax.dot_general(router, normed_two, (((0,), (1,)), ((), ())), precision=highest)
    named = jnp.arange(EXPERTS, dtype=jnp.int32)[:, None, None]
    chosen = jnp.any(expert_choices.T[None, :, :] == named, axis=1)
    top = jnp.max(jnp.where(chosen, logits, -jnp.inf), axis=0, keepdims=True)
    weight = jnp.where(chosen, jnp.exp(jnp.where(chosen, logits - top, 0.0)), 0.0)
    gates = weight / jnp.sum(weight, axis=0, keepdims=True)

    me = lax.axis_index("expert")
    moved = normed_two.astype(bf16)
    by_peer = gates.reshape(peers, experts, rows)
    gates_to = [
        lax.dynamic_index_in_dim(by_peer, (me + d) % peers, 0, keepdims=False) for d in range(peers)
    ]
    x_in, gates_in = [moved], [gates_to[0]]
    for d in range(1, peers):
        message = after(pack(gates_to[d], moved, 3), cot_in)
        x_in.append(shift(message, "expert", d))
        gates_in.append(unpack(x_in[d], rows, (experts, rows), 3))
    rank, counts = rank_table(jnp.stack(choices_in), me * experts, experts)

    def by_step(values):
        return values.reshape((-1, blocks) + values.shape[1:]).swapaxes(1, 2)

    def lay(values):
        if len(values) == blocks:
            return values
        return [jnp.concatenate([v[:rows] for v in values[b::blocks]]) for b in range(blocks)]

    def unlay(values):
        if len(values) == peers:
            return values
        return [values[d % blocks][d // blocks * rows :][:rows] for d in range(peers)]

    rank_steps, gate_steps = by_step(rank), by_step(jnp.stack(gates_in))
    count_steps = by_step(counts)
    mixed_parts, slot_parts, gate_grad_parts, expert_grad = [], [], [], []
    for part in range(halves):
        own = slice(part * half, (part + 1) * half)
        flat = lambda v: v[:, own].reshape(-1, 1, blocks * rows)
        mixed_out, slot_out, gate_out, grad_out = expert_layer(
            flat(rank_steps),
            flat(gate_steps),
            count_steps[:, own].reshape(-1, blocks),
            lay(x_in),
            lay(cot_in),
            expert_all[part],
            rows,
        )
        mixed_parts.append(mixed_out)
        slot_parts.append(slot_out)
        gate_grad_parts.append(gate_out.reshape(-1, half, blocks, rows))
        expert_grad.append(
            lax.psum_scatter(grad_out, "tensor", scatter_dimension=2, tiled=True)
        )

    def both(parts):
        if len(parts) == 1:
            return unlay(parts[0])
        return unlay([sum(v.astype(f32) for v in same).astype(bf16) for same in zip(*parts)])

    gate_out = jnp.concatenate(gate_grad_parts, axis=1).swapaxes(1, 2).reshape(peers, experts, rows)
    slot_out, mixed_out = both(slot_parts), both(mixed_parts)
    slot_back, gate_back = [slot_out[0]], [gate_out[0]]
    for d in range(1, peers):
        message = shift(pack(gate_out[d], slot_out[d], 3), "expert", -d)
        slot_back.append(message[:rows])
        gate_back.append(unpack(message, rows, (experts, rows), 3))
    gate_grads = jnp.roll(jnp.stack(gate_back), me, axis=0).reshape(EXPERTS, rows)
    slot_sum = sum(v.astype(f32) for v in slot_back)
    mixed_out = after(mixed_out, slot_back)
    mixed_back = [mixed_out[0]] + [shift(mixed_out[d], "expert", -d) for d in range(1, peers)]
    mixed = state + sum(v.astype(f32) for v in mixed_back)
    logit_grads = gates * (gate_grads - jnp.sum(gates * gate_grads, axis=0, keepdims=True))
    router_grad = lax.dot_general(
        logit_grads, normed_two, (((1,), (0,)), ((), ())), precision=highest
    )
    normed_two_grad = slot_sum + lax.dot_general(
        logit_grads, router, (((0,), (1,)), ((), ())), precision=highest
    )
    gain_two_grad = jnp.sum(normed_two_grad * unit, axis=0)
    unit_grad = normed_two_grad * gains[1]
    state_grad = cotangent.astype(f32) + scale_two * (
        unit_grad - unit * jnp.mean(unit_grad * unit, axis=-1, keepdims=True)
    )

    branch = state_grad.astype(bf16)
    head_grads_rows = jnp.einsum(
        "cd,td->ct", out_all, branch, preferred_element_type=f32
    ).astype(bf16)
    head_grads, expert_grad[0] = lax.optimization_barrier(
        (to_heads(head_grads_rows, ranks), expert_grad[0])
    )
    out_grad = jnp.einsum("ct,td->cd", heads_rows, branch, preferred_element_type=f32)
    out_grad = spread(out_grad.astype(bf16).reshape(ranks, -1, D), "tensor")
    out_grad = jnp.sum(out_grad.astype(f32), axis=0)
    query_grad, key_grad, value_grad = attention_backward(
        lowest, start, queries, heads, head_grads, log_sums, keys, keys_t, values
    )
    turned_grad = rotate(jnp.concatenate([query_grad, key_grad], axis=0), cosine, -sine)
    projected_grad = jnp.concatenate([turned_grad, value_grad], axis=0).astype(bf16)
    attention_grad = jnp.einsum(
        "td,ct->dc", gathered, projected_grad, preferred_element_type=f32
    )
    gain_one_grad = (
        jnp.sum(attention_grad * attention_low.astype(f32), axis=1) / gains[0]
    )
    projected_rows, expert_grad[-1] = lax.optimization_barrier(
        (to_rows(projected_grad, ranks), expert_grad[-1])
    )
    normed_grad = jnp.einsum(
        "ct,cd->td", projected_rows, attention_all, preferred_element_type=f32
    )
    unit_one = inputs * scale_one
    unit_one_grad = normed_grad * gains[0]
    input_grad = state_grad + scale_one * (
        unit_one_grad - unit_one * jnp.mean(unit_one_grad * unit_one, axis=-1, keepdims=True)
    )

    early = [jnp.concatenate([router_grad, gain_two_grad[None]], axis=0)]
    early = total(total(early, "expert"), "tensor")[0]
    router_grad, gain_two_grad = early[:EXPERTS].T, early[EXPERTS]
    attention_grad, out_grad, gain_one_grad = total(
        [attention_grad.astype(bf16), out_grad.astype(bf16), gain_one_grad[None]], "expert"
    )
    attention_grad = attention_grad.astype(f32).reshape(w_attention.shape)
    out_grad = out_grad.astype(f32).reshape(w_out.shape)
    gain_one_grad = total([gain_one_grad], "tensor")[0][0]
    gain_grad = jnp.stack([gain_one_grad, gain_two_grad])
    expert_grad = jnp.concatenate(expert_grad, axis=0).astype(f32)
    gate_up_grad, down_grad = expert_grad[:, :2], expert_grad[:, 2]
    gain_first, gain_second, gain_new = adamw(gains, gain_grad, gain_moment, gain_square, 1.0, 0.0)
    router_first, router_second, router_new = adamw(
        router, router_grad, router_moment, router_square, D ** (-0.5), decay_rate
    )
    attention_first, attention_second, attention_new = adamw(
        w_attention,
        attention_grad,
        attention_moment,
        attention_square,
        2.0 * D ** (-0.5),
        decay_rate,
    )
    out_first, out_second, out_new = adamw(
        w_out, out_grad, out_moment, out_square, 16.0 * (H * HD) ** (-0.5), decay_rate
    )
    gate_up_first, gate_up_second, gate_up_new = adamw(
        w_gate_up,
        gate_up_grad.swapaxes(2, 3),
        gate_up_moment,
        gate_up_square,
        2.0 * D ** (-0.5),
        decay_rate,
    )
    down_first, down_second, down_new = adamw(
        w_down, down_grad, down_moment, down_square, 8.0 * FF ** (-0.5), decay_rate
    )
    return (
        mixed,
        input_grad,
        gain_first,
        gain_second,
        gain_new,
        router_first,
        router_second,
        router_new,
        attention_first,
        attention_second,
        attention_new,
        out_first,
        out_second,
        out_new,
        gate_up_first,
        gate_up_second,
        gate_up_new,
        down_first,
        down_second,
        down_new,
    )


def solution(mesh):
    placed = (
        P(("expert", "tensor"), None),
        P(("expert", "tensor"), None),
        P("expert", None),
        P(("expert", "tensor"), None),
        P(),
        P(),
        P(),
        P(),
        P(),
        P(),
        P(None, "tensor", None),
        P(None, "tensor", None),
        P(None, "tensor", None),
        P("tensor", None, None),
        P("tensor", None, None),
        P("tensor", None, None),
        P("expert", None, None, "tensor"),
        P("expert", None, None, "tensor"),
        P("expert", None, None, "tensor"),
        P("expert", "tensor", None),
        P("expert", "tensor", None),
        P("expert", "tensor", None),
    )
    return jax.shard_map(
        on_device,
        mesh=mesh,
        in_specs=placed,
        out_specs=(
            P(("expert", "tensor"), None),
            P(("expert", "tensor"), None),
            P(),
            P(),
            P(),
            P(),
            P(),
            P(),
            P(None, "tensor", None),
            P(None, "tensor", None),
            P(None, "tensor", None),
            P("tensor", None, None),
            P("tensor", None, None),
            P("tensor", None, None),
            P("expert", None, None, "tensor"),
            P("expert", None, None, "tensor"),
            P("expert", None, None, "tensor"),
            P("expert", "tensor", None),
            P("expert", "tensor", None),
            P("expert", "tensor", None),
        ),
        check_vma=False,
    )
```

```python
from functools import partial

import jax
import jax.numpy as jnp
from jax import lax
from jax.experimental import pallas as pl
from jax.experimental.pallas import tpu as pltpu
from jax.sharding import PartitionSpec as P

D = 1024
H = 16
HD = 64
FF = 512
EXPERTS = 32
TOPK = 8
G = 2
STEP = 10

norm_eps = 1e-06
rope_base = 10000.0
masked_score = -1e30
beta_one = 0.9
beta_two = 0.95
adam_eps = 1e-08
decay_rate = 0.1
highest = lax.Precision.HIGHEST

QT = 256
KT = 256
RT = 256

f32 = jnp.float32
bf16 = jnp.bfloat16

NN = (((1,), (0,)), ((), ()))
NT = (((1,), (1,)), ((), ()))
TN = (((0,), (0,)), ((), ()))


def mm(a, b, dims):
    return lax.dot_general(a, b, dims, preferred_element_type=f32)


def attention_tile(j, i, start, k_ref):
    keys = k_ref[pl.ds(pl.multiple_of(j * KT, KT), KT), :]
    key_id = j * KT + lax.broadcasted_iota(jnp.int32, (KT, QT), 0)
    row_id = i * QT + lax.broadcasted_iota(jnp.int32, (KT, QT), 1)
    return keys, (key_id >= start) & (key_id <= row_id)


def attention_forward_kernel(low_ref, start_ref, q_ref, k_ref, v_ref, o_ref, sum_ref):
    i = pl.program_id(0)
    start = start_ref[...]

    def step(j, carry):
        keys, mask = attention_tile(j, i, start, k_ref)
        values = v_ref[:, pl.ds(pl.multiple_of(j * KT, KT), KT)]
        out = []
        for g in range(G):
            top, total, acc = carry[g]
            scores = mm(keys, q_ref[g * HD : (g + 1) * HD, :], NN)
            scores = jnp.where(mask, scores, masked_score)
            new_top = jnp.maximum(top, jnp.max(scores, axis=0, keepdims=True))
            probs = jnp.exp(scores - new_top)
            shrink = jnp.exp(top - new_top)
            total = total * shrink + jnp.sum(probs, axis=0, keepdims=True)
            acc = acc * shrink + mm(values, probs.astype(bf16), NN)
            out.append((new_top, total, acc))
        return tuple(out)

    zero = (
        jnp.full((1, QT), masked_score, f32),
        jnp.zeros((1, QT), f32),
        jnp.zeros((HD, QT), f32),
    )
    done = lax.fori_loop(low_ref[i], i + 1, step, (zero,) * G)
    for g in range(G):
        top, total, acc = done[g]
        o_ref[g * HD : (g + 1) * HD, :] = (acc / total).astype(bf16)
        sum_ref[g : g + 1, :] = top + jnp.log(total)


def attention_backward_kernel(
    low_ref, start_ref, q_ref, o_ref, d_ref, sum_ref, k_ref, kt_ref, v_ref, dq_ref, dk_ref, dv_ref
):
    i = pl.program_id(0)
    start = start_ref[...]

    @pl.when(i == 0)
    def _():
        dk_ref[...] = jnp.zeros_like(dk_ref)
        dv_ref[...] = jnp.zeros_like(dv_ref)

    grads, inner = [], []
    for g in range(G):
        part = slice(g * HD, (g + 1) * HD)
        grads.append(d_ref[part, :])
        inner.append(
            jnp.sum(d_ref[part, :].astype(f32) * o_ref[part, :].astype(f32), axis=0, keepdims=True)
        )

    def step(j, carry):
        keys, mask = attention_tile(j, i, start, k_ref)
        columns = pl.ds(pl.multiple_of(j * KT, KT), KT)
        values = v_ref[columns, :]
        keys_t = kt_ref[:, columns]
        dk = jnp.zeros((HD, KT), f32)
        dv = jnp.zeros((HD, KT), f32)
        out = []
        for g in range(G):
            query = q_ref[g * HD : (g + 1) * HD, :]
            scores = mm(keys, query, NN)
            probs = jnp.where(mask, jnp.exp(scores - sum_ref[g : g + 1, :]), 0.0)
            probs_grad = mm(values, grads[g], NN)
            score_grad = (probs * (probs_grad - inner[g])).astype(bf16)
            dv += mm(grads[g], probs.astype(bf16), NT)
            dk += mm(query, score_grad, NT)
            out.append(carry[g] + mm(keys_t, score_grad, NN))
        dk_ref[:, columns] += dk
        dv_ref[:, columns] += dv
        return tuple(out)

    done = lax.fori_loop(low_ref[i], i + 1, step, (jnp.zeros((HD, QT), f32),) * G)
    for g in range(G):
        dq_ref[g * HD : (g + 1) * HD, :] = done[g] * HD ** (-0.5)


def attention_forward(low, start, q, k, vt):
    rows = q.shape[1]
    tile = lambda height: pl.BlockSpec((height, QT), lambda i, s: (0, i))
    whole = lambda a: pl.BlockSpec(a.shape, lambda i, s: (0, 0))
    return pl.pallas_call(
        attention_forward_kernel,
        out_shape=(
            jax.ShapeDtypeStruct((G * HD, rows), bf16),
            jax.ShapeDtypeStruct((G, rows), f32),
        ),
        grid_spec=pltpu.PrefetchScalarGridSpec(
            num_scalar_prefetch=1,
            grid=(rows // QT,),
            in_specs=[tile(1), tile(G * HD), whole(k), whole(vt)],
            out_specs=[tile(G * HD), tile(G)],
        ),
        compiler_params=pltpu.CompilerParams(vmem_limit_bytes=24 << 20),
        cost_estimate=pl.CostEstimate(flops=1 << 20, bytes_accessed=1 << 20, transcendentals=0),
        name="attention_forward",
    )(low, start, q, k, vt)


def attention_backward(low, start, q, o, d, sums, k, kt, v):
    rows = q.shape[1]
    tile = lambda height: pl.BlockSpec((height, QT), lambda i, s: (0, i))
    whole = lambda a: pl.BlockSpec(a.shape, lambda i, s: (0, 0))
    return pl.pallas_call(
        attention_backward_kernel,
        out_shape=(
            jax.ShapeDtypeStruct((G * HD, rows), f32),
            jax.ShapeDtypeStruct((HD, rows), f32),
            jax.ShapeDtypeStruct((HD, rows), f32),
        ),
        grid_spec=pltpu.PrefetchScalarGridSpec(
            num_scalar_prefetch=1,
            grid=(rows // QT,),
            in_specs=[tile(1), tile(G * HD), tile(G * HD), tile(G * HD), tile(G)]
            + [whole(k), whole(kt), whole(v)],
            out_specs=[tile(G * HD), whole(kt), whole(kt)],
        ),
        compiler_params=pltpu.CompilerParams(vmem_limit_bytes=24 << 20),
        cost_estimate=pl.CostEstimate(flops=1 << 20, bytes_accessed=1 << 20, transcendentals=0),
        name="attention_backward",
    )(low, start, q, o, d, sums, k, kt, v)


def expert_kernel(blocks, rows, part, parts, offset_ref, count_ref, rank_ref, *refs):
    take = lambda n: (refs[:n], refs[n:])
    x_refs, refs = take(blocks)
    cot_refs, refs = take(blocks)
    mixed_before, refs = take(blocks if part else 0)
    slot_before, refs = take(blocks if part else 0)
    (w_ref,), refs = take(1)
    mixed_refs, refs = take(blocks)
    slot_refs, refs = take(blocks)
    w_grad_ref, mixed_acc, slot_acc, w_acc, xs, cs, gates, gate_grads, tail = refs
    high = tail.shape[1]
    seg = rows // 2
    chunk, expert = pl.program_id(0), pl.program_id(1)
    step = chunk * pl.num_programs(1) + expert

    @pl.when(step == 0)
    def _():
        xs[...] = jnp.zeros_like(xs)
        cs[...] = jnp.zeros_like(cs)

    @pl.when(expert == 0)
    def _():
        tail[...] = jnp.zeros_like(tail)
        if part:
            for block in range(blocks):
                place = slice(block * rows, (block + 1) * rows)
                mixed_acc[place, :] = mixed_before[block][...].astype(f32)
                slot_acc[place, :] = slot_before[block][:rows, :].astype(f32)
        else:
            mixed_acc[...] = jnp.zeros_like(mixed_acc)
            slot_acc[...] = jnp.zeros_like(slot_acc)

    @pl.when((chunk == 0) | (pl.num_programs(1) > 1))
    def _():
        w_acc[...] = jnp.zeros_like(w_acc)

    gates[...] = jnp.zeros_like(gates)
    own = part * pl.num_programs(1) + expert

    def gate_row(block):
        terms = x_refs[block][rows:, :rows].astype(f32)
        terms = terms[:high] + terms[high:]
        here = lax.broadcasted_iota(jnp.int32, (high, rows), 0) == own
        return jnp.sum(jnp.where(here, terms, 0.0), axis=0, keepdims=True)

    def picks(block):
        rank = rank_ref[0, :, block * rows : (block + 1) * rows]
        return lax.broadcasted_iota(jnp.int32, (seg, rows), 0) == rank

    for block in range(blocks):
        first = offset_ref[step * (blocks + 1) + block]
        count = count_ref[step * blocks + block]

        @pl.when(count > 0)
        def _():
            hit = picks(block)
            one = jnp.where(hit, 1.0, 0.0).astype(bf16)
            place = pl.ds(pl.multiple_of(first, 16), seg)
            xs[place, :] = mm(one, x_refs[block][:rows, :], NN).astype(bf16)
            cs[place, :] = mm(one, cot_refs[block][...], NN).astype(bf16)
            gates[place, :] = jnp.sum(jnp.where(hit, gate_row(block), 0.0), axis=1, keepdims=True)

    used = offset_ref[step * (blocks + 1) + blocks]

    def tile(t, carry):
        place = pl.ds(pl.multiple_of(t * RT, RT), RT)
        x, c, gate = xs[place, :], cs[place, :], gates[place, :]
        gate_pre = mm(x, w_ref[0, 0], NT)
        up_pre = mm(x, w_ref[0, 1], NT)
        sigmoid = jax.nn.sigmoid(gate_pre)
        active = gate_pre * sigmoid
        inner = active * up_pre
        plain = mm(c, w_ref[0, 2], NT)
        gate_grads[place, :] = jnp.sum(plain * inner, axis=1, keepdims=True)
        inner_grad = plain * gate
        gate_pre_grad = inner_grad * up_pre * sigmoid * (1.0 + gate_pre * (1.0 - sigmoid))
        gate_pre_grad = gate_pre_grad.astype(bf16)
        up_pre_grad = (inner_grad * active).astype(bf16)
        scaled = (inner * gate).astype(bf16)
        w_acc[0] += mm(gate_pre_grad, x, TN)
        w_acc[1] += mm(up_pre_grad, x, TN)
        w_acc[2] += mm(scaled, c, TN)
        cs[place, :] = mm(scaled, w_ref[0, 2], NN).astype(bf16)
        xs[place, :] = (
            mm(gate_pre_grad, w_ref[0, 0], NN) + mm(up_pre_grad, w_ref[0, 1], NN)
        ).astype(bf16)
        return carry

    lax.fori_loop(0, (used + RT - 1) // RT, tile, 0)

    for block in range(blocks):
        first = offset_ref[step * (blocks + 1) + block]
        count = count_ref[step * blocks + block]
        whole = slice(block * rows, (block + 1) * rows)

        @pl.when(count > 0)
        def _():
            hit = picks(block)
            one = jnp.where(hit, 1.0, 0.0).astype(bf16)
            place = pl.ds(pl.multiple_of(first, 16), seg)
            mixed_acc[whole, :] += mm(one, cs[place, :], TN)
            slot_acc[whole, :] += mm(one, xs[place, :], TN)
            tail[block, pl.ds(own, 1), :] = jnp.sum(
                jnp.where(hit, gate_grads[place, :], 0.0), axis=0, keepdims=True
            )

    w_grad_ref[0] = w_acc[...].astype(bf16)

    @pl.when(expert == pl.num_programs(1) - 1)
    def _():
        for block in range(blocks):
            place = slice(block * rows, (block + 1) * rows)
            mixed_refs[block][...] = mixed_acc[place, :].astype(bf16)
            slot_refs[block][:rows, :] = slot_acc[place, :].astype(bf16)
            upper = tail[block].astype(bf16)
            lower = (tail[block] - upper.astype(f32)).astype(bf16)
            terms = jnp.concatenate([upper, lower], axis=0)
            if part:
                terms = terms + slot_before[block][rows:, :rows]
            slot_refs[block][rows:, :] = jnp.concatenate(
                [terms, jnp.zeros((2 * high, D - rows), bf16)], axis=1
            )


def expert_layer(part, parts, rank, counts, x, cot, before, weights, rows, high):
    experts, blocks = weights.shape[0], len(x)
    height = blocks * rows
    chunks = rank.shape[0] // experts
    padded = -(-counts // 16) * 16
    offsets = jnp.concatenate(
        [jnp.zeros((chunks * experts, 1), jnp.int32), jnp.cumsum(padded, axis=1)], axis=1
    )
    room = -(-blocks * (rows // 2) // RT) * RT
    tall = rows + 2 * high

    def tokens(h, **mode):
        return [pl.BlockSpec((h, D), lambda c, e, a, b: (c, 0), **mode) for _ in range(blocks)]

    held = dict(pipeline_mode=pl.Buffered(1))
    line = pl.BlockSpec((1, 1, height), lambda c, e, a, b: (c * experts + e, 0, 0))
    weight = lambda: pl.BlockSpec((1, 3, FF, D), lambda c, e, a, b: (e, 0, 0, 0))
    out = pl.pallas_call(
        partial(expert_kernel, blocks, rows, part, parts),
        out_shape=[jax.ShapeDtypeStruct((chunks * rows, D), bf16)] * blocks
        + [jax.ShapeDtypeStruct((chunks * tall, D), bf16)] * blocks
        + [jax.ShapeDtypeStruct(weights.shape, bf16)],
        grid_spec=pltpu.PrefetchScalarGridSpec(
            num_scalar_prefetch=2,
            grid=(chunks, experts),
            in_specs=[line]
            + tokens(tall, **held)
            + tokens(rows, **held)
            + (tokens(rows, **held) + tokens(tall, **held) if part else [])
            + [weight()],
            out_specs=tokens(rows) + tokens(tall) + [weight()],
            scratch_shapes=[
                pltpu.VMEM((height, D), f32),
                pltpu.VMEM((height, D), f32),
                pltpu.VMEM((3, FF, D), f32),
                pltpu.VMEM((room, D), bf16),
                pltpu.VMEM((room, D), bf16),
                pltpu.VMEM((room, 1), f32),
                pltpu.VMEM((room, 1), f32),
                pltpu.VMEM((blocks, high, rows), f32),
            ],
        ),
        compiler_params=pltpu.CompilerParams(vmem_limit_bytes=58 << 20),
        cost_estimate=pl.CostEstimate(flops=1 << 20, bytes_accessed=1 << 20, transcendentals=0),
        name="experts",
    )(offsets.reshape(-1), counts.reshape(-1), rank, *x, *cot, *before, weights)
    return list(out[: 2 * blocks]), out[-1]


def angles(position):
    half = HD // 2
    frequency = rope_base ** (-jnp.arange(half, dtype=f32) * 2.0 / HD)
    angle = frequency[:, None] * position.astype(f32)[None, :]
    return jnp.cos(angle), jnp.sin(angle)


def rotate(values, cosine, sine):
    half = HD // 2
    parts = values.reshape(-1, HD, values.shape[1])
    first, second = parts[:, :half], parts[:, half:]
    return jnp.concatenate(
        [first * cosine - second * sine, second * cosine + first * sine], axis=1
    ).reshape(values.shape)


def doc_table(lengths, count):
    ends = jnp.cumsum(lengths)
    places = jnp.arange(count, dtype=jnp.int32)
    after = (places[None, :] >= ends[:, None]).astype(jnp.int32)
    starts = jnp.sum(after * lengths[:, None], axis=0)
    return (starts, places - starts)


def rank_table(choices, first, experts):
    named = (first + jnp.arange(experts, dtype=jnp.int32))[None, :, None, None]
    hits = jnp.any(choices[:, None, :, :] == named, axis=2)
    order = jnp.arange(choices.shape[2])
    before = (order[:, None] < order[None, :]).astype(bf16)
    rank = jnp.einsum("ber,rs->bes", hits.astype(bf16), before, preferred_element_type=f32)
    rank = jnp.where(hits, rank.astype(jnp.int32), -1)
    return rank, jnp.sum(hits.astype(jnp.int32), axis=2)


def shift(value, axis, step):
    size = lax.axis_size(axis)
    return lax.ppermute(value, axis, [(i, (i + step) % size) for i in range(size)])


def below(rows, values, parts):
    terms, rest = [], values.astype(f32)
    high = -(-values.shape[0] // 8) * 8
    rest = jnp.pad(rest, ((0, high - values.shape[0]), (0, D - values.shape[1])))
    for _ in range(parts):
        term = rest.astype(bf16)
        terms.append(term)
        rest = rest - term.astype(f32)
    if parts * high % 16:
        terms.append(jnp.zeros_like(term))
    return jnp.concatenate([rows] + terms, axis=0)


def total(values, axis):
    size = lax.axis_size(axis)
    distance = 1
    while distance < size:
        pairs = [(i, i ^ distance) for i in range(size)]
        other = [lax.ppermute(v, axis, pairs) for v in values]
        values = [(v.astype(f32) + o.astype(f32)).astype(v.dtype) for v, o in zip(values, other)]
        distance *= 2
    return values


def spread(values, axis):
    return lax.all_to_all(values, axis, split_axis=0, concat_axis=0, tiled=True)


def to_rows(values, ranks):
    width = values.shape[0]
    parts = values.reshape(width, ranks, -1).swapaxes(0, 1)
    return spread(parts, "tensor").reshape(ranks * width, -1)


def to_heads(values, ranks):
    parts = spread(values.reshape(ranks, -1, values.shape[1]), "tensor")
    return parts.swapaxes(0, 1).reshape(parts.shape[1], -1)


def adamw(weight, grad, first, second, rate, decay):
    first = beta_one * first + (1.0 - beta_one) * grad
    second = beta_two * second + (1.0 - beta_two) * grad * grad
    step = first / (1.0 - beta_one**STEP) / (jnp.sqrt(second / (1.0 - beta_two**STEP)) + adam_eps)
    return (first, second, weight - rate * (step + decay * weight))


def on_device(
    tokens,
    cotangent,
    doc_lengths,
    expert_choices,
    gains,
    gain_moment,
    gain_square,
    router,
    router_moment,
    router_square,
    w_attention,
    attention_moment,
    attention_square,
    w_out,
    out_moment,
    out_square,
    w_gate_up,
    gate_up_moment,
    gate_up_square,
    w_down,
    down_moment,
    down_square,
):
    ranks = lax.axis_size("tensor")
    peers = lax.axis_size("expert")
    rows = tokens.shape[0]
    group_rows = rows * ranks
    experts = w_gate_up.shape[0]
    blocks = min(peers, 4)
    halves = 2 if experts % 2 == 0 else 1
    half = experts // halves
    hidden = w_down.shape[1]

    inputs = tokens.astype(f32)
    scale_one = lax.rsqrt(jnp.mean(inputs * inputs, axis=-1, keepdims=True) + norm_eps)
    normed = (inputs * scale_one * gains[0]).astype(bf16)
    gathered = lax.all_gather(normed, "tensor", axis=0, tiled=True)

    attention_low = w_attention.reshape(D, -1).astype(bf16)
    out_low = w_out.reshape(-1, D).astype(bf16)
    expert_low = jnp.concatenate(
        [w_gate_up.swapaxes(2, 3).astype(bf16), w_down.astype(bf16)[:, None]], axis=1
    )
    width = out_low.shape[0]
    both_all = lax.all_gather(
        jnp.concatenate([out_low, attention_low.T], axis=0), "tensor", axis=0, tiled=False
    )
    out_all = both_all[:, :width].reshape(-1, D)
    attention_all = both_all[:, width:].reshape(-1, D)
    expert_all = [
        lax.all_gather(expert_low[part * half : (part + 1) * half], "tensor", axis=2, tiled=True)
        for part in range(halves)
    ]

    message = below(cotangent, expert_choices.T, 1)
    messages = [shift(message, "expert", d) for d in range(1, peers)]
    cot_in = [cotangent] + messages
    choices_in = [expert_choices.T] + [
        m[rows : rows + TOPK, :rows].astype(jnp.int32) for m in messages
    ]

    start, position = doc_table(doc_lengths[0], group_rows)
    cosine, sine = angles(position)
    lowest = start[::QT] // KT
    start = start[None, :]
    projected = jnp.einsum("dc,td->ct", attention_low, gathered, preferred_element_type=f32)
    turned = rotate(projected[: (G + 1) * HD], cosine, sine).astype(bf16)
    queries = turned[: G * HD] * bf16(HD ** (-0.5))
    keys_t = turned[G * HD :]
    values_t = projected[(G + 1) * HD :].astype(bf16)
    keys, values = keys_t.T, values_t.T
    heads, log_sums = attention_forward(lowest, start, queries, keys, values_t)

    heads_rows = to_rows(heads, ranks)
    attended = jnp.einsum("ct,cd->td", heads_rows, out_all, preferred_element_type=f32)
    state = inputs + attended
    scale_two = lax.rsqrt(jnp.mean(state * state, axis=-1, keepdims=True) + norm_eps)
    unit = state * scale_two
    normed_two = unit * gains[1]

    logits = lax.dot_general(router, normed_two, (((0,), (1,)), ((), ())), precision=highest)
    named = jnp.arange(EXPERTS, dtype=jnp.int32)[:, None, None]
    chosen = jnp.any(expert_choices.T[None, :, :] == named, axis=1)
    top = jnp.max(jnp.where(chosen, logits, -jnp.inf), axis=0, keepdims=True)
    weight = jnp.where(chosen, jnp.exp(jnp.where(chosen, logits - top, 0.0)), 0.0)
    gates = weight / jnp.sum(weight, axis=0, keepdims=True)

    me = lax.axis_index("expert")
    moved = normed_two.astype(bf16)
    by_peer = gates.reshape(peers, experts, rows)
    gates_to = [
        lax.dynamic_index_in_dim(by_peer, (me + d) % peers, 0, keepdims=False) for d in range(peers)
    ]
    high = -(-experts // 8) * 8
    x_in = [below(moved, gates_to[0], 2)]
    for d in range(1, peers):
        x_in.append(shift(below(moved, gates_to[d], 2), "expert", d))
    rank, counts = rank_table(jnp.stack(choices_in), me * experts, experts)

    def by_step(values):
        return values.reshape((-1, blocks) + values.shape[1:]).swapaxes(1, 2)

    def lay(values, height):
        if len(values) == blocks:
            return values
        return [jnp.concatenate([v[:height] for v in values[b::blocks]]) for b in range(blocks)]

    def unlay(values):
        if len(values) == peers:
            return values
        height = values[0].shape[0] * blocks // peers
        return [values[d % blocks][d // blocks * height :][:height] for d in range(peers)]

    rank_steps, count_steps = by_step(rank), by_step(counts)
    x_laid, cot_laid = lay(x_in, rows + 2 * high), lay(cot_in, rows)
    before, expert_grad = [], []
    for part in range(halves):
        own = slice(part * half, (part + 1) * half)
        before, grad_out = expert_layer(
            part,
            halves,
            rank_steps[:, own].reshape(-1, 1, blocks * rows),
            count_steps[:, own].reshape(-1, blocks),
            x_laid,
            cot_laid,
            before,
            expert_all[part],
            rows,
            high,
        )
        expert_grad.append(lax.psum_scatter(grad_out, "tensor", scatter_dimension=2, tiled=True))
    mixed_out, slot_out = unlay(before[:blocks]), unlay(before[blocks:])
    slot_back = [slot_out[0]] + [shift(slot_out[d], "expert", -d) for d in range(1, peers)]
    slot_back, mixed_out = lax.optimization_barrier((slot_back, mixed_out))
    mixed_back = [mixed_out[0]] + [shift(mixed_out[d], "expert", -d) for d in range(1, peers)]
    mixed = state + sum(v.astype(f32) for v in mixed_back)

    gate_grads = jnp.concatenate(
        [
            v[rows : rows + experts, :rows].astype(f32)
            + v[rows + high : rows + high + experts, :rows].astype(f32)
            for v in slot_back
        ]
    )
    near_gates = jnp.concatenate(gates_to)
    near_router = jnp.roll(router.T.reshape(peers, experts, D), -me, axis=0).reshape(EXPERTS, D)
    logit_grads = near_gates * (
        gate_grads - jnp.sum(near_gates * gate_grads, axis=0, keepdims=True)
    )
    router_grad = lax.dot_general(
        logit_grads, normed_two, (((1,), (0,)), ((), ())), precision=highest
    )
    router_grad = jnp.roll(router_grad.reshape(peers, experts, D), me, axis=0).reshape(EXPERTS, D)
    normed_two_grad = sum(v[:rows].astype(f32) for v in slot_back) + lax.dot_general(
        logit_grads, near_router, (((0,), (0,)), ((), ())), precision=highest
    )
    gain_two_grad = jnp.sum(normed_two_grad * unit, axis=0)
    unit_grad = normed_two_grad * gains[1]
    state_grad = cotangent.astype(f32) + scale_two * (
        unit_grad - unit * jnp.mean(unit_grad * unit, axis=-1, keepdims=True)
    )

    early = jnp.concatenate([router_grad, gain_two_grad[None]], axis=0)
    early = jnp.pad(early, ((0, -early.shape[0] % ranks), (0, 0))).reshape(ranks, -1, D)

    branch = state_grad.astype(bf16)
    head_grads_rows = jnp.einsum(
        "cd,td->ct", out_all, branch, preferred_element_type=f32
    ).astype(bf16)
    head_grads, expert_grad[0] = lax.optimization_barrier(
        (to_heads(head_grads_rows, ranks), expert_grad[0])
    )
    out_grad = jnp.einsum("ct,td->cd", heads_rows, branch, preferred_element_type=f32)
    out_grad = spread(out_grad.astype(bf16).reshape(ranks, -1, D), "tensor")
    query_grad, key_grad, value_grad = attention_backward(
        lowest, start, queries, heads, head_grads, log_sums, keys, keys_t, values
    )
    value_grad, out_grad, early = lax.optimization_barrier((value_grad, out_grad, early))
    out_grad = jnp.sum(out_grad.astype(f32), axis=0)
    turned_grad = rotate(jnp.concatenate([query_grad, key_grad], axis=0), cosine, -sine)
    projected_grad = jnp.concatenate([turned_grad, value_grad], axis=0).astype(bf16)
    attention_grad = jnp.einsum(
        "td,ct->dc", gathered, projected_grad, preferred_element_type=f32
    )
    gain_one_grad = (
        jnp.sum(attention_grad * attention_low.astype(f32), axis=1) / gains[0]
    )
    projected_late, expert_grad[-1] = lax.optimization_barrier(
        (projected_grad, expert_grad[-1])
    )
    projected_rows = to_rows(projected_late, ranks)
    normed_grad = jnp.einsum(
        "ct,cd->td", projected_rows, attention_all, preferred_element_type=f32
    )
    unit_one = inputs * scale_one
    unit_one_grad = normed_grad * gains[0]
    input_grad = state_grad + scale_one * (
        unit_one_grad - unit_one * jnp.mean(unit_one_grad * unit_one, axis=-1, keepdims=True)
    )

    early = jnp.sum(spread(early, "tensor"), axis=0)
    early = total([early], "expert")[0]
    early = spread(jnp.broadcast_to(early[None], (ranks,) + early.shape), "tensor").reshape(-1, D)
    router_grad, gain_two_grad = early[:EXPERTS].T, early[EXPERTS]
    attention_grad, out_grad = lax.psum(
        (attention_grad.astype(bf16), out_grad.astype(bf16)), "expert"
    )
    attention_grad = attention_grad.astype(f32).reshape(-1, 128)
    out_grad = out_grad.astype(f32).reshape(w_out.shape)
    gain_one_grad, projected_rows = lax.optimization_barrier((gain_one_grad, projected_rows))
    gain_one_grad = total(total([gain_one_grad[None]], "expert"), "tensor")[0][0]
    gain_grad = jnp.stack([gain_one_grad, gain_two_grad])
    expert_grad = jnp.concatenate(expert_grad, axis=0).astype(f32)
    gate_up_grad, down_grad = expert_grad[:, :2], expert_grad[:, 2]
    gain_first, gain_second, gain_new = adamw(gains, gain_grad, gain_moment, gain_square, 1.0, 0.0)
    router_first, router_second, router_new = adamw(
        router, router_grad, router_moment, router_square, D ** (-0.5), decay_rate
    )
    attention_first, attention_second, attention_new = (
        v.reshape(w_attention.shape)
        for v in adamw(
            w_attention.reshape(-1, 128),
            attention_grad,
            attention_moment.reshape(-1, 128),
            attention_square.reshape(-1, 128),
            2.0 * D ** (-0.5),
            decay_rate,
        )
    )
    out_first, out_second, out_new = adamw(
        w_out, out_grad, out_moment, out_square, 16.0 * (H * HD) ** (-0.5), decay_rate
    )
    gate_up_first, gate_up_second, gate_up_new = adamw(
        w_gate_up,
        gate_up_grad.swapaxes(2, 3),
        gate_up_moment,
        gate_up_square,
        2.0 * D ** (-0.5),
        decay_rate,
    )
    down_first, down_second, down_new = adamw(
        w_down, down_grad, down_moment, down_square, 8.0 * FF ** (-0.5), decay_rate
    )
    return (
        mixed,
        input_grad,
        gain_first,
        gain_second,
        gain_new,
        router_first,
        router_second,
        router_new,
        attention_first,
        attention_second,
        attention_new,
        out_first,
        out_second,
        out_new,
        gate_up_first,
        gate_up_second,
        gate_up_new,
        down_first,
        down_second,
        down_new,
    )


def solution(mesh):
    placed = (
        P(("expert", "tensor"), None),
        P(("expert", "tensor"), None),
        P("expert", None),
        P(("expert", "tensor"), None),
        P(),
        P(),
        P(),
        P(),
        P(),
        P(),
        P(None, "tensor", None),
        P(None, "tensor", None),
        P(None, "tensor", None),
        P("tensor", None, None),
        P("tensor", None, None),
        P("tensor", None, None),
        P("expert", None, None, "tensor"),
        P("expert", None, None, "tensor"),
        P("expert", None, None, "tensor"),
        P("expert", "tensor", None),
        P("expert", "tensor", None),
        P("expert", "tensor", None),
    )
    return jax.shard_map(
        on_device,
        mesh=mesh,
        in_specs=placed,
        out_specs=(
            P(("expert", "tensor"), None),
            P(("expert", "tensor"), None),
            P(),
            P(),
            P(),
            P(),
            P(),
            P(),
            P(None, "tensor", None),
            P(None, "tensor", None),
            P(None, "tensor", None),
            P("tensor", None, None),
            P("tensor", None, None),
            P("tensor", None, None),
            P("expert", None, None, "tensor"),
            P("expert", None, None, "tensor"),
            P("expert", None, None, "tensor"),
            P("expert", "tensor", None),
            P("expert", "tensor", None),
            P("expert", "tensor", None),
        ),
        check_vma=False,
    )
```

```python
from functools import partial

import jax
import jax.numpy as jnp
from jax import lax
from jax.experimental import pallas as pl
from jax.experimental.pallas import tpu as pltpu
from jax.sharding import PartitionSpec as P

D = 1024
H = 16
HD = 64
FF = 512
EXPERTS = 32
TOPK = 8
G = 2
STEP = 10

norm_eps = 1e-06
rope_base = 10000.0
masked_score = -1e30
beta_one = 0.9
beta_two = 0.95
adam_eps = 1e-08
decay_rate = 0.1
highest = lax.Precision.HIGHEST

QT = 256
KT = 256
RT = 256

f32 = jnp.float32
bf16 = jnp.bfloat16

NN = (((1,), (0,)), ((), ()))
NT = (((1,), (1,)), ((), ()))
TN = (((0,), (0,)), ((), ()))


def mm(a, b, dims):
    return lax.dot_general(a, b, dims, preferred_element_type=f32)


def attention_tile(j, i, start, k_ref):
    keys = k_ref[pl.ds(pl.multiple_of(j * KT, KT), KT), :]
    key_id = j * KT + lax.broadcasted_iota(jnp.int32, (KT, QT), 0)
    row_id = i * QT + lax.broadcasted_iota(jnp.int32, (KT, QT), 1)
    return keys, (key_id >= start) & (key_id <= row_id)


def attention_forward_kernel(low_ref, start_ref, q_ref, k_ref, v_ref, o_ref, sum_ref):
    i = pl.program_id(0)
    start = start_ref[...]

    def step(j, carry):
        keys, mask = attention_tile(j, i, start, k_ref)
        values = v_ref[:, pl.ds(pl.multiple_of(j * KT, KT), KT)]
        out = []
        for g in range(G):
            top, total, acc = carry[g]
            scores = mm(keys, q_ref[g * HD : (g + 1) * HD, :], NN)
            scores = jnp.where(mask, scores, masked_score)
            new_top = jnp.maximum(top, jnp.max(scores, axis=0, keepdims=True))
            probs = jnp.exp(scores - new_top)
            shrink = jnp.exp(top - new_top)
            total = total * shrink + jnp.sum(probs, axis=0, keepdims=True)
            acc = acc * shrink + mm(values, probs.astype(bf16), NN)
            out.append((new_top, total, acc))
        return tuple(out)

    zero = (
        jnp.full((1, QT), masked_score, f32),
        jnp.zeros((1, QT), f32),
        jnp.zeros((HD, QT), f32),
    )
    done = lax.fori_loop(low_ref[i], i + 1, step, (zero,) * G)
    for g in range(G):
        top, total, acc = done[g]
        o_ref[g * HD : (g + 1) * HD, :] = (acc / total).astype(bf16)
        sum_ref[g : g + 1, :] = top + jnp.log(total)


def attention_backward_kernel(
    low_ref, start_ref, q_ref, o_ref, d_ref, sum_ref, k_ref, kt_ref, v_ref, dq_ref, dk_ref, dv_ref
):
    i = pl.program_id(0)
    start = start_ref[...]

    @pl.when(i == 0)
    def _():
        dk_ref[...] = jnp.zeros_like(dk_ref)
        dv_ref[...] = jnp.zeros_like(dv_ref)

    grads, inner = [], []
    for g in range(G):
        part = slice(g * HD, (g + 1) * HD)
        grads.append(d_ref[part, :])
        inner.append(
            jnp.sum(d_ref[part, :].astype(f32) * o_ref[part, :].astype(f32), axis=0, keepdims=True)
        )

    def step(j, carry):
        keys, mask = attention_tile(j, i, start, k_ref)
        columns = pl.ds(pl.multiple_of(j * KT, KT), KT)
        values = v_ref[columns, :]
        keys_t = kt_ref[:, columns]
        dk = jnp.zeros((HD, KT), f32)
        dv = jnp.zeros((HD, KT), f32)
        out = []
        for g in range(G):
            query = q_ref[g * HD : (g + 1) * HD, :]
            scores = mm(keys, query, NN)
            probs = jnp.where(mask, jnp.exp(scores - sum_ref[g : g + 1, :]), 0.0)
            probs_grad = mm(values, grads[g], NN)
            score_grad = (probs * (probs_grad - inner[g])).astype(bf16)
            dv += mm(grads[g], probs.astype(bf16), NT)
            dk += mm(query, score_grad, NT)
            out.append(carry[g] + mm(keys_t, score_grad, NN))
        dk_ref[:, columns] += dk
        dv_ref[:, columns] += dv
        return tuple(out)

    done = lax.fori_loop(low_ref[i], i + 1, step, (jnp.zeros((HD, QT), f32),) * G)
    for g in range(G):
        dq_ref[g * HD : (g + 1) * HD, :] = done[g] * HD ** (-0.5)


def attention_forward(low, start, q, k, vt):
    rows = q.shape[1]
    tile = lambda height: pl.BlockSpec((height, QT), lambda i, s: (0, i))
    whole = lambda a: pl.BlockSpec(a.shape, lambda i, s: (0, 0))
    return pl.pallas_call(
        attention_forward_kernel,
        out_shape=(
            jax.ShapeDtypeStruct((G * HD, rows), bf16),
            jax.ShapeDtypeStruct((G, rows), f32),
        ),
        grid_spec=pltpu.PrefetchScalarGridSpec(
            num_scalar_prefetch=1,
            grid=(rows // QT,),
            in_specs=[tile(1), tile(G * HD), whole(k), whole(vt)],
            out_specs=[tile(G * HD), tile(G)],
        ),
        compiler_params=pltpu.CompilerParams(vmem_limit_bytes=24 << 20),
        cost_estimate=pl.CostEstimate(flops=1 << 20, bytes_accessed=1 << 20, transcendentals=0),
        name="attention_forward",
    )(low, start, q, k, vt)


def attention_backward(low, start, q, o, d, sums, k, kt, v):
    rows = q.shape[1]
    tile = lambda height: pl.BlockSpec((height, QT), lambda i, s: (0, i))
    whole = lambda a: pl.BlockSpec(a.shape, lambda i, s: (0, 0))
    return pl.pallas_call(
        attention_backward_kernel,
        out_shape=(
            jax.ShapeDtypeStruct((G * HD, rows), f32),
            jax.ShapeDtypeStruct((HD, rows), f32),
            jax.ShapeDtypeStruct((HD, rows), f32),
        ),
        grid_spec=pltpu.PrefetchScalarGridSpec(
            num_scalar_prefetch=1,
            grid=(rows // QT,),
            in_specs=[tile(1), tile(G * HD), tile(G * HD), tile(G * HD), tile(G)]
            + [whole(k), whole(kt), whole(v)],
            out_specs=[tile(G * HD), whole(kt), whole(kt)],
        ),
        compiler_params=pltpu.CompilerParams(vmem_limit_bytes=24 << 20),
        cost_estimate=pl.CostEstimate(flops=1 << 20, bytes_accessed=1 << 20, transcendentals=0),
        name="attention_backward",
    )(low, start, q, o, d, sums, k, kt, v)


def expert_kernel(blocks, rows, part, parts, offset_ref, count_ref, rank_ref, *refs):
    take = lambda n: (refs[:n], refs[n:])
    x_refs, refs = take(blocks)
    cot_refs, refs = take(blocks)
    mixed_before, refs = take(blocks if part else 0)
    slot_before, refs = take(blocks if part else 0)
    (w_ref,), refs = take(1)
    mixed_refs, refs = take(blocks)
    slot_refs, refs = take(blocks)
    w_grad_ref, mixed_acc, slot_acc, w_acc, xs, cs, gates, gate_grads, tail = refs
    high = tail.shape[1]
    seg = rows // 2
    chunk, expert = pl.program_id(0), pl.program_id(1)
    step = chunk * pl.num_programs(1) + expert

    @pl.when(step == 0)
    def _():
        xs[...] = jnp.zeros_like(xs)
        cs[...] = jnp.zeros_like(cs)

    @pl.when(expert == 0)
    def _():
        tail[...] = jnp.zeros_like(tail)
        if part:
            for block in range(blocks):
                place = slice(block * rows, (block + 1) * rows)
                mixed_acc[place, :] = mixed_before[block][...].astype(f32)
                slot_acc[place, :] = slot_before[block][:rows, :].astype(f32)
        else:
            mixed_acc[...] = jnp.zeros_like(mixed_acc)
            slot_acc[...] = jnp.zeros_like(slot_acc)

    @pl.when((chunk == 0) | (pl.num_programs(1) > 1))
    def _():
        w_acc[...] = jnp.zeros_like(w_acc)

    gates[...] = jnp.zeros_like(gates)
    own = part * pl.num_programs(1) + expert

    def gate_row(block):
        terms = x_refs[block][rows:, :rows].astype(f32)
        terms = terms[:high] + terms[high:]
        here = lax.broadcasted_iota(jnp.int32, (high, rows), 0) == own
        return jnp.sum(jnp.where(here, terms, 0.0), axis=0, keepdims=True)

    def picks(block):
        rank = rank_ref[0, :, block * rows : (block + 1) * rows]
        return lax.broadcasted_iota(jnp.int32, (seg, rows), 0) == rank

    for block in range(blocks):
        first = offset_ref[step * (blocks + 1) + block]
        count = count_ref[step * blocks + block]

        @pl.when(count > 0)
        def _():
            hit = picks(block)
            one = jnp.where(hit, 1.0, 0.0).astype(bf16)
            place = pl.ds(pl.multiple_of(first, 16), seg)
            xs[place, :] = mm(one, x_refs[block][:rows, :], NN).astype(bf16)
            cs[place, :] = mm(one, cot_refs[block][...], NN).astype(bf16)
            gates[place, :] = jnp.sum(jnp.where(hit, gate_row(block), 0.0), axis=1, keepdims=True)

    used = offset_ref[step * (blocks + 1) + blocks]

    def tile(t, carry):
        place = pl.ds(pl.multiple_of(t * RT, RT), RT)
        x, c, gate = xs[place, :], cs[place, :], gates[place, :]
        gate_pre = mm(x, w_ref[0, 0], NT)
        up_pre = mm(x, w_ref[0, 1], NT)
        sigmoid = jax.nn.sigmoid(gate_pre)
        active = gate_pre * sigmoid
        inner = active * up_pre
        plain = mm(c, w_ref[0, 2], NT)
        gate_grads[place, :] = jnp.sum(plain * inner, axis=1, keepdims=True)
        inner_grad = plain * gate
        gate_pre_grad = inner_grad * up_pre * sigmoid * (1.0 + gate_pre * (1.0 - sigmoid))
        gate_pre_grad = gate_pre_grad.astype(bf16)
        up_pre_grad = (inner_grad * active).astype(bf16)
        scaled = (inner * gate).astype(bf16)
        w_acc[0] += mm(gate_pre_grad, x, TN)
        w_acc[1] += mm(up_pre_grad, x, TN)
        w_acc[2] += mm(scaled, c, TN)
        cs[place, :] = mm(scaled, w_ref[0, 2], NN).astype(bf16)
        xs[place, :] = (
            mm(gate_pre_grad, w_ref[0, 0], NN) + mm(up_pre_grad, w_ref[0, 1], NN)
        ).astype(bf16)
        return carry

    lax.fori_loop(0, (used + RT - 1) // RT, tile, 0)

    for block in range(blocks):
        first = offset_ref[step * (blocks + 1) + block]
        count = count_ref[step * blocks + block]
        whole = slice(block * rows, (block + 1) * rows)

        @pl.when(count > 0)
        def _():
            hit = picks(block)
            one = jnp.where(hit, 1.0, 0.0).astype(bf16)
            place = pl.ds(pl.multiple_of(first, 16), seg)
            mixed_acc[whole, :] += mm(one, cs[place, :], TN)
            slot_acc[whole, :] += mm(one, xs[place, :], TN)
            tail[block, pl.ds(own, 1), :] = jnp.sum(
                jnp.where(hit, gate_grads[place, :], 0.0), axis=0, keepdims=True
            )

    w_grad_ref[0] = w_acc[...].astype(bf16)

    @pl.when(expert == pl.num_programs(1) - 1)
    def _():
        for block in range(blocks):
            place = slice(block * rows, (block + 1) * rows)
            mixed_refs[block][...] = mixed_acc[place, :].astype(bf16)
            slot_refs[block][:rows, :] = slot_acc[place, :].astype(bf16)
            upper = tail[block].astype(bf16)
            lower = (tail[block] - upper.astype(f32)).astype(bf16)
            terms = jnp.concatenate([upper, lower], axis=0)
            if part:
                terms = terms + slot_before[block][rows:, :rows]
            slot_refs[block][rows:, :] = jnp.concatenate(
                [terms, jnp.zeros((2 * high, D - rows), bf16)], axis=1
            )


def expert_layer(part, parts, rank, counts, x, cot, before, weights, rows, high):
    experts, blocks = weights.shape[0], len(x)
    height = blocks * rows
    chunks = rank.shape[0] // experts
    padded = -(-counts // 16) * 16
    offsets = jnp.concatenate(
        [jnp.zeros((chunks * experts, 1), jnp.int32), jnp.cumsum(padded, axis=1)], axis=1
    )
    room = -(-blocks * (rows // 2) // RT) * RT
    tall = rows + 2 * high

    def tokens(h, **mode):
        return [pl.BlockSpec((h, D), lambda c, e, a, b: (c, 0), **mode) for _ in range(blocks)]

    held = dict(pipeline_mode=pl.Buffered(1))
    line = pl.BlockSpec((1, 1, height), lambda c, e, a, b: (c * experts + e, 0, 0))
    weight = lambda: pl.BlockSpec((1, 3, FF, D), lambda c, e, a, b: (e, 0, 0, 0))
    out = pl.pallas_call(
        partial(expert_kernel, blocks, rows, part, parts),
        out_shape=[jax.ShapeDtypeStruct((chunks * rows, D), bf16)] * blocks
        + [jax.ShapeDtypeStruct((chunks * tall, D), bf16)] * blocks
        + [jax.ShapeDtypeStruct(weights.shape, bf16)],
        grid_spec=pltpu.PrefetchScalarGridSpec(
            num_scalar_prefetch=2,
            grid=(chunks, experts),
            in_specs=[line]
            + tokens(tall, **held)
            + tokens(rows, **held)
            + (tokens(rows, **held) + tokens(tall, **held) if part else [])
            + [weight()],
            out_specs=tokens(rows) + tokens(tall) + [weight()],
            scratch_shapes=[
                pltpu.VMEM((height, D), f32),
                pltpu.VMEM((height, D), f32),
                pltpu.VMEM((3, FF, D), f32),
                pltpu.VMEM((room, D), bf16),
                pltpu.VMEM((room, D), bf16),
                pltpu.VMEM((room, 1), f32),
                pltpu.VMEM((room, 1), f32),
                pltpu.VMEM((blocks, high, rows), f32),
            ],
        ),
        compiler_params=pltpu.CompilerParams(vmem_limit_bytes=58 << 20),
        cost_estimate=pl.CostEstimate(flops=1 << 20, bytes_accessed=1 << 20, transcendentals=0),
        name="experts",
    )(offsets.reshape(-1), counts.reshape(-1), rank, *x, *cot, *before, weights)
    return list(out[: 2 * blocks]), out[-1]


def angles(position):
    half = HD // 2
    frequency = rope_base ** (-jnp.arange(half, dtype=f32) * 2.0 / HD)
    angle = frequency[:, None] * position.astype(f32)[None, :]
    return jnp.cos(angle), jnp.sin(angle)


def rotate(values, cosine, sine):
    half = HD // 2
    parts = values.reshape(-1, HD, values.shape[1])
    first, second = parts[:, :half], parts[:, half:]
    return jnp.concatenate(
        [first * cosine - second * sine, second * cosine + first * sine], axis=1
    ).reshape(values.shape)


def doc_table(lengths, count):
    ends = jnp.cumsum(lengths)
    places = jnp.arange(count, dtype=jnp.int32)
    after = (places[None, :] >= ends[:, None]).astype(jnp.int32)
    starts = jnp.sum(after * lengths[:, None], axis=0)
    return (starts, places - starts)


def rank_table(choices, first, experts):
    named = (first + jnp.arange(experts, dtype=jnp.int32))[None, :, None, None]
    hits = jnp.any(choices[:, None, :, :] == named, axis=2)
    order = jnp.arange(choices.shape[2])
    before = (order[:, None] < order[None, :]).astype(bf16)
    rank = jnp.einsum("ber,rs->bes", hits.astype(bf16), before, preferred_element_type=f32)
    rank = jnp.where(hits, rank.astype(jnp.int32), -1)
    return rank, jnp.sum(hits.astype(jnp.int32), axis=2)


def shift(value, axis, step):
    size = lax.axis_size(axis)
    return lax.ppermute(value, axis, [(i, (i + step) % size) for i in range(size)])


def below(rows, values, parts):
    terms, rest = [], values.astype(f32)
    high = -(-values.shape[0] // 8) * 8
    rest = jnp.pad(rest, ((0, high - values.shape[0]), (0, D - values.shape[1])))
    for _ in range(parts):
        term = rest.astype(bf16)
        terms.append(term)
        rest = rest - term.astype(f32)
    if parts * high % 16:
        terms.append(jnp.zeros_like(term))
    return jnp.concatenate([rows] + terms, axis=0)


def total(values, axis):
    size = lax.axis_size(axis)
    distance = 1
    while distance < size:
        pairs = [(i, i ^ distance) for i in range(size)]
        other = [lax.ppermute(v, axis, pairs) for v in values]
        values = [(v.astype(f32) + o.astype(f32)).astype(v.dtype) for v, o in zip(values, other)]
        distance *= 2
    return values


def spread(values, axis):
    return lax.all_to_all(values, axis, split_axis=0, concat_axis=0, tiled=True)


def to_rows(values, ranks):
    width = values.shape[0]
    parts = values.reshape(width, ranks, -1).swapaxes(0, 1)
    return spread(parts, "tensor").reshape(ranks * width, -1)


def to_heads(values, ranks):
    parts = spread(values.reshape(ranks, -1, values.shape[1]), "tensor")
    return parts.swapaxes(0, 1).reshape(parts.shape[1], -1)


def adamw(weight, grad, first, second, rate, decay):
    first = beta_one * first + (1.0 - beta_one) * grad
    second = beta_two * second + (1.0 - beta_two) * grad * grad
    step = first / (1.0 - beta_one**STEP) / (jnp.sqrt(second / (1.0 - beta_two**STEP)) + adam_eps)
    return (first, second, weight - rate * (step + decay * weight))


def adamw_kernel(rate, weight_ref, grad_ref, first_ref, second_ref, *out_refs):
    out = adamw(
        weight_ref[...], grad_ref[...].astype(f32), first_ref[...], second_ref[...], rate, decay_rate
    )
    for ref, value in zip(out_refs, out):
        ref[...] = value


def adamw_rows(weight, grad, first, second, rate):
    block = pl.BlockSpec((weight.shape[0] // 4, weight.shape[1]), lambda i: (i, 0))
    return pl.pallas_call(
        partial(adamw_kernel, rate),
        out_shape=[jax.ShapeDtypeStruct(weight.shape, f32)] * 3,
        grid=(4,),
        in_specs=[block] * 4,
        out_specs=[block] * 3,
        compiler_params=pltpu.CompilerParams(vmem_limit_bytes=16 << 20),
        cost_estimate=pl.CostEstimate(flops=1 << 20, bytes_accessed=1 << 20, transcendentals=0),
        name="adamw",
    )(weight, grad, first, second)


def on_device(
    tokens,
    cotangent,
    doc_lengths,
    expert_choices,
    gains,
    gain_moment,
    gain_square,
    router,
    router_moment,
    router_square,
    w_attention,
    attention_moment,
    attention_square,
    w_out,
    out_moment,
    out_square,
    w_gate_up,
    gate_up_moment,
    gate_up_square,
    w_down,
    down_moment,
    down_square,
):
    ranks = lax.axis_size("tensor")
    peers = lax.axis_size("expert")
    rows = tokens.shape[0]
    group_rows = rows * ranks
    experts = w_gate_up.shape[0]
    blocks = min(peers, 4)
    halves = 2 if experts % 2 == 0 else 1
    half = experts // halves
    hidden = w_down.shape[1]

    inputs = tokens.astype(f32)
    scale_one = lax.rsqrt(jnp.mean(inputs * inputs, axis=-1, keepdims=True) + norm_eps)
    normed = (inputs * scale_one * gains[0]).astype(bf16)
    gathered = lax.all_gather(normed, "tensor", axis=0, tiled=True)

    attention_low = w_attention.reshape(D, -1).astype(bf16)
    out_low = w_out.reshape(-1, D).astype(bf16)
    expert_low = jnp.concatenate(
        [w_gate_up.swapaxes(2, 3).astype(bf16), w_down.astype(bf16)[:, None]], axis=1
    )
    out_all = lax.all_gather(out_low, "tensor", axis=0, tiled=True)
    expert_all = [
        lax.all_gather(expert_low[part * half : (part + 1) * half], "tensor", axis=2, tiled=True)
        for part in range(halves)
    ]

    attention_all = lax.all_gather(attention_low.T, "tensor", axis=0, tiled=True)

    message = below(cotangent, expert_choices.T, 1)
    messages = [shift(message, "expert", d) for d in range(1, peers)]
    cot_in = [cotangent] + messages
    choices_in = [expert_choices.T] + [
        m[rows : rows + TOPK, :rows].astype(jnp.int32) for m in messages
    ]

    start, position = doc_table(doc_lengths[0], group_rows)
    cosine, sine = angles(position)
    lowest = start[::QT] // KT
    start = start[None, :]
    projected = jnp.einsum("dc,td->ct", attention_low, gathered, preferred_element_type=f32)
    turned = rotate(projected[: (G + 1) * HD], cosine, sine).astype(bf16)
    queries = turned[: G * HD] * bf16(HD ** (-0.5))
    keys_t = turned[G * HD :]
    values_t = projected[(G + 1) * HD :].astype(bf16)
    keys, values = keys_t.T, values_t.T
    heads, log_sums = attention_forward(lowest, start, queries, keys, values_t)

    heads_rows = to_rows(heads, ranks)
    attended = jnp.einsum("ct,cd->td", heads_rows, out_all, preferred_element_type=f32)
    state = inputs + attended
    scale_two = lax.rsqrt(jnp.mean(state * state, axis=-1, keepdims=True) + norm_eps)
    unit = state * scale_two
    normed_two = unit * gains[1]

    logits = lax.dot_general(router, normed_two, (((0,), (1,)), ((), ())), precision=highest)
    named = jnp.arange(EXPERTS, dtype=jnp.int32)[:, None, None]
    chosen = jnp.any(expert_choices.T[None, :, :] == named, axis=1)
    top = jnp.max(jnp.where(chosen, logits, -jnp.inf), axis=0, keepdims=True)
    weight = jnp.where(chosen, jnp.exp(jnp.where(chosen, logits - top, 0.0)), 0.0)
    gates = weight / jnp.sum(weight, axis=0, keepdims=True)

    me = lax.axis_index("expert")
    moved = normed_two.astype(bf16)
    by_peer = gates.reshape(peers, experts, rows)
    gates_to = [
        lax.dynamic_index_in_dim(by_peer, (me + d) % peers, 0, keepdims=False) for d in range(peers)
    ]
    high = -(-experts // 8) * 8
    x_in = [below(moved, gates_to[0], 2)]
    for d in range(1, peers):
        x_in.append(shift(below(moved, gates_to[d], 2), "expert", d))
    rank, counts = rank_table(jnp.stack(choices_in), me * experts, experts)

    def by_step(values):
        return values.reshape((-1, blocks) + values.shape[1:]).swapaxes(1, 2)

    def lay(values, height):
        if len(values) == blocks:
            return values
        return [jnp.concatenate([v[:height] for v in values[b::blocks]]) for b in range(blocks)]

    def unlay(values):
        if len(values) == peers:
            return values
        height = values[0].shape[0] * blocks // peers
        return [values[d % blocks][d // blocks * height :][:height] for d in range(peers)]

    rank_steps, count_steps = by_step(rank), by_step(counts)
    x_laid, cot_laid = lay(x_in, rows + 2 * high), lay(cot_in, rows)
    before, expert_grad = [], []
    for part in range(halves):
        own = slice(part * half, (part + 1) * half)
        before, grad_out = expert_layer(
            part,
            halves,
            rank_steps[:, own].reshape(-1, 1, blocks * rows),
            count_steps[:, own].reshape(-1, blocks),
            x_laid,
            cot_laid,
            before,
            expert_all[part],
            rows,
            high,
        )
        expert_grad.append(lax.psum_scatter(grad_out, "tensor", scatter_dimension=2, tiled=True))
    mixed_out, slot_out = unlay(before[:blocks]), unlay(before[blocks:])
    slot_out, attention_all = lax.optimization_barrier((slot_out, attention_all))
    slot_back = [slot_out[0]] + [shift(slot_out[d], "expert", -d) for d in range(1, peers)]
    gate_grads = jnp.concatenate(
        [
            v[rows : rows + experts, :rows].astype(f32)
            + v[rows + high : rows + high + experts, :rows].astype(f32)
            for v in slot_back
        ]
    )
    near_gates = jnp.concatenate(gates_to)
    near_router = jnp.roll(router.T.reshape(peers, experts, D), -me, axis=0).reshape(EXPERTS, D)
    logit_grads = near_gates * (
        gate_grads - jnp.sum(near_gates * gate_grads, axis=0, keepdims=True)
    )
    router_grad = lax.dot_general(
        logit_grads, normed_two, (((1,), (0,)), ((), ())), precision=highest
    )
    router_grad = jnp.roll(router_grad.reshape(peers, experts, D), me, axis=0).reshape(EXPERTS, D)
    normed_two_grad = sum(v[:rows].astype(f32) for v in slot_back) + lax.dot_general(
        logit_grads, near_router, (((0,), (0,)), ((), ())), precision=highest
    )
    gain_two_grad = jnp.sum(normed_two_grad * unit, axis=0)
    unit_grad = normed_two_grad * gains[1]
    state_grad = cotangent.astype(f32) + scale_two * (
        unit_grad - unit * jnp.mean(unit_grad * unit, axis=-1, keepdims=True)
    )

    early = jnp.concatenate([router_grad, gain_two_grad[None]], axis=0)
    early = jnp.pad(early, ((0, -early.shape[0] % ranks), (0, 0))).reshape(ranks, -1, D)

    branch = state_grad.astype(bf16)
    head_grads_rows = jnp.einsum(
        "cd,td->ct", out_all, branch, preferred_element_type=f32
    ).astype(bf16)
    head_grads, expert_grad[0] = lax.optimization_barrier(
        (to_heads(head_grads_rows, ranks), expert_grad[0])
    )
    slot_back, mixed_out = lax.optimization_barrier((slot_back, mixed_out))
    mixed_back = [mixed_out[0]] + [shift(mixed_out[d], "expert", -d) for d in range(1, peers)]
    out_grad = jnp.einsum("ct,td->cd", heads_rows, branch, preferred_element_type=f32)
    out_grad = spread(out_grad.astype(bf16).reshape(ranks, -1, D), "tensor")
    query_grad, key_grad, value_grad = attention_backward(
        lowest, start, queries, heads, head_grads, log_sums, keys, keys_t, values
    )
    value_grad, out_grad, mixed_back = lax.optimization_barrier((value_grad, out_grad, mixed_back))
    mixed = state + sum(v.astype(f32) for v in mixed_back)
    out_grad = jnp.sum(out_grad.astype(f32), axis=0)
    turned_grad = rotate(jnp.concatenate([query_grad, key_grad], axis=0), cosine, -sine)
    projected_grad = jnp.concatenate([turned_grad, value_grad], axis=0).astype(bf16)
    attention_grad = jnp.einsum(
        "td,ct->dc", gathered, projected_grad, preferred_element_type=f32
    )
    gain_one_grad = (
        jnp.sum(attention_grad * attention_low.astype(f32), axis=1) / gains[0]
    )
    projected_late, expert_grad[-1] = lax.optimization_barrier(
        (projected_grad, expert_grad[-1])
    )
    projected_rows = to_rows(projected_late, ranks)
    projected_rows, early, gain_one_grad = lax.optimization_barrier(
        (projected_rows, early, gain_one_grad)
    )
    normed_grad = jnp.einsum(
        "ct,cd->td", projected_rows, attention_all, preferred_element_type=f32
    )
    attention_grad, out_grad = lax.psum(
        (attention_grad.astype(bf16), out_grad.astype(bf16)), "expert"
    )
    unit_one = inputs * scale_one
    unit_one_grad = normed_grad * gains[0]
    input_grad = state_grad + scale_one * (
        unit_one_grad - unit_one * jnp.mean(unit_one_grad * unit_one, axis=-1, keepdims=True)
    )

    early = jnp.sum(spread(early, "tensor"), axis=0)
    early = total([early], "expert")[0]
    early, attention_grad, out_grad = lax.optimization_barrier((early, attention_grad, out_grad))
    early = spread(jnp.broadcast_to(early[None], (ranks,) + early.shape), "tensor").reshape(-1, D)
    router_grad, gain_two_grad = early[:EXPERTS].T, early[EXPERTS]
    out_grad = out_grad.astype(f32).reshape(w_out.shape)
    gain_one_grad = total(total([gain_one_grad[None]], "expert"), "tensor")[0][0]
    gain_grad = jnp.stack([gain_one_grad, gain_two_grad])
    expert_grad = jnp.concatenate(expert_grad, axis=0).astype(f32)
    gate_up_grad, down_grad = expert_grad[:, :2], expert_grad[:, 2]
    gain_first, gain_second, gain_new = adamw(gains, gain_grad, gain_moment, gain_square, 1.0, 0.0)
    router_first, router_second, router_new = adamw(
        router, router_grad, router_moment, router_square, D ** (-0.5), decay_rate
    )
    attention_first, attention_second, attention_new = (
        v.reshape(w_attention.shape)
        for v in adamw_rows(
            w_attention.reshape(-1, 128),
            attention_grad.reshape(-1, 128),
            attention_moment.reshape(-1, 128),
            attention_square.reshape(-1, 128),
            2.0 * D ** (-0.5),
        )
    )
    out_first, out_second, out_new = adamw(
        w_out, out_grad, out_moment, out_square, 16.0 * (H * HD) ** (-0.5), decay_rate
    )
    gate_up_first, gate_up_second, gate_up_new = adamw(
        w_gate_up,
        gate_up_grad.swapaxes(2, 3),
        gate_up_moment,
        gate_up_square,
        2.0 * D ** (-0.5),
        decay_rate,
    )
    down_first, down_second, down_new = adamw(
        w_down, down_grad, down_moment, down_square, 8.0 * FF ** (-0.5), decay_rate
    )
    return (
        mixed,
        input_grad,
        gain_first,
        gain_second,
        gain_new,
        router_first,
        router_second,
        router_new,
        attention_first,
        attention_second,
        attention_new,
        out_first,
        out_second,
        out_new,
        gate_up_first,
        gate_up_second,
        gate_up_new,
        down_first,
        down_second,
        down_new,
    )


def solution(mesh):
    placed = (
        P(("expert", "tensor"), None),
        P(("expert", "tensor"), None),
        P("expert", None),
        P(("expert", "tensor"), None),
        P(),
        P(),
        P(),
        P(),
        P(),
        P(),
        P(None, "tensor", None),
        P(None, "tensor", None),
        P(None, "tensor", None),
        P("tensor", None, None),
        P("tensor", None, None),
        P("tensor", None, None),
        P("expert", None, None, "tensor"),
        P("expert", None, None, "tensor"),
        P("expert", None, None, "tensor"),
        P("expert", "tensor", None),
        P("expert", "tensor", None),
        P("expert", "tensor", None),
    )
    return jax.shard_map(
        on_device,
        mesh=mesh,
        in_specs=placed,
        out_specs=(
            P(("expert", "tensor"), None),
            P(("expert", "tensor"), None),
            P(),
            P(),
            P(),
            P(),
            P(),
            P(),
            P(None, "tensor", None),
            P(None, "tensor", None),
            P(None, "tensor", None),
            P("tensor", None, None),
            P("tensor", None, None),
            P("tensor", None, None),
            P("expert", None, None, "tensor"),
            P("expert", None, None, "tensor"),
            P("expert", None, None, "tensor"),
            P("expert", "tensor", None),
            P("expert", "tensor", None),
            P("expert", "tensor", None),
        ),
        check_vma=False,
    )
```

```python
from functools import partial

import jax
import jax.numpy as jnp
from jax import lax
from jax.experimental import pallas as pl
from jax.experimental.pallas import tpu as pltpu
from jax.sharding import PartitionSpec as P

D = 1024
H = 16
HD = 64
FF = 512
EXPERTS = 32
TOPK = 8
G = 2
STEP = 10

norm_eps = 1e-06
rope_base = 10000.0
masked_score = -1e30
beta_one = 0.9
beta_two = 0.95
adam_eps = 1e-08
decay_rate = 0.1
highest = lax.Precision.HIGHEST

QT = 256
KT = 256
RT = 256
CT = 512

f32 = jnp.float32
bf16 = jnp.bfloat16

NN = (((1,), (0,)), ((), ()))
NT = (((1,), (1,)), ((), ()))
TN = (((0,), (0,)), ((), ()))


def mm(a, b, dims):
    return lax.dot_general(a, b, dims, preferred_element_type=f32)


def attention_tile(j, i, start, k_ref):
    keys = k_ref[pl.ds(pl.multiple_of(j * KT, KT), KT), :]
    key_id = j * KT + lax.broadcasted_iota(jnp.int32, (KT, QT), 0)
    row_id = i * QT + lax.broadcasted_iota(jnp.int32, (KT, QT), 1)
    return keys, (key_id >= start) & (key_id <= row_id)


def attention_forward_kernel(low_ref, start_ref, q_ref, k_ref, v_ref, o_ref, sum_ref):
    i = pl.program_id(0)
    start = start_ref[...]

    def step(j, carry):
        keys, mask = attention_tile(j, i, start, k_ref)
        values = v_ref[:, pl.ds(pl.multiple_of(j * KT, KT), KT)]
        out = []
        for g in range(G):
            top, total, acc = carry[g]
            scores = mm(keys, q_ref[g * HD : (g + 1) * HD, :], NN)
            scores = jnp.where(mask, scores, masked_score)
            new_top = jnp.maximum(top, jnp.max(scores, axis=0, keepdims=True))
            probs = jnp.exp(scores - new_top)
            shrink = jnp.exp(top - new_top)
            total = total * shrink + jnp.sum(probs, axis=0, keepdims=True)
            acc = acc * shrink + mm(values, probs.astype(bf16), NN)
            out.append((new_top, total, acc))
        return tuple(out)

    zero = (
        jnp.full((1, QT), masked_score, f32),
        jnp.zeros((1, QT), f32),
        jnp.zeros((HD, QT), f32),
    )
    done = lax.fori_loop(low_ref[i], i + 1, step, (zero,) * G)
    for g in range(G):
        top, total, acc = done[g]
        o_ref[g * HD : (g + 1) * HD, :] = (acc / total).astype(bf16)
        sum_ref[g : g + 1, :] = top + jnp.log(total)


def attention_backward_kernel(
    low_ref, start_ref, q_ref, o_ref, d_ref, sum_ref, k_ref, kt_ref, v_ref, dq_ref, dk_ref, dv_ref
):
    i = pl.program_id(0)
    start = start_ref[...]

    @pl.when(i == 0)
    def _():
        dk_ref[...] = jnp.zeros_like(dk_ref)
        dv_ref[...] = jnp.zeros_like(dv_ref)

    grads, inner = [], []
    for g in range(G):
        part = slice(g * HD, (g + 1) * HD)
        grads.append(d_ref[part, :])
        inner.append(
            jnp.sum(d_ref[part, :].astype(f32) * o_ref[part, :].astype(f32), axis=0, keepdims=True)
        )

    def step(j, carry):
        keys, mask = attention_tile(j, i, start, k_ref)
        columns = pl.ds(pl.multiple_of(j * KT, KT), KT)
        values = v_ref[columns, :]
        keys_t = kt_ref[:, columns]
        dk = jnp.zeros((HD, KT), f32)
        dv = jnp.zeros((HD, KT), f32)
        out = []
        for g in range(G):
            query = q_ref[g * HD : (g + 1) * HD, :]
            scores = mm(keys, query, NN)
            probs = jnp.where(mask, jnp.exp(scores - sum_ref[g : g + 1, :]), 0.0)
            probs_grad = mm(values, grads[g], NN)
            score_grad = (probs * (probs_grad - inner[g])).astype(bf16)
            dv += mm(grads[g], probs.astype(bf16), NT)
            dk += mm(query, score_grad, NT)
            out.append(carry[g] + mm(keys_t, score_grad, NN))
        dk_ref[:, columns] += dk
        dv_ref[:, columns] += dv
        return tuple(out)

    done = lax.fori_loop(low_ref[i], i + 1, step, (jnp.zeros((HD, QT), f32),) * G)
    for g in range(G):
        dq_ref[g * HD : (g + 1) * HD, :] = done[g] * HD ** (-0.5)


def attention_forward(low, start, q, k, vt):
    rows = q.shape[1]
    tile = lambda height: pl.BlockSpec((height, QT), lambda i, s: (0, i))
    whole = lambda a: pl.BlockSpec(a.shape, lambda i, s: (0, 0))
    return pl.pallas_call(
        attention_forward_kernel,
        out_shape=(
            jax.ShapeDtypeStruct((G * HD, rows), bf16),
            jax.ShapeDtypeStruct((G, rows), f32),
        ),
        grid_spec=pltpu.PrefetchScalarGridSpec(
            num_scalar_prefetch=1,
            grid=(rows // QT,),
            in_specs=[tile(1), tile(G * HD), whole(k), whole(vt)],
            out_specs=[tile(G * HD), tile(G)],
        ),
        compiler_params=pltpu.CompilerParams(vmem_limit_bytes=24 << 20),
        cost_estimate=pl.CostEstimate(flops=1 << 20, bytes_accessed=1 << 20, transcendentals=0),
        name="attention_forward",
    )(low, start, q, k, vt)


def attention_backward(low, start, q, o, d, sums, k, kt, v):
    rows = q.shape[1]
    tile = lambda height: pl.BlockSpec((height, QT), lambda i, s: (0, i))
    whole = lambda a: pl.BlockSpec(a.shape, lambda i, s: (0, 0))
    return pl.pallas_call(
        attention_backward_kernel,
        out_shape=(
            jax.ShapeDtypeStruct((G * HD, rows), f32),
            jax.ShapeDtypeStruct((HD, rows), f32),
            jax.ShapeDtypeStruct((HD, rows), f32),
        ),
        grid_spec=pltpu.PrefetchScalarGridSpec(
            num_scalar_prefetch=1,
            grid=(rows // QT,),
            in_specs=[tile(1), tile(G * HD), tile(G * HD), tile(G * HD), tile(G)]
            + [whole(k), whole(kt), whole(v)],
            out_specs=[tile(G * HD), whole(kt), whole(kt)],
        ),
        compiler_params=pltpu.CompilerParams(vmem_limit_bytes=24 << 20),
        cost_estimate=pl.CostEstimate(flops=1 << 20, bytes_accessed=1 << 20, transcendentals=0),
        name="attention_backward",
    )(low, start, q, o, d, sums, k, kt, v)


def expert_kernel(blocks, rows, part, parts, offset_ref, count_ref, rank_ref, *refs):
    take = lambda n: (refs[:n], refs[n:])
    x_refs, refs = take(blocks)
    cot_refs, refs = take(blocks)
    mixed_before, refs = take(blocks if part else 0)
    slot_before, refs = take(blocks if part else 0)
    (w_ref,), refs = take(1)
    mixed_refs, refs = take(blocks)
    slot_refs, refs = take(blocks)
    w_grad_ref, mixed_acc, slot_acc, xs, cs, ps, ss, gates, gate_grads, tail = refs[:10]
    w_acc = refs[10] if len(refs) > 10 else None
    high = tail.shape[1]
    seg = rows // 2
    chunk, expert = pl.program_id(0), pl.program_id(1)
    step = chunk * pl.num_programs(1) + expert

    @pl.when(step == 0)
    def _():
        xs[...] = jnp.zeros_like(xs)
        cs[...] = jnp.zeros_like(cs)

    @pl.when(expert == 0)
    def _():
        tail[...] = jnp.zeros_like(tail)
        if part:
            for block in range(blocks):
                place = slice(block * rows, (block + 1) * rows)
                mixed_acc[place, :] = mixed_before[block][...].astype(f32)
                slot_acc[place, :] = slot_before[block][:rows, :].astype(f32)
        else:
            mixed_acc[...] = jnp.zeros_like(mixed_acc)
            slot_acc[...] = jnp.zeros_like(slot_acc)

    if w_acc is not None:

        @pl.when(chunk == 0)
        def _():
            w_acc[...] = jnp.zeros_like(w_acc)

    gates[...] = jnp.zeros_like(gates)
    own = part * pl.num_programs(1) + expert

    def gate_row(block):
        terms = x_refs[block][rows:, :rows].astype(f32)
        terms = terms[:high] + terms[high:]
        here = lax.broadcasted_iota(jnp.int32, (high, rows), 0) == own
        return jnp.sum(jnp.where(here, terms, 0.0), axis=0, keepdims=True)

    def picks(block):
        rank = rank_ref[0, :, block * rows : (block + 1) * rows]
        return lax.broadcasted_iota(jnp.int32, (seg, rows), 0) == rank

    for block in range(blocks):
        first = offset_ref[step * (blocks + 1) + block]
        count = count_ref[step * blocks + block]

        @pl.when(count > 0)
        def _():
            hit = picks(block)
            one = jnp.where(hit, 1.0, 0.0).astype(bf16)
            place = pl.ds(pl.multiple_of(first, 16), seg)
            xs[place, :] = mm(one, x_refs[block][:rows, :], NN).astype(bf16)
            cs[place, :] = mm(one, cot_refs[block][...], NN).astype(bf16)
            gates[place, :] = jnp.sum(jnp.where(hit, gate_row(block), 0.0), axis=1, keepdims=True)

    used = offset_ref[step * (blocks + 1) + blocks]

    def tile(t, carry):
        place = pl.ds(pl.multiple_of(t * RT, RT), RT)
        x, c, gate = xs[place, :], cs[place, :], gates[place, :]
        gate_pre = mm(x, w_ref[0, 0], NT)
        up_pre = mm(x, w_ref[0, 1], NT)
        sigmoid = jax.nn.sigmoid(gate_pre)
        active = gate_pre * sigmoid
        inner = active * up_pre
        plain = mm(c, w_ref[0, 2], NT)
        gate_grads[place, :] = jnp.sum(plain * inner, axis=1, keepdims=True)
        inner_grad = plain * gate
        gate_pre_grad = inner_grad * up_pre * sigmoid * (1.0 + gate_pre * (1.0 - sigmoid))
        ps[0, place, :] = gate_pre_grad.astype(bf16)
        ps[1, place, :] = (inner_grad * active).astype(bf16)
        ss[place, :] = (inner * gate).astype(bf16)
        return carry

    def back(t, carry):
        place = pl.ds(pl.multiple_of(t * RT, RT), RT)
        cs[place, :] = mm(ss[place, :], w_ref[0, 2], NN).astype(bf16)
        xs[place, :] = (
            mm(ps[0, place, :], w_ref[0, 0], NN) + mm(ps[1, place, :], w_ref[0, 1], NN)
        ).astype(bf16)
        return carry

    tiles = jnp.maximum((used + RT - 1) // RT, 1)
    lax.fori_loop(0, tiles, tile, 0)
    for n in range(1, xs.shape[0] // RT + 1):

        @pl.when(tiles == n)
        def _():
            place = slice(0, n * RT)
            for k, (left, right) in enumerate(((ps.at[0], xs), (ps.at[1], xs), (ss, cs))):
                for column in range(0, D, CT):
                    part_of = slice(column, column + CT)
                    grad = mm(left[place, :], right[place, part_of], TN)
                    if w_acc is None:
                        w_grad_ref[0, k, :, part_of] = grad.astype(bf16)
                    else:
                        w_acc[k, :, part_of] += grad

    if w_acc is not None:
        w_grad_ref[0] = w_acc[...].astype(bf16)
    lax.fori_loop(0, tiles, back, 0)

    for block in range(blocks):
        first = offset_ref[step * (blocks + 1) + block]
        count = count_ref[step * blocks + block]
        whole = slice(block * rows, (block + 1) * rows)

        @pl.when(count > 0)
        def _():
            hit = picks(block)
            one = jnp.where(hit, 1.0, 0.0).astype(bf16)
            place = pl.ds(pl.multiple_of(first, 16), seg)
            mixed_acc[whole, :] += mm(one, cs[place, :], TN)
            slot_acc[whole, :] += mm(one, xs[place, :], TN)
            tail[block, pl.ds(own, 1), :] = jnp.sum(
                jnp.where(hit, gate_grads[place, :], 0.0), axis=0, keepdims=True
            )

    @pl.when(expert == pl.num_programs(1) - 1)
    def _():
        for block in range(blocks):
            place = slice(block * rows, (block + 1) * rows)
            mixed_refs[block][...] = mixed_acc[place, :].astype(bf16)
            slot_refs[block][:rows, :] = slot_acc[place, :].astype(bf16)
            upper = tail[block].astype(bf16)
            lower = (tail[block] - upper.astype(f32)).astype(bf16)
            terms = jnp.concatenate([upper, lower], axis=0)
            if part:
                terms = terms + slot_before[block][rows:, :rows]
            slot_refs[block][rows:, :] = jnp.concatenate(
                [terms, jnp.zeros((2 * high, D - rows), bf16)], axis=1
            )


def expert_layer(part, parts, rank, counts, x, cot, before, weights, rows, high):
    experts, blocks = weights.shape[0], len(x)
    height = blocks * rows
    chunks = rank.shape[0] // experts
    padded = -(-counts // 16) * 16
    offsets = jnp.concatenate(
        [jnp.zeros((chunks * experts, 1), jnp.int32), jnp.cumsum(padded, axis=1)], axis=1
    )
    room = -(-blocks * (rows // 2) // RT) * RT
    tall = rows + 2 * high

    def tokens(h, **mode):
        return [pl.BlockSpec((h, D), lambda c, e, a, b: (c, 0), **mode) for _ in range(blocks)]

    held = dict(pipeline_mode=pl.Buffered(1))
    line = pl.BlockSpec((1, 1, height), lambda c, e, a, b: (c * experts + e, 0, 0))
    weight = lambda: pl.BlockSpec((1, 3, FF, D), lambda c, e, a, b: (e, 0, 0, 0))
    out = pl.pallas_call(
        partial(expert_kernel, blocks, rows, part, parts),
        out_shape=[jax.ShapeDtypeStruct((chunks * rows, D), bf16)] * blocks
        + [jax.ShapeDtypeStruct((chunks * tall, D), bf16)] * blocks
        + [jax.ShapeDtypeStruct(weights.shape, bf16)],
        grid_spec=pltpu.PrefetchScalarGridSpec(
            num_scalar_prefetch=2,
            grid=(chunks, experts),
            in_specs=[line]
            + tokens(tall, **held)
            + tokens(rows, **held)
            + (tokens(rows, **held) + tokens(tall, **held) if part else [])
            + [weight()],
            out_specs=tokens(rows) + tokens(tall) + [weight()],
            scratch_shapes=[
                pltpu.VMEM((height, D), f32),
                pltpu.VMEM((height, D), f32),
                pltpu.VMEM((room, D), bf16),
                pltpu.VMEM((room, D), bf16),
                pltpu.VMEM((2, room, FF), bf16),
                pltpu.VMEM((room, FF), bf16),
                pltpu.VMEM((room, 1), f32),
                pltpu.VMEM((room, 1), f32),
                pltpu.VMEM((blocks, high, rows), f32),
            ]
            + ([pltpu.VMEM((3, FF, D), f32)] if chunks > 1 else []),
        ),
        compiler_params=pltpu.CompilerParams(vmem_limit_bytes=58 << 20),
        cost_estimate=pl.CostEstimate(flops=1 << 20, bytes_accessed=1 << 20, transcendentals=0),
        name="experts",
    )(offsets.reshape(-1), counts.reshape(-1), rank, *x, *cot, *before, weights)
    return list(out[: 2 * blocks]), out[-1]


def angles(position):
    half = HD // 2
    frequency = rope_base ** (-jnp.arange(half, dtype=f32) * 2.0 / HD)
    angle = frequency[:, None] * position.astype(f32)[None, :]
    return jnp.cos(angle), jnp.sin(angle)


def rotate(values, cosine, sine):
    half = HD // 2
    parts = values.reshape(-1, HD, values.shape[1])
    first, second = parts[:, :half], parts[:, half:]
    return jnp.concatenate(
        [first * cosine - second * sine, second * cosine + first * sine], axis=1
    ).reshape(values.shape)


def doc_table(lengths, count):
    ends = jnp.cumsum(lengths)
    places = jnp.arange(count, dtype=jnp.int32)
    after = (places[None, :] >= ends[:, None]).astype(jnp.int32)
    starts = jnp.sum(after * lengths[:, None], axis=0)
    return (starts, places - starts)


def rank_table(choices, first, experts):
    named = (first + jnp.arange(experts, dtype=jnp.int32))[None, :, None, None]
    hits = jnp.any(choices[:, None, :, :] == named, axis=2)
    order = jnp.arange(choices.shape[2])
    before = (order[:, None] < order[None, :]).astype(bf16)
    rank = jnp.einsum("ber,rs->bes", hits.astype(bf16), before, preferred_element_type=f32)
    rank = jnp.where(hits, rank.astype(jnp.int32), -1)
    return rank, jnp.sum(hits.astype(jnp.int32), axis=2)


def shift(value, axis, step):
    size = lax.axis_size(axis)
    return lax.ppermute(value, axis, [(i, (i + step) % size) for i in range(size)])


def below(rows, values, parts):
    terms, rest = [], values.astype(f32)
    high = -(-values.shape[0] // 8) * 8
    rest = jnp.pad(rest, ((0, high - values.shape[0]), (0, D - values.shape[1])))
    for _ in range(parts):
        term = rest.astype(bf16)
        terms.append(term)
        rest = rest - term.astype(f32)
    if parts * high % 16:
        terms.append(jnp.zeros_like(term))
    return jnp.concatenate([rows] + terms, axis=0)


def total(values, axis):
    size = lax.axis_size(axis)
    distance = 1
    while distance < size:
        pairs = [(i, i ^ distance) for i in range(size)]
        other = [lax.ppermute(v, axis, pairs) for v in values]
        values = [(v.astype(f32) + o.astype(f32)).astype(v.dtype) for v, o in zip(values, other)]
        distance *= 2
    return values


def spread(values, axis):
    return lax.all_to_all(values, axis, split_axis=0, concat_axis=0, tiled=True)


def to_rows(values, ranks):
    width = values.shape[0]
    parts = values.reshape(width, ranks, -1).swapaxes(0, 1)
    return spread(parts, "tensor").reshape(ranks * width, -1)


def to_heads(values, ranks):
    parts = spread(values.reshape(ranks, -1, values.shape[1]), "tensor")
    return parts.swapaxes(0, 1).reshape(parts.shape[1], -1)


def adamw(weight, grad, first, second, rate, decay):
    first = beta_one * first + (1.0 - beta_one) * grad
    second = beta_two * second + (1.0 - beta_two) * grad * grad
    step = first / (1.0 - beta_one**STEP) / (jnp.sqrt(second / (1.0 - beta_two**STEP)) + adam_eps)
    return (first, second, weight - rate * (step + decay * weight))


def adamw_kernel(rate, weight_ref, grad_ref, first_ref, second_ref, *out_refs):
    out = adamw(
        weight_ref[...], grad_ref[...].astype(f32), first_ref[...], second_ref[...], rate, decay_rate
    )
    for ref, value in zip(out_refs, out):
        ref[...] = value


def adamw_rows(weight, grad, first, second, rate):
    block = pl.BlockSpec((weight.shape[0] // 4, weight.shape[1]), lambda i: (i, 0))
    return pl.pallas_call(
        partial(adamw_kernel, rate),
        out_shape=[jax.ShapeDtypeStruct(weight.shape, f32)] * 3,
        grid=(4,),
        in_specs=[block] * 4,
        out_specs=[block] * 3,
        compiler_params=pltpu.CompilerParams(vmem_limit_bytes=16 << 20),
        cost_estimate=pl.CostEstimate(flops=1 << 20, bytes_accessed=1 << 20, transcendentals=0),
        name="adamw",
    )(weight, grad, first, second)


def on_device(
    tokens,
    cotangent,
    doc_lengths,
    expert_choices,
    gains,
    gain_moment,
    gain_square,
    router,
    router_moment,
    router_square,
    w_attention,
    attention_moment,
    attention_square,
    w_out,
    out_moment,
    out_square,
    w_gate_up,
    gate_up_moment,
    gate_up_square,
    w_down,
    down_moment,
    down_square,
):
    ranks = lax.axis_size("tensor")
    peers = lax.axis_size("expert")
    rows = tokens.shape[0]
    group_rows = rows * ranks
    experts = w_gate_up.shape[0]
    blocks = min(peers, 4)
    halves = 2 if experts % 2 == 0 else 1
    half = experts // halves
    hidden = w_down.shape[1]

    inputs = tokens.astype(f32)
    scale_one = lax.rsqrt(jnp.mean(inputs * inputs, axis=-1, keepdims=True) + norm_eps)
    normed = (inputs * scale_one * gains[0]).astype(bf16)
    gathered = lax.all_gather(normed, "tensor", axis=0, tiled=True)

    attention_low = w_attention.reshape(D, -1).astype(bf16)
    out_low = w_out.reshape(-1, D).astype(bf16)
    expert_low = jnp.concatenate(
        [w_gate_up.swapaxes(2, 3).astype(bf16), w_down.astype(bf16)[:, None]], axis=1
    )
    out_all = lax.all_gather(out_low, "tensor", axis=0, tiled=True)
    expert_all = [
        lax.all_gather(expert_low[part * half : (part + 1) * half], "tensor", axis=2, tiled=True)
        for part in range(halves)
    ]

    attention_all = lax.all_gather(attention_low.T, "tensor", axis=0, tiled=True)

    message = below(cotangent, expert_choices.T, 1)
    messages = [shift(message, "expert", d) for d in range(1, peers)]
    cot_in = [cotangent] + messages
    choices_in = [expert_choices.T] + [
        m[rows : rows + TOPK, :rows].astype(jnp.int32) for m in messages
    ]

    start, position = doc_table(doc_lengths[0], group_rows)
    cosine, sine = angles(position)
    lowest = start[::QT] // KT
    start = start[None, :]
    projected = jnp.einsum("dc,td->ct", attention_low, gathered, preferred_element_type=f32)
    turned = rotate(projected[: (G + 1) * HD], cosine, sine).astype(bf16)
    queries = turned[: G * HD] * bf16(HD ** (-0.5))
    keys_t = turned[G * HD :]
    values_t = projected[(G + 1) * HD :].astype(bf16)
    keys, values = keys_t.T, values_t.T
    heads, log_sums = attention_forward(lowest, start, queries, keys, values_t)

    heads_rows, values = lax.optimization_barrier((to_rows(heads, ranks), values))
    attended = jnp.einsum("ct,cd->td", heads_rows, out_all, preferred_element_type=f32)
    state = inputs + attended
    scale_two = lax.rsqrt(jnp.mean(state * state, axis=-1, keepdims=True) + norm_eps)
    unit = state * scale_two
    normed_two = unit * gains[1]

    logits = lax.dot_general(router, normed_two, (((0,), (1,)), ((), ())), precision=highest)
    named = jnp.arange(EXPERTS, dtype=jnp.int32)[:, None, None]
    chosen = jnp.any(expert_choices.T[None, :, :] == named, axis=1)
    top = jnp.max(jnp.where(chosen, logits, -jnp.inf), axis=0, keepdims=True)
    weight = jnp.where(chosen, jnp.exp(jnp.where(chosen, logits - top, 0.0)), 0.0)
    gates = weight / jnp.sum(weight, axis=0, keepdims=True)

    me = lax.axis_index("expert")
    moved = normed_two.astype(bf16)
    by_peer = gates.reshape(peers, experts, rows)
    gates_to = [
        lax.dynamic_index_in_dim(by_peer, (me + d) % peers, 0, keepdims=False) for d in range(peers)
    ]
    high = -(-experts // 8) * 8
    x_in = [below(moved, gates_to[0], 2)]
    for d in range(1, peers):
        x_in.append(shift(below(moved, gates_to[d], 2), "expert", d))
    rank, counts = rank_table(jnp.stack(choices_in), me * experts, experts)

    def by_step(values):
        return values.reshape((-1, blocks) + values.shape[1:]).swapaxes(1, 2)

    def lay(values, height):
        if len(values) == blocks:
            return values
        return [jnp.concatenate([v[:height] for v in values[b::blocks]]) for b in range(blocks)]

    def unlay(values):
        if len(values) == peers:
            return values
        height = values[0].shape[0] * blocks // peers
        return [values[d % blocks][d // blocks * height :][:height] for d in range(peers)]

    rank_steps, count_steps = by_step(rank), by_step(counts)
    x_laid, cot_laid = lay(x_in, rows + 2 * high), lay(cot_in, rows)
    before, expert_grad = [], []
    for part in range(halves):
        own = slice(part * half, (part + 1) * half)
        before, grad_out = expert_layer(
            part,
            halves,
            rank_steps[:, own].reshape(-1, 1, blocks * rows),
            count_steps[:, own].reshape(-1, blocks),
            x_laid,
            cot_laid,
            before,
            expert_all[part],
            rows,
            high,
        )
        expert_grad.append(lax.psum_scatter(grad_out, "tensor", scatter_dimension=2, tiled=True))
    mixed_out, slot_out = unlay(before[:blocks]), unlay(before[blocks:])
    slot_out, attention_all = lax.optimization_barrier((slot_out, attention_all))
    slot_back = [slot_out[0]] + [shift(slot_out[d], "expert", -d) for d in range(1, peers)]
    slot_back, mixed_out = lax.optimization_barrier((slot_back, mixed_out))
    mixed_back = [mixed_out[0]] + [shift(mixed_out[d], "expert", -d) for d in range(1, peers)]

    gate_grads = jnp.concatenate(
        [
            v[rows : rows + experts, :rows].astype(f32)
            + v[rows + high : rows + high + experts, :rows].astype(f32)
            for v in slot_back
        ]
    )
    near_gates = jnp.concatenate(gates_to)
    near_router = jnp.roll(router.T.reshape(peers, experts, D), -me, axis=0).reshape(EXPERTS, D)
    logit_grads = near_gates * (
        gate_grads - jnp.sum(near_gates * gate_grads, axis=0, keepdims=True)
    )
    normed_two_grad = sum(v[:rows].astype(f32) for v in slot_back) + lax.dot_general(
        logit_grads, near_router, (((0,), (0,)), ((), ())), precision=highest
    )
    gain_two_grad = jnp.sum(normed_two_grad * unit, axis=0)
    unit_grad = normed_two_grad * gains[1]
    state_grad = cotangent.astype(f32) + scale_two * (
        unit_grad - unit * jnp.mean(unit_grad * unit, axis=-1, keepdims=True)
    )

    branch = state_grad.astype(bf16)
    head_grads_rows = jnp.einsum(
        "cd,td->ct", out_all, branch, preferred_element_type=f32
    ).astype(bf16)
    head_grads, expert_grad[0] = lax.optimization_barrier(
        (to_heads(head_grads_rows, ranks), expert_grad[0])
    )
    out_grad = jnp.einsum("ct,td->cd", heads_rows, branch, preferred_element_type=f32)
    out_grad = spread(out_grad.astype(bf16).reshape(ranks, -1, D), "tensor")
    query_grad, key_grad, value_grad = attention_backward(
        lowest, start, queries, heads, head_grads, log_sums, keys, keys_t, values
    )
    value_grad, out_grad, logit_grads = lax.optimization_barrier(
        (value_grad, out_grad, logit_grads)
    )
    out_grad = jnp.sum(out_grad.astype(f32), axis=0)
    router_grad = lax.dot_general(
        logit_grads, normed_two, (((1,), (0,)), ((), ())), precision=highest
    )
    router_grad = jnp.roll(router_grad.reshape(peers, experts, D), me, axis=0).reshape(EXPERTS, D)
    early = jnp.concatenate([router_grad, gain_two_grad[None]], axis=0)
    early = jnp.pad(early, ((0, -early.shape[0] % ranks), (0, 0))).reshape(ranks, -1, D)
    turned_grad = rotate(jnp.concatenate([query_grad, key_grad], axis=0), cosine, -sine)
    projected_grad = jnp.concatenate([turned_grad, value_grad], axis=0).astype(bf16)
    attention_grad = jnp.einsum(
        "td,ct->dc", gathered, projected_grad, preferred_element_type=f32
    )
    gain_one_grad = (
        jnp.sum(attention_grad * attention_low.astype(f32), axis=1) / gains[0]
    )
    projected_late, expert_grad[-1] = lax.optimization_barrier(
        (projected_grad, expert_grad[-1])
    )
    projected_rows = to_rows(projected_late, ranks)
    projected_rows, early, gain_one_grad, mixed_back = lax.optimization_barrier(
        (projected_rows, early, gain_one_grad, mixed_back)
    )
    mixed = state + sum(v.astype(f32) for v in mixed_back)
    normed_grad = jnp.einsum(
        "ct,cd->td", projected_rows, attention_all, preferred_element_type=f32
    )
    attention_grad, out_grad = lax.psum(
        (attention_grad.astype(bf16), out_grad.astype(bf16)), "expert"
    )
    unit_one = inputs * scale_one
    unit_one_grad = normed_grad * gains[0]
    input_grad = state_grad + scale_one * (
        unit_one_grad - unit_one * jnp.mean(unit_one_grad * unit_one, axis=-1, keepdims=True)
    )

    early = jnp.sum(spread(early, "tensor"), axis=0)
    early = total([early], "expert")[0]
    early, attention_grad, out_grad = lax.optimization_barrier((early, attention_grad, out_grad))
    early = spread(jnp.broadcast_to(early[None], (ranks,) + early.shape), "tensor").reshape(-1, D)
    router_grad, gain_two_grad = early[:EXPERTS].T, early[EXPERTS]
    out_grad = out_grad.astype(f32).reshape(w_out.shape)
    gain_one_grad = total(total([gain_one_grad[None]], "expert"), "tensor")[0][0]
    gain_grad = jnp.stack([gain_one_grad, gain_two_grad])
    expert_grad = jnp.concatenate(expert_grad, axis=0).astype(f32)
    gate_up_grad, down_grad = expert_grad[:, :2], expert_grad[:, 2]
    gain_first, gain_second, gain_new = adamw(gains, gain_grad, gain_moment, gain_square, 1.0, 0.0)
    router_first, router_second, router_new = adamw(
        router, router_grad, router_moment, router_square, D ** (-0.5), decay_rate
    )
    attention_first, attention_second, attention_new = (
        v.reshape(w_attention.shape)
        for v in adamw_rows(
            w_attention.reshape(-1, 128),
            attention_grad.reshape(-1, 128),
            attention_moment.reshape(-1, 128),
            attention_square.reshape(-1, 128),
            2.0 * D ** (-0.5),
        )
    )
    out_first, out_second, out_new = adamw(
        w_out, out_grad, out_moment, out_square, 16.0 * (H * HD) ** (-0.5), decay_rate
    )
    gate_up_first, gate_up_second, gate_up_new = adamw(
        w_gate_up,
        gate_up_grad.swapaxes(2, 3),
        gate_up_moment,
        gate_up_square,
        2.0 * D ** (-0.5),
        decay_rate,
    )
    down_first, down_second, down_new = adamw(
        w_down, down_grad, down_moment, down_square, 8.0 * FF ** (-0.5), decay_rate
    )
    return (
        mixed,
        input_grad,
        gain_first,
        gain_second,
        gain_new,
        router_first,
        router_second,
        router_new,
        attention_first,
        attention_second,
        attention_new,
        out_first,
        out_second,
        out_new,
        gate_up_first,
        gate_up_second,
        gate_up_new,
        down_first,
        down_second,
        down_new,
    )


def solution(mesh):
    placed = (
        P(("expert", "tensor"), None),
        P(("expert", "tensor"), None),
        P("expert", None),
        P(("expert", "tensor"), None),
        P(),
        P(),
        P(),
        P(),
        P(),
        P(),
        P(None, "tensor", None),
        P(None, "tensor", None),
        P(None, "tensor", None),
        P("tensor", None, None),
        P("tensor", None, None),
        P("tensor", None, None),
        P("expert", None, None, "tensor"),
        P("expert", None, None, "tensor"),
        P("expert", None, None, "tensor"),
        P("expert", "tensor", None),
        P("expert", "tensor", None),
        P("expert", "tensor", None),
    )
    return jax.shard_map(
        on_device,
        mesh=mesh,
        in_specs=placed,
        out_specs=(
            P(("expert", "tensor"), None),
            P(("expert", "tensor"), None),
            P(),
            P(),
            P(),
            P(),
            P(),
            P(),
            P(None, "tensor", None),
            P(None, "tensor", None),
            P(None, "tensor", None),
            P("tensor", None, None),
            P("tensor", None, None),
            P("tensor", None, None),
            P("expert", None, None, "tensor"),
            P("expert", None, None, "tensor"),
            P("expert", None, None, "tensor"),
            P("expert", "tensor", None),
            P("expert", "tensor", None),
            P("expert", "tensor", None),
        ),
        check_vma=False,
    )
```

```python
from functools import partial

import jax
import jax.numpy as jnp
from jax import lax
from jax.experimental import pallas as pl
from jax.experimental.pallas import tpu as pltpu
from jax.sharding import PartitionSpec as P

D = 1024
H = 16
HD = 64
FF = 512
EXPERTS = 32
TOPK = 8
G = 2
STEP = 10

norm_eps = 1e-06
rope_base = 10000.0
masked_score = -1e30
beta_one = 0.9
beta_two = 0.95
adam_eps = 1e-08
decay_rate = 0.1
highest = lax.Precision.HIGHEST

QT = 256
KT = 256
RT = 256
CT = 512

f32 = jnp.float32
bf16 = jnp.bfloat16

NN = (((1,), (0,)), ((), ()))
NT = (((1,), (1,)), ((), ()))
TN = (((0,), (0,)), ((), ()))


def mm(a, b, dims):
    return lax.dot_general(a, b, dims, preferred_element_type=f32)


def attention_tile(j, i, start, k_ref):
    keys = k_ref[pl.ds(pl.multiple_of(j * KT, KT), KT), :]
    key_id = j * KT + lax.broadcasted_iota(jnp.int32, (KT, QT), 0)
    row_id = i * QT + lax.broadcasted_iota(jnp.int32, (KT, QT), 1)
    return keys, (key_id >= start) & (key_id <= row_id)


def attention_forward_kernel(low_ref, start_ref, q_ref, k_ref, v_ref, o_ref, sum_ref):
    i = pl.program_id(0)
    start = start_ref[...]

    def step(j, carry):
        keys, mask = attention_tile(j, i, start, k_ref)
        values = v_ref[:, pl.ds(pl.multiple_of(j * KT, KT), KT)]
        out = []
        for g in range(G):
            top, total, acc = carry[g]
            scores = mm(keys, q_ref[g * HD : (g + 1) * HD, :], NN)
            scores = jnp.where(mask, scores, masked_score)
            new_top = jnp.maximum(top, jnp.max(scores, axis=0, keepdims=True))
            probs = jnp.exp(scores - new_top)
            shrink = jnp.exp(top - new_top)
            total = total * shrink + jnp.sum(probs, axis=0, keepdims=True)
            acc = acc * shrink + mm(values, probs.astype(bf16), NN)
            out.append((new_top, total, acc))
        return tuple(out)

    zero = (
        jnp.full((1, QT), masked_score, f32),
        jnp.zeros((1, QT), f32),
        jnp.zeros((HD, QT), f32),
    )
    done = lax.fori_loop(low_ref[i], i + 1, step, (zero,) * G)
    for g in range(G):
        top, total, acc = done[g]
        o_ref[g * HD : (g + 1) * HD, :] = (acc / total).astype(bf16)
        sum_ref[g : g + 1, :] = top + jnp.log(total)


def attention_backward_kernel(
    low_ref, start_ref, q_ref, o_ref, d_ref, sum_ref, k_ref, kt_ref, v_ref, dq_ref, dk_ref, dv_ref
):
    i = pl.program_id(0)
    start = start_ref[...]

    @pl.when(i == 0)
    def _():
        dk_ref[...] = jnp.zeros_like(dk_ref)
        dv_ref[...] = jnp.zeros_like(dv_ref)

    grads, inner = [], []
    for g in range(G):
        part = slice(g * HD, (g + 1) * HD)
        grads.append(d_ref[part, :])
        inner.append(
            jnp.sum(d_ref[part, :].astype(f32) * o_ref[part, :].astype(f32), axis=0, keepdims=True)
        )

    def step(j, carry):
        keys, mask = attention_tile(j, i, start, k_ref)
        columns = pl.ds(pl.multiple_of(j * KT, KT), KT)
        values = v_ref[columns, :]
        keys_t = kt_ref[:, columns]
        dk = jnp.zeros((HD, KT), f32)
        dv = jnp.zeros((HD, KT), f32)
        out = []
        for g in range(G):
            query = q_ref[g * HD : (g + 1) * HD, :]
            scores = mm(keys, query, NN)
            probs = jnp.where(mask, jnp.exp(scores - sum_ref[g : g + 1, :]), 0.0)
            probs_grad = mm(values, grads[g], NN)
            score_grad = (probs * (probs_grad - inner[g])).astype(bf16)
            dv += mm(grads[g], probs.astype(bf16), NT)
            dk += mm(query, score_grad, NT)
            out.append(carry[g] + mm(keys_t, score_grad, NN))
        dk_ref[:, columns] += dk
        dv_ref[:, columns] += dv
        return tuple(out)

    done = lax.fori_loop(low_ref[i], i + 1, step, (jnp.zeros((HD, QT), f32),) * G)
    for g in range(G):
        dq_ref[g * HD : (g + 1) * HD, :] = done[g] * HD ** (-0.5)


def attention_forward(low, start, q, k, vt):
    rows = q.shape[1]
    tile = lambda height: pl.BlockSpec((height, QT), lambda i, s: (0, i))
    whole = lambda a: pl.BlockSpec(a.shape, lambda i, s: (0, 0))
    return pl.pallas_call(
        attention_forward_kernel,
        out_shape=(
            jax.ShapeDtypeStruct((G * HD, rows), bf16),
            jax.ShapeDtypeStruct((G, rows), f32),
        ),
        grid_spec=pltpu.PrefetchScalarGridSpec(
            num_scalar_prefetch=1,
            grid=(rows // QT,),
            in_specs=[tile(1), tile(G * HD), whole(k), whole(vt)],
            out_specs=[tile(G * HD), tile(G)],
        ),
        compiler_params=pltpu.CompilerParams(vmem_limit_bytes=24 << 20),
        cost_estimate=pl.CostEstimate(flops=1 << 20, bytes_accessed=1 << 20, transcendentals=0),
        name="attention_forward",
    )(low, start, q, k, vt)


def attention_backward(low, start, q, o, d, sums, k, kt, v):
    rows = q.shape[1]
    tile = lambda height: pl.BlockSpec((height, QT), lambda i, s: (0, i))
    whole = lambda a: pl.BlockSpec(a.shape, lambda i, s: (0, 0))
    return pl.pallas_call(
        attention_backward_kernel,
        out_shape=(
            jax.ShapeDtypeStruct((G * HD, rows), f32),
            jax.ShapeDtypeStruct((HD, rows), f32),
            jax.ShapeDtypeStruct((HD, rows), f32),
        ),
        grid_spec=pltpu.PrefetchScalarGridSpec(
            num_scalar_prefetch=1,
            grid=(rows // QT,),
            in_specs=[tile(1), tile(G * HD), tile(G * HD), tile(G * HD), tile(G)]
            + [whole(k), whole(kt), whole(v)],
            out_specs=[tile(G * HD), whole(kt), whole(kt)],
        ),
        compiler_params=pltpu.CompilerParams(vmem_limit_bytes=24 << 20),
        cost_estimate=pl.CostEstimate(flops=1 << 20, bytes_accessed=1 << 20, transcendentals=0),
        name="attention_backward",
    )(low, start, q, o, d, sums, k, kt, v)


def expert_kernel(blocks, rows, part, parts, offset_ref, count_ref, rank_ref, *refs):
    take = lambda n: (refs[:n], refs[n:])
    x_refs, refs = take(blocks)
    cot_refs, refs = take(blocks)
    mixed_before, refs = take(blocks if part else 0)
    slot_before, refs = take(blocks if part else 0)
    (w_ref,), refs = take(1)
    mixed_refs, refs = take(blocks)
    slot_refs, refs = take(blocks)
    w_grad_ref, mixed_acc, slot_acc, xs, cs, ps, ss, gates, gate_grads, tail = refs[:10]
    w_acc = refs[10] if len(refs) > 10 else None
    high = tail.shape[1]
    seg = rows // 2
    chunk, expert = pl.program_id(0), pl.program_id(1)
    step = chunk * pl.num_programs(1) + expert

    @pl.when(step == 0)
    def _():
        xs[...] = jnp.zeros_like(xs)
        cs[...] = jnp.zeros_like(cs)

    @pl.when(expert == 0)
    def _():
        tail[...] = jnp.zeros_like(tail)
        if part:
            for block in range(blocks):
                place = slice(block * rows, (block + 1) * rows)
                mixed_acc[place, :] = mixed_before[block][...].astype(f32)
                slot_acc[place, :] = slot_before[block][:rows, :].astype(f32)
        else:
            mixed_acc[...] = jnp.zeros_like(mixed_acc)
            slot_acc[...] = jnp.zeros_like(slot_acc)

    if w_acc is not None:

        @pl.when(chunk == 0)
        def _():
            w_acc[...] = jnp.zeros_like(w_acc)

    gates[...] = jnp.zeros_like(gates)
    own = part * pl.num_programs(1) + expert

    def gate_row(block):
        terms = x_refs[block][rows:, :rows].astype(f32)
        terms = terms[:high] + terms[high:]
        here = lax.broadcasted_iota(jnp.int32, (high, rows), 0) == own
        return jnp.sum(jnp.where(here, terms, 0.0), axis=0, keepdims=True)

    def picks(block):
        rank = rank_ref[0, :, block * rows : (block + 1) * rows]
        return lax.broadcasted_iota(jnp.int32, (seg, rows), 0) == rank

    for block in range(blocks):
        first = offset_ref[step * (blocks + 1) + block]
        count = count_ref[step * blocks + block]

        @pl.when(count > 0)
        def _():
            hit = picks(block)
            one = jnp.where(hit, 1.0, 0.0).astype(bf16)
            place = pl.ds(pl.multiple_of(first, 16), seg)
            xs[place, :] = mm(one, x_refs[block][:rows, :], NN).astype(bf16)
            cs[place, :] = mm(one, cot_refs[block][...], NN).astype(bf16)
            gates[place, :] = jnp.sum(jnp.where(hit, gate_row(block), 0.0), axis=1, keepdims=True)

    used = offset_ref[step * (blocks + 1) + blocks]

    def tile(t, carry):
        place = pl.ds(pl.multiple_of(t * RT, RT), RT)
        x, c, gate = xs[place, :], cs[place, :], gates[place, :]
        gate_pre = mm(x, w_ref[0, 0], NT)
        up_pre = mm(x, w_ref[0, 1], NT)
        sigmoid = jax.nn.sigmoid(gate_pre)
        active = gate_pre * sigmoid
        inner = active * up_pre
        plain = mm(c, w_ref[0, 2], NT)
        gate_grads[place, :] = jnp.sum(plain * inner, axis=1, keepdims=True)
        inner_grad = plain * gate
        gate_pre_grad = inner_grad * up_pre * sigmoid * (1.0 + gate_pre * (1.0 - sigmoid))
        ps[0, place, :] = gate_pre_grad.astype(bf16)
        ps[1, place, :] = (inner_grad * active).astype(bf16)
        ss[place, :] = (inner * gate).astype(bf16)
        return carry

    def back(t, carry):
        place = pl.ds(pl.multiple_of(t * RT, RT), RT)
        cs[place, :] = mm(ss[place, :], w_ref[0, 2], NN).astype(bf16)
        xs[place, :] = (
            mm(ps[0, place, :], w_ref[0, 0], NN) + mm(ps[1, place, :], w_ref[0, 1], NN)
        ).astype(bf16)
        return carry

    tiles = jnp.maximum((used + RT - 1) // RT, 1)
    lax.fori_loop(0, tiles, tile, 0)
    for n in range(1, xs.shape[0] // RT + 1):

        @pl.when(tiles == n)
        def _():
            place = slice(0, n * RT)
            for k, (left, right) in enumerate(((ps.at[0], xs), (ps.at[1], xs), (ss, cs))):
                for column in range(0, D, CT):
                    part_of = slice(column, column + CT)
                    grad = mm(left[place, :], right[place, part_of], TN)
                    if w_acc is None:
                        w_grad_ref[0, k, :, part_of] = grad.astype(bf16)
                    else:
                        w_acc[k, :, part_of] += grad

    if w_acc is not None:
        w_grad_ref[0] = w_acc[...].astype(bf16)
    lax.fori_loop(0, tiles, back, 0)

    for block in range(blocks):
        first = offset_ref[step * (blocks + 1) + block]
        count = count_ref[step * blocks + block]
        whole = slice(block * rows, (block + 1) * rows)

        @pl.when(count > 0)
        def _():
            hit = picks(block)
            one = jnp.where(hit, 1.0, 0.0).astype(bf16)
            place = pl.ds(pl.multiple_of(first, 16), seg)
            mixed_acc[whole, :] += mm(one, cs[place, :], TN)
            slot_acc[whole, :] += mm(one, xs[place, :], TN)
            tail[block, pl.ds(own, 1), :] = jnp.sum(
                jnp.where(hit, gate_grads[place, :], 0.0), axis=0, keepdims=True
            )

    @pl.when(expert == pl.num_programs(1) - 1)
    def _():
        for block in range(blocks):
            place = slice(block * rows, (block + 1) * rows)
            mixed_refs[block][...] = mixed_acc[place, :].astype(bf16)
            slot_refs[block][:rows, :] = slot_acc[place, :].astype(bf16)
            upper = tail[block].astype(bf16)
            lower = (tail[block] - upper.astype(f32)).astype(bf16)
            terms = jnp.concatenate([upper, lower], axis=0)
            if part:
                terms = terms + slot_before[block][rows:, :rows]
            slot_refs[block][rows:, :] = jnp.concatenate(
                [terms, jnp.zeros((2 * high, D - rows), bf16)], axis=1
            )


def expert_layer(part, parts, rank, counts, x, cot, before, weights, rows, high):
    experts, blocks = weights.shape[0], len(x)
    height = blocks * rows
    chunks = rank.shape[0] // experts
    padded = -(-counts // 16) * 16
    offsets = jnp.concatenate(
        [jnp.zeros((chunks * experts, 1), jnp.int32), jnp.cumsum(padded, axis=1)], axis=1
    )
    room = -(-blocks * (rows // 2) // RT) * RT
    tall = rows + 2 * high

    def tokens(h, **mode):
        return [pl.BlockSpec((h, D), lambda c, e, a, b: (c, 0), **mode) for _ in range(blocks)]

    held = dict(pipeline_mode=pl.Buffered(1))
    line = pl.BlockSpec((1, 1, height), lambda c, e, a, b: (c * experts + e, 0, 0))
    weight = lambda: pl.BlockSpec((1, 3, FF, D), lambda c, e, a, b: (e, 0, 0, 0))
    out = pl.pallas_call(
        partial(expert_kernel, blocks, rows, part, parts),
        out_shape=[jax.ShapeDtypeStruct((chunks * rows, D), bf16)] * blocks
        + [jax.ShapeDtypeStruct((chunks * tall, D), bf16)] * blocks
        + [jax.ShapeDtypeStruct(weights.shape, bf16)],
        grid_spec=pltpu.PrefetchScalarGridSpec(
            num_scalar_prefetch=2,
            grid=(chunks, experts),
            in_specs=[line]
            + tokens(tall, **held)
            + tokens(rows, **held)
            + (tokens(rows, **held) + tokens(tall, **held) if part else [])
            + [weight()],
            out_specs=tokens(rows) + tokens(tall) + [weight()],
            scratch_shapes=[
                pltpu.VMEM((height, D), f32),
                pltpu.VMEM((height, D), f32),
                pltpu.VMEM((room, D), bf16),
                pltpu.VMEM((room, D), bf16),
                pltpu.VMEM((2, room, FF), bf16),
                pltpu.VMEM((room, FF), bf16),
                pltpu.VMEM((room, 1), f32),
                pltpu.VMEM((room, 1), f32),
                pltpu.VMEM((blocks, high, rows), f32),
            ]
            + ([pltpu.VMEM((3, FF, D), f32)] if chunks > 1 else []),
        ),
        compiler_params=pltpu.CompilerParams(vmem_limit_bytes=58 << 20),
        cost_estimate=pl.CostEstimate(flops=1 << 20, bytes_accessed=1 << 20, transcendentals=0),
        name="experts",
    )(offsets.reshape(-1), counts.reshape(-1), rank, *x, *cot, *before, weights)
    return list(out[: 2 * blocks]), out[-1]


def angles(position):
    half = HD // 2
    frequency = rope_base ** (-jnp.arange(half, dtype=f32) * 2.0 / HD)
    angle = frequency[:, None] * position.astype(f32)[None, :]
    return jnp.cos(angle), jnp.sin(angle)


def rotate(values, cosine, sine):
    half = HD // 2
    parts = values.reshape(-1, HD, values.shape[1])
    first, second = parts[:, :half], parts[:, half:]
    return jnp.concatenate(
        [first * cosine - second * sine, second * cosine + first * sine], axis=1
    ).reshape(values.shape)


def doc_table(lengths, count):
    ends = jnp.cumsum(lengths)
    places = jnp.arange(count, dtype=jnp.int32)
    after = (places[None, :] >= ends[:, None]).astype(jnp.int32)
    starts = jnp.sum(after * lengths[:, None], axis=0)
    return (starts, places - starts)


def rank_table(choices, first, experts):
    named = (first + jnp.arange(experts, dtype=jnp.int32))[None, :, None, None]
    hits = jnp.any(choices[:, None, :, :] == named, axis=2)
    order = jnp.arange(choices.shape[2])
    before = (order[:, None] < order[None, :]).astype(bf16)
    rank = jnp.einsum("ber,rs->bes", hits.astype(bf16), before, preferred_element_type=f32)
    rank = jnp.where(hits, rank.astype(jnp.int32), -1)
    return rank, jnp.sum(hits.astype(jnp.int32), axis=2)


def shift(value, axis, step):
    size = lax.axis_size(axis)
    return lax.ppermute(value, axis, [(i, (i + step) % size) for i in range(size)])


def below(rows, values, parts):
    terms, rest = [], values.astype(f32)
    high = -(-values.shape[0] // 8) * 8
    rest = jnp.pad(rest, ((0, high - values.shape[0]), (0, D - values.shape[1])))
    for _ in range(parts):
        term = rest.astype(bf16)
        terms.append(term)
        rest = rest - term.astype(f32)
    if parts * high % 16:
        terms.append(jnp.zeros_like(term))
    return jnp.concatenate([rows] + terms, axis=0)


def total(values, axis):
    size = lax.axis_size(axis)
    distance = 1
    while distance < size:
        pairs = [(i, i ^ distance) for i in range(size)]
        other = [lax.ppermute(v, axis, pairs) for v in values]
        values = [(v.astype(f32) + o.astype(f32)).astype(v.dtype) for v, o in zip(values, other)]
        distance *= 2
    return values


def spread(values, axis):
    return lax.all_to_all(values, axis, split_axis=0, concat_axis=0, tiled=True)


def to_rows(values, ranks):
    width = values.shape[0]
    parts = values.reshape(width, ranks, -1).swapaxes(0, 1)
    return spread(parts, "tensor").reshape(ranks * width, -1)


def to_heads(values, ranks):
    parts = spread(values.reshape(ranks, -1, values.shape[1]), "tensor")
    return parts.swapaxes(0, 1).reshape(parts.shape[1], -1)


def adamw(weight, grad, first, second, rate, decay):
    first = beta_one * first + (1.0 - beta_one) * grad
    second = beta_two * second + (1.0 - beta_two) * grad * grad
    step = first / (1.0 - beta_one**STEP) / (jnp.sqrt(second / (1.0 - beta_two**STEP)) + adam_eps)
    return (first, second, weight - rate * (step + decay * weight))


def adamw_kernel(rate, weight_ref, grad_ref, first_ref, second_ref, *out_refs):
    out = adamw(
        weight_ref[...], grad_ref[...].astype(f32), first_ref[...], second_ref[...], rate, decay_rate
    )
    for ref, value in zip(out_refs, out):
        ref[...] = value


def adamw_rows(weight, grad, first, second, rate):
    block = pl.BlockSpec((weight.shape[0] // 4, weight.shape[1]), lambda i: (i, 0))
    return pl.pallas_call(
        partial(adamw_kernel, rate),
        out_shape=[jax.ShapeDtypeStruct(weight.shape, f32)] * 3,
        grid=(4,),
        in_specs=[block] * 4,
        out_specs=[block] * 3,
        compiler_params=pltpu.CompilerParams(vmem_limit_bytes=16 << 20),
        cost_estimate=pl.CostEstimate(flops=1 << 20, bytes_accessed=1 << 20, transcendentals=0),
        name="adamw",
    )(weight, grad, first, second)


def on_device(
    tokens,
    cotangent,
    doc_lengths,
    expert_choices,
    gains,
    gain_moment,
    gain_square,
    router,
    router_moment,
    router_square,
    w_attention,
    attention_moment,
    attention_square,
    w_out,
    out_moment,
    out_square,
    w_gate_up,
    gate_up_moment,
    gate_up_square,
    w_down,
    down_moment,
    down_square,
):
    ranks = lax.axis_size("tensor")
    peers = lax.axis_size("expert")
    rows = tokens.shape[0]
    group_rows = rows * ranks
    experts = w_gate_up.shape[0]
    blocks = min(peers, 4)
    halves = 2 if experts % 2 == 0 else 1
    half = experts // halves
    hidden = w_down.shape[1]

    inputs = tokens.astype(f32)
    scale_one = lax.rsqrt(jnp.mean(inputs * inputs, axis=-1, keepdims=True) + norm_eps)
    normed = (inputs * scale_one * gains[0]).astype(bf16)
    gathered = lax.all_gather(normed, "tensor", axis=0, tiled=True)

    attention_low = w_attention.reshape(D, -1).astype(bf16)
    out_low = w_out.reshape(-1, D).astype(bf16)
    expert_low = jnp.concatenate(
        [w_gate_up.swapaxes(2, 3).astype(bf16), w_down.astype(bf16)[:, None]], axis=1
    )
    out_all = lax.all_gather(out_low, "tensor", axis=0, tiled=True)
    expert_all = [
        lax.all_gather(expert_low[part * half : (part + 1) * half], "tensor", axis=2, tiled=True)
        for part in range(halves)
    ]

    attention_all = lax.all_gather(attention_low.T, "tensor", axis=0, tiled=True)

    message = below(cotangent, expert_choices.T, 1)
    messages = [shift(message, "expert", d) for d in range(1, peers)]

    start, position = doc_table(doc_lengths[0], group_rows)
    cosine, sine = angles(position)
    lowest = start[::QT] // KT
    start = start[None, :]
    projected = jnp.einsum("dc,td->ct", attention_low, gathered, preferred_element_type=f32)
    turned = rotate(projected[: (G + 1) * HD], cosine, sine).astype(bf16)
    queries = turned[: G * HD] * bf16(HD ** (-0.5))
    keys_t = turned[G * HD :]
    values_t = projected[(G + 1) * HD :].astype(bf16)
    keys, values = keys_t.T, values_t.T
    heads, log_sums = attention_forward(lowest, start, queries, keys, values_t)

    heads_rows, values, messages = lax.optimization_barrier(
        (to_rows(heads, ranks), values, messages)
    )
    cot_in = [cotangent] + messages
    choices_in = [expert_choices.T] + [
        m[rows : rows + TOPK, :rows].astype(jnp.int32) for m in messages
    ]
    attended = jnp.einsum("ct,cd->td", heads_rows, out_all, preferred_element_type=f32)
    state = inputs + attended
    scale_two = lax.rsqrt(jnp.mean(state * state, axis=-1, keepdims=True) + norm_eps)
    unit = state * scale_two
    normed_two = unit * gains[1]

    logits = lax.dot_general(router, normed_two, (((0,), (1,)), ((), ())), precision=highest)
    named = jnp.arange(EXPERTS, dtype=jnp.int32)[:, None, None]
    chosen = jnp.any(expert_choices.T[None, :, :] == named, axis=1)
    top = jnp.max(jnp.where(chosen, logits, -jnp.inf), axis=0, keepdims=True)
    weight = jnp.where(chosen, jnp.exp(jnp.where(chosen, logits - top, 0.0)), 0.0)
    gates = weight / jnp.sum(weight, axis=0, keepdims=True)

    me = lax.axis_index("expert")
    moved = normed_two.astype(bf16)
    by_peer = gates.reshape(peers, experts, rows)
    gates_to = [
        lax.dynamic_index_in_dim(by_peer, (me + d) % peers, 0, keepdims=False) for d in range(peers)
    ]
    high = -(-experts // 8) * 8
    x_in = [below(moved, gates_to[0], 2)]
    for d in range(1, peers):
        x_in.append(shift(below(moved, gates_to[d], 2), "expert", d))
    rank, counts = rank_table(jnp.stack(choices_in), me * experts, experts)

    def by_step(values):
        return values.reshape((-1, blocks) + values.shape[1:]).swapaxes(1, 2)

    def lay(values, height):
        if len(values) == blocks:
            return values
        return [jnp.concatenate([v[:height] for v in values[b::blocks]]) for b in range(blocks)]

    def unlay(values):
        if len(values) == peers:
            return values
        height = values[0].shape[0] * blocks // peers
        return [values[d % blocks][d // blocks * height :][:height] for d in range(peers)]

    rank_steps, count_steps = by_step(rank), by_step(counts)
    x_laid, cot_laid = lay(x_in, rows + 2 * high), lay(cot_in, rows)
    before, expert_grad = [], []
    for part in range(halves):
        own = slice(part * half, (part + 1) * half)
        before, grad_out = expert_layer(
            part,
            halves,
            rank_steps[:, own].reshape(-1, 1, blocks * rows),
            count_steps[:, own].reshape(-1, blocks),
            x_laid,
            cot_laid,
            before,
            expert_all[part],
            rows,
            high,
        )
        expert_grad.append(lax.psum_scatter(grad_out, "tensor", scatter_dimension=2, tiled=True))
    mixed_out, slot_out = unlay(before[:blocks]), unlay(before[blocks:])
    slot_out, attention_all = lax.optimization_barrier((slot_out, attention_all))
    slot_back = [slot_out[0]] + [shift(slot_out[d], "expert", -d) for d in range(1, peers)]
    slot_back, mixed_out = lax.optimization_barrier((slot_back, mixed_out))
    mixed_back = [mixed_out[0]] + [shift(mixed_out[d], "expert", -d) for d in range(1, peers)]

    gate_grads = jnp.concatenate(
        [
            v[rows : rows + experts, :rows].astype(f32)
            + v[rows + high : rows + high + experts, :rows].astype(f32)
            for v in slot_back
        ]
    )
    near_gates = jnp.concatenate(gates_to)
    near_router = jnp.roll(router.T.reshape(peers, experts, D), -me, axis=0).reshape(EXPERTS, D)
    logit_grads = near_gates * (
        gate_grads - jnp.sum(near_gates * gate_grads, axis=0, keepdims=True)
    )
    normed_two_grad = sum(v[:rows].astype(f32) for v in slot_back) + lax.dot_general(
        logit_grads, near_router, (((0,), (0,)), ((), ())), precision=highest
    )
    gain_two_grad = jnp.sum(normed_two_grad * unit, axis=0)
    unit_grad = normed_two_grad * gains[1]
    state_grad = cotangent.astype(f32) + scale_two * (
        unit_grad - unit * jnp.mean(unit_grad * unit, axis=-1, keepdims=True)
    )

    branch = state_grad.astype(bf16)
    head_grads_rows = jnp.einsum(
        "cd,td->ct", out_all, branch, preferred_element_type=f32
    ).astype(bf16)
    head_grads, expert_grad[0] = lax.optimization_barrier(
        (to_heads(head_grads_rows, ranks), expert_grad[0])
    )
    out_grad = jnp.einsum("ct,td->cd", heads_rows, branch, preferred_element_type=f32)
    out_grad = spread(out_grad.astype(bf16).reshape(ranks, -1, D), "tensor")
    query_grad, key_grad, value_grad = attention_backward(
        lowest, start, queries, heads, head_grads, log_sums, keys, keys_t, values
    )
    value_grad, out_grad, logit_grads = lax.optimization_barrier(
        (value_grad, out_grad, logit_grads)
    )
    out_grad = jnp.sum(out_grad.astype(f32), axis=0)
    router_grad = lax.dot_general(
        logit_grads, normed_two, (((1,), (0,)), ((), ())), precision=highest
    )
    router_grad = jnp.roll(router_grad.reshape(peers, experts, D), me, axis=0).reshape(EXPERTS, D)
    early = jnp.concatenate([router_grad, gain_two_grad[None]], axis=0)
    early = jnp.pad(early, ((0, -early.shape[0] % ranks), (0, 0))).reshape(ranks, -1, D)
    turned_grad = rotate(jnp.concatenate([query_grad, key_grad], axis=0), cosine, -sine)
    projected_grad = jnp.concatenate([turned_grad, value_grad], axis=0).astype(bf16)
    attention_grad = jnp.einsum(
        "td,ct->dc", gathered, projected_grad, preferred_element_type=f32
    )
    attention_grad, expert_grad = lax.optimization_barrier((attention_grad, expert_grad))
    gain_one_grad = (
        jnp.sum(attention_grad * attention_low.astype(f32), axis=1) / gains[0]
    )
    projected_late, expert_grad[-1] = lax.optimization_barrier(
        (projected_grad, expert_grad[-1])
    )
    projected_rows = to_rows(projected_late, ranks)
    projected_rows, early, gain_one_grad, mixed_back = lax.optimization_barrier(
        (projected_rows, early, gain_one_grad, mixed_back)
    )
    mixed = state + sum(v.astype(f32) for v in mixed_back)
    normed_grad = jnp.einsum(
        "ct,cd->td", projected_rows, attention_all, preferred_element_type=f32
    )
    attention_grad, out_grad = lax.psum(
        (attention_grad.astype(bf16), out_grad.astype(bf16)), "expert"
    )
    unit_one = inputs * scale_one
    unit_one_grad = normed_grad * gains[0]
    input_grad = state_grad + scale_one * (
        unit_one_grad - unit_one * jnp.mean(unit_one_grad * unit_one, axis=-1, keepdims=True)
    )

    early = jnp.sum(spread(early, "tensor"), axis=0)
    early = total([early], "expert")[0]
    early, attention_grad, out_grad = lax.optimization_barrier((early, attention_grad, out_grad))
    early = spread(jnp.broadcast_to(early[None], (ranks,) + early.shape), "tensor").reshape(-1, D)
    router_grad, gain_two_grad = early[:EXPERTS].T, early[EXPERTS]
    out_grad = out_grad.astype(f32).reshape(w_out.shape)
    gain_one_grad = total(total([gain_one_grad[None]], "expert"), "tensor")[0][0]
    gain_grad = jnp.stack([gain_one_grad, gain_two_grad])
    expert_grad = jnp.concatenate(expert_grad, axis=0).astype(f32)
    gate_up_grad, down_grad = expert_grad[:, :2], expert_grad[:, 2]
    gain_first, gain_second, gain_new = adamw(gains, gain_grad, gain_moment, gain_square, 1.0, 0.0)
    router_first, router_second, router_new = adamw(
        router, router_grad, router_moment, router_square, D ** (-0.5), decay_rate
    )
    attention_first, attention_second, attention_new = (
        v.reshape(w_attention.shape)
        for v in adamw_rows(
            w_attention.reshape(-1, 128),
            attention_grad.reshape(-1, 128),
            attention_moment.reshape(-1, 128),
            attention_square.reshape(-1, 128),
            2.0 * D ** (-0.5),
        )
    )
    out_first, out_second, out_new = adamw(
        w_out, out_grad, out_moment, out_square, 16.0 * (H * HD) ** (-0.5), decay_rate
    )
    gate_up_first, gate_up_second, gate_up_new = adamw(
        w_gate_up,
        gate_up_grad.swapaxes(2, 3),
        gate_up_moment,
        gate_up_square,
        2.0 * D ** (-0.5),
        decay_rate,
    )
    down_first, down_second, down_new = adamw(
        w_down, down_grad, down_moment, down_square, 8.0 * FF ** (-0.5), decay_rate
    )
    return (
        mixed,
        input_grad,
        gain_first,
        gain_second,
        gain_new,
        router_first,
        router_second,
        router_new,
        attention_first,
        attention_second,
        attention_new,
        out_first,
        out_second,
        out_new,
        gate_up_first,
        gate_up_second,
        gate_up_new,
        down_first,
        down_second,
        down_new,
    )


def solution(mesh):
    placed = (
        P(("expert", "tensor"), None),
        P(("expert", "tensor"), None),
        P("expert", None),
        P(("expert", "tensor"), None),
        P(),
        P(),
        P(),
        P(),
        P(),
        P(),
        P(None, "tensor", None),
        P(None, "tensor", None),
        P(None, "tensor", None),
        P("tensor", None, None),
        P("tensor", None, None),
        P("tensor", None, None),
        P("expert", None, None, "tensor"),
        P("expert", None, None, "tensor"),
        P("expert", None, None, "tensor"),
        P("expert", "tensor", None),
        P("expert", "tensor", None),
        P("expert", "tensor", None),
    )
    return jax.shard_map(
        on_device,
        mesh=mesh,
        in_specs=placed,
        out_specs=(
            P(("expert", "tensor"), None),
            P(("expert", "tensor"), None),
            P(),
            P(),
            P(),
            P(),
            P(),
            P(),
            P(None, "tensor", None),
            P(None, "tensor", None),
            P(None, "tensor", None),
            P("tensor", None, None),
            P("tensor", None, None),
            P("tensor", None, None),
            P("expert", None, None, "tensor"),
            P("expert", None, None, "tensor"),
            P("expert", None, None, "tensor"),
            P("expert", "tensor", None),
            P("expert", "tensor", None),
            P("expert", "tensor", None),
        ),
        check_vma=False,
    )
```

```python
from functools import partial

import jax
import jax.numpy as jnp
from jax import lax
from jax.experimental import pallas as pl
from jax.experimental.pallas import tpu as pltpu
from jax.sharding import PartitionSpec as P

D = 1024
H = 16
HD = 64
FF = 512
EXPERTS = 32
TOPK = 8
G = 2
STEP = 10

norm_eps = 1e-06
rope_base = 10000.0
masked_score = -1e30
beta_one = 0.9
beta_two = 0.95
adam_eps = 1e-08
decay_rate = 0.1
highest = lax.Precision.HIGHEST

QT = 256
KT = 256
RT = 256
CT = 512

f32 = jnp.float32
bf16 = jnp.bfloat16

NN = (((1,), (0,)), ((), ()))
NT = (((1,), (1,)), ((), ()))
TN = (((0,), (0,)), ((), ()))


def mm(a, b, dims):
    return lax.dot_general(a, b, dims, preferred_element_type=f32)


def attention_tile(j, i, start, k_ref):
    keys = k_ref[pl.ds(pl.multiple_of(j * KT, KT), KT), :]
    key_id = j * KT + lax.broadcasted_iota(jnp.int32, (KT, QT), 0)
    row_id = i * QT + lax.broadcasted_iota(jnp.int32, (KT, QT), 1)
    return keys, (key_id >= start) & (key_id <= row_id)


def attention_forward_kernel(low_ref, start_ref, q_ref, k_ref, v_ref, o_ref, sum_ref):
    i = pl.program_id(0)
    start = start_ref[...]

    def step(j, carry):
        keys, mask = attention_tile(j, i, start, k_ref)
        values = v_ref[:, pl.ds(pl.multiple_of(j * KT, KT), KT)]
        out = []
        for g in range(G):
            top, total, acc = carry[g]
            scores = mm(keys, q_ref[g * HD : (g + 1) * HD, :], NN)
            scores = jnp.where(mask, scores, masked_score)
            new_top = jnp.maximum(top, jnp.max(scores, axis=0, keepdims=True))
            probs = jnp.exp(scores - new_top)
            shrink = jnp.exp(top - new_top)
            total = total * shrink + jnp.sum(probs, axis=0, keepdims=True)
            acc = acc * shrink + mm(values, probs.astype(bf16), NN)
            out.append((new_top, total, acc))
        return tuple(out)

    zero = (
        jnp.full((1, QT), masked_score, f32),
        jnp.zeros((1, QT), f32),
        jnp.zeros((HD, QT), f32),
    )
    done = lax.fori_loop(low_ref[i], i + 1, step, (zero,) * G)
    for g in range(G):
        top, total, acc = done[g]
        o_ref[g * HD : (g + 1) * HD, :] = (acc / total).astype(bf16)
        sum_ref[g : g + 1, :] = top + jnp.log(total)


def attention_backward_kernel(
    low_ref, start_ref, q_ref, o_ref, d_ref, sum_ref, k_ref, kt_ref, v_ref, dq_ref, dk_ref, dv_ref
):
    i = pl.program_id(0)
    start = start_ref[...]

    @pl.when(i == 0)
    def _():
        dk_ref[...] = jnp.zeros_like(dk_ref)
        dv_ref[...] = jnp.zeros_like(dv_ref)

    grads, inner = [], []
    for g in range(G):
        part = slice(g * HD, (g + 1) * HD)
        grads.append(d_ref[part, :])
        inner.append(
            jnp.sum(d_ref[part, :].astype(f32) * o_ref[part, :].astype(f32), axis=0, keepdims=True)
        )

    def step(j, carry):
        keys, mask = attention_tile(j, i, start, k_ref)
        columns = pl.ds(pl.multiple_of(j * KT, KT), KT)
        values = v_ref[columns, :]
        keys_t = kt_ref[:, columns]
        dk = jnp.zeros((HD, KT), f32)
        dv = jnp.zeros((HD, KT), f32)
        out = []
        for g in range(G):
            query = q_ref[g * HD : (g + 1) * HD, :]
            scores = mm(keys, query, NN)
            probs = jnp.where(mask, jnp.exp(scores - sum_ref[g : g + 1, :]), 0.0)
            probs_grad = mm(values, grads[g], NN)
            score_grad = (probs * (probs_grad - inner[g])).astype(bf16)
            dv += mm(grads[g], probs.astype(bf16), NT)
            dk += mm(query, score_grad, NT)
            out.append(carry[g] + mm(keys_t, score_grad, NN))
        dk_ref[:, columns] += dk
        dv_ref[:, columns] += dv
        return tuple(out)

    done = lax.fori_loop(low_ref[i], i + 1, step, (jnp.zeros((HD, QT), f32),) * G)
    for g in range(G):
        dq_ref[g * HD : (g + 1) * HD, :] = done[g] * HD ** (-0.5)


def attention_forward(low, start, q, k, vt):
    rows = q.shape[1]
    tile = lambda height: pl.BlockSpec((height, QT), lambda i, s: (0, i))
    whole = lambda a: pl.BlockSpec(a.shape, lambda i, s: (0, 0))
    return pl.pallas_call(
        attention_forward_kernel,
        out_shape=(
            jax.ShapeDtypeStruct((G * HD, rows), bf16),
            jax.ShapeDtypeStruct((G, rows), f32),
        ),
        grid_spec=pltpu.PrefetchScalarGridSpec(
            num_scalar_prefetch=1,
            grid=(rows // QT,),
            in_specs=[tile(1), tile(G * HD), whole(k), whole(vt)],
            out_specs=[tile(G * HD), tile(G)],
        ),
        compiler_params=pltpu.CompilerParams(vmem_limit_bytes=24 << 20),
        cost_estimate=pl.CostEstimate(flops=1 << 20, bytes_accessed=1 << 20, transcendentals=0),
        name="attention_forward",
    )(low, start, q, k, vt)


def attention_backward(low, start, q, o, d, sums, k, kt, v):
    rows = q.shape[1]
    tile = lambda height: pl.BlockSpec((height, QT), lambda i, s: (0, i))
    whole = lambda a: pl.BlockSpec(a.shape, lambda i, s: (0, 0))
    return pl.pallas_call(
        attention_backward_kernel,
        out_shape=(
            jax.ShapeDtypeStruct((G * HD, rows), f32),
            jax.ShapeDtypeStruct((HD, rows), f32),
            jax.ShapeDtypeStruct((HD, rows), f32),
        ),
        grid_spec=pltpu.PrefetchScalarGridSpec(
            num_scalar_prefetch=1,
            grid=(rows // QT,),
            in_specs=[tile(1), tile(G * HD), tile(G * HD), tile(G * HD), tile(G)]
            + [whole(k), whole(kt), whole(v)],
            out_specs=[tile(G * HD), whole(kt), whole(kt)],
        ),
        compiler_params=pltpu.CompilerParams(vmem_limit_bytes=24 << 20),
        cost_estimate=pl.CostEstimate(flops=1 << 20, bytes_accessed=1 << 20, transcendentals=0),
        name="attention_backward",
    )(low, start, q, o, d, sums, k, kt, v)


def expert_kernel(blocks, rows, part, parts, offset_ref, count_ref, rank_ref, *refs):
    take = lambda n: (refs[:n], refs[n:])
    x_refs, refs = take(blocks)
    cot_refs, refs = take(blocks)
    mixed_before, refs = take(blocks if part else 0)
    slot_before, refs = take(blocks if part else 0)
    (w_ref,), refs = take(1)
    mixed_refs, refs = take(blocks)
    slot_refs, refs = take(blocks)
    w_grad_ref, mixed_acc, slot_acc, xs, cs, ps, ss, gates, gate_grads, tail = refs[:10]
    w_acc = refs[10] if len(refs) > 10 else None
    high = tail.shape[1]
    seg = rows // 2
    chunk, expert = pl.program_id(0), pl.program_id(1)
    step = chunk * pl.num_programs(1) + expert

    @pl.when(step == 0)
    def _():
        xs[...] = jnp.zeros_like(xs)
        cs[...] = jnp.zeros_like(cs)

    @pl.when(expert == 0)
    def _():
        tail[...] = jnp.zeros_like(tail)
        if part:
            for block in range(blocks):
                place = slice(block * rows, (block + 1) * rows)
                mixed_acc[place, :] = mixed_before[block][...].astype(f32)
                slot_acc[place, :] = slot_before[block][:rows, :].astype(f32)
        else:
            mixed_acc[...] = jnp.zeros_like(mixed_acc)
            slot_acc[...] = jnp.zeros_like(slot_acc)

    if w_acc is not None:

        @pl.when(chunk == 0)
        def _():
            w_acc[...] = jnp.zeros_like(w_acc)

    gates[...] = jnp.zeros_like(gates)
    own = part * pl.num_programs(1) + expert

    def gate_row(block):
        terms = x_refs[block][rows:, :rows].astype(f32)
        terms = terms[:high] + terms[high:]
        here = lax.broadcasted_iota(jnp.int32, (high, rows), 0) == own
        return jnp.sum(jnp.where(here, terms, 0.0), axis=0, keepdims=True)

    def picks(block):
        rank = rank_ref[0, :, block * rows : (block + 1) * rows]
        return lax.broadcasted_iota(jnp.int32, (seg, rows), 0) == rank

    for block in range(blocks):
        first = offset_ref[step * (blocks + 1) + block]
        count = count_ref[step * blocks + block]

        @pl.when(count > 0)
        def _():
            hit = picks(block)
            one = jnp.where(hit, 1.0, 0.0).astype(bf16)
            place = pl.ds(pl.multiple_of(first, 16), seg)
            xs[place, :] = mm(one, x_refs[block][:rows, :], NN).astype(bf16)
            cs[place, :] = mm(one, cot_refs[block][...], NN).astype(bf16)
            gates[place, :] = jnp.sum(jnp.where(hit, gate_row(block), 0.0), axis=1, keepdims=True)

    used = offset_ref[step * (blocks + 1) + blocks]

    def tile(t, carry):
        place = pl.ds(pl.multiple_of(t * RT, RT), RT)
        x, c, gate = xs[place, :], cs[place, :], gates[place, :]
        gate_pre = mm(x, w_ref[0, 0], NT)
        up_pre = mm(x, w_ref[0, 1], NT)
        sigmoid = jax.nn.sigmoid(gate_pre)
        active = gate_pre * sigmoid
        inner = active * up_pre
        plain = mm(c, w_ref[0, 2], NT)
        gate_grads[place, :] = jnp.sum(plain * inner, axis=1, keepdims=True)
        inner_grad = plain * gate
        gate_pre_grad = inner_grad * up_pre * sigmoid * (1.0 + gate_pre * (1.0 - sigmoid))
        ps[0, place, :] = gate_pre_grad.astype(bf16)
        ps[1, place, :] = (inner_grad * active).astype(bf16)
        ss[place, :] = (inner * gate).astype(bf16)
        return carry

    def back(t, carry):
        place = pl.ds(pl.multiple_of(t * RT, RT), RT)
        cs[place, :] = mm(ss[place, :], w_ref[0, 2], NN).astype(bf16)
        xs[place, :] = (
            mm(ps[0, place, :], w_ref[0, 0], NN) + mm(ps[1, place, :], w_ref[0, 1], NN)
        ).astype(bf16)
        return carry

    tiles = jnp.maximum((used + RT - 1) // RT, 1)
    lax.fori_loop(0, tiles, tile, 0)
    for n in range(1, xs.shape[0] // RT + 1):

        @pl.when(tiles == n)
        def _():
            place = slice(0, n * RT)
            for k, (left, right) in enumerate(((ps.at[0], xs), (ps.at[1], xs), (ss, cs))):
                for column in range(0, D, CT):
                    part_of = slice(column, column + CT)
                    grad = mm(left[place, :], right[place, part_of], TN)
                    if w_acc is None:
                        w_grad_ref[0, k, :, part_of] = grad.astype(bf16)
                    else:
                        w_acc[k, :, part_of] += grad

    if w_acc is not None:
        w_grad_ref[0] = w_acc[...].astype(bf16)
    lax.fori_loop(0, tiles, back, 0)

    for block in range(blocks):
        first = offset_ref[step * (blocks + 1) + block]
        count = count_ref[step * blocks + block]
        whole = slice(block * rows, (block + 1) * rows)

        @pl.when(count > 0)
        def _():
            hit = picks(block)
            one = jnp.where(hit, 1.0, 0.0).astype(bf16)
            place = pl.ds(pl.multiple_of(first, 16), seg)
            mixed_acc[whole, :] += mm(one, cs[place, :], TN)
            slot_acc[whole, :] += mm(one, xs[place, :], TN)
            tail[block, pl.ds(own, 1), :] = jnp.sum(
                jnp.where(hit, gate_grads[place, :], 0.0), axis=0, keepdims=True
            )

    @pl.when(expert == pl.num_programs(1) - 1)
    def _():
        for block in range(blocks):
            place = slice(block * rows, (block + 1) * rows)
            mixed_refs[block][...] = mixed_acc[place, :].astype(bf16)
            slot_refs[block][:rows, :] = slot_acc[place, :].astype(bf16)
            upper = tail[block].astype(bf16)
            lower = (tail[block] - upper.astype(f32)).astype(bf16)
            terms = jnp.concatenate([upper, lower], axis=0)
            if part:
                terms = terms + slot_before[block][rows:, :rows]
            slot_refs[block][rows:, :] = jnp.concatenate(
                [terms, jnp.zeros((2 * high, D - rows), bf16)], axis=1
            )


def expert_layer(part, parts, rank, counts, x, cot, before, weights, rows, high):
    experts, blocks = weights.shape[0], len(x)
    height = blocks * rows
    chunks = rank.shape[0] // experts
    padded = -(-counts // 16) * 16
    offsets = jnp.concatenate(
        [jnp.zeros((chunks * experts, 1), jnp.int32), jnp.cumsum(padded, axis=1)], axis=1
    )
    room = -(-blocks * (rows // 2) // RT) * RT
    tall = rows + 2 * high

    def tokens(h, **mode):
        return [pl.BlockSpec((h, D), lambda c, e, a, b: (c, 0), **mode) for _ in range(blocks)]

    held = dict(pipeline_mode=pl.Buffered(1))
    line = pl.BlockSpec((1, 1, height), lambda c, e, a, b: (c * experts + e, 0, 0))
    weight = lambda: pl.BlockSpec((1, 3, FF, D), lambda c, e, a, b: (e, 0, 0, 0))
    out = pl.pallas_call(
        partial(expert_kernel, blocks, rows, part, parts),
        out_shape=[jax.ShapeDtypeStruct((chunks * rows, D), bf16)] * blocks
        + [jax.ShapeDtypeStruct((chunks * tall, D), bf16)] * blocks
        + [jax.ShapeDtypeStruct(weights.shape, bf16)],
        grid_spec=pltpu.PrefetchScalarGridSpec(
            num_scalar_prefetch=2,
            grid=(chunks, experts),
            in_specs=[line]
            + tokens(tall, **held)
            + tokens(rows, **held)
            + (tokens(rows, **held) + tokens(tall, **held) if part else [])
            + [weight()],
            out_specs=tokens(rows) + tokens(tall) + [weight()],
            scratch_shapes=[
                pltpu.VMEM((height, D), f32),
                pltpu.VMEM((height, D), f32),
                pltpu.VMEM((room, D), bf16),
                pltpu.VMEM((room, D), bf16),
                pltpu.VMEM((2, room, FF), bf16),
                pltpu.VMEM((room, FF), bf16),
                pltpu.VMEM((room, 1), f32),
                pltpu.VMEM((room, 1), f32),
                pltpu.VMEM((blocks, high, rows), f32),
            ]
            + ([pltpu.VMEM((3, FF, D), f32)] if chunks > 1 else []),
        ),
        compiler_params=pltpu.CompilerParams(vmem_limit_bytes=58 << 20),
        cost_estimate=pl.CostEstimate(flops=1 << 20, bytes_accessed=1 << 20, transcendentals=0),
        name="experts",
    )(offsets.reshape(-1), counts.reshape(-1), rank, *x, *cot, *before, weights)
    return list(out[: 2 * blocks]), out[-1]


def angles(position):
    half = HD // 2
    frequency = rope_base ** (-jnp.arange(half, dtype=f32) * 2.0 / HD)
    angle = frequency[:, None] * position.astype(f32)[None, :]
    return jnp.cos(angle), jnp.sin(angle)


def rotate(values, cosine, sine):
    half = HD // 2
    parts = values.reshape(-1, HD, values.shape[1])
    first, second = parts[:, :half], parts[:, half:]
    return jnp.concatenate(
        [first * cosine - second * sine, second * cosine + first * sine], axis=1
    ).reshape(values.shape)


def doc_table(lengths, count):
    ends = jnp.cumsum(lengths)
    places = jnp.arange(count, dtype=jnp.int32)
    after = (places[None, :] >= ends[:, None]).astype(jnp.int32)
    starts = jnp.sum(after * lengths[:, None], axis=0)
    return (starts, places - starts)


def rank_table(choices, first, experts):
    named = (first + jnp.arange(experts, dtype=jnp.int32))[None, :, None, None]
    hits = jnp.any(choices[:, None, :, :] == named, axis=2)
    order = jnp.arange(choices.shape[2])
    before = (order[:, None] < order[None, :]).astype(bf16)
    rank = jnp.einsum("ber,rs->bes", hits.astype(bf16), before, preferred_element_type=f32)
    rank = jnp.where(hits, rank.astype(jnp.int32), -1)
    return rank, jnp.sum(hits.astype(jnp.int32), axis=2)


def shift(value, axis, step):
    size = lax.axis_size(axis)
    return lax.ppermute(value, axis, [(i, (i + step) % size) for i in range(size)])


def below(rows, values, parts):
    terms, rest = [], values.astype(f32)
    high = -(-values.shape[0] // 8) * 8
    rest = jnp.pad(rest, ((0, high - values.shape[0]), (0, D - values.shape[1])))
    for _ in range(parts):
        term = rest.astype(bf16)
        terms.append(term)
        rest = rest - term.astype(f32)
    if parts * high % 16:
        terms.append(jnp.zeros_like(term))
    return jnp.concatenate([rows] + terms, axis=0)


def total(values, axis):
    size = lax.axis_size(axis)
    distance = 1
    while distance < size:
        pairs = [(i, i ^ distance) for i in range(size)]
        other = [lax.ppermute(v, axis, pairs) for v in values]
        values = [(v.astype(f32) + o.astype(f32)).astype(v.dtype) for v, o in zip(values, other)]
        distance *= 2
    return values


def spread(values, axis):
    return lax.all_to_all(values, axis, split_axis=0, concat_axis=0, tiled=True)


def to_rows(values, ranks):
    width = values.shape[0]
    parts = values.reshape(width, ranks, -1).swapaxes(0, 1)
    return spread(parts, "tensor").reshape(ranks * width, -1)


def to_heads(values, ranks):
    parts = spread(values.reshape(ranks, -1, values.shape[1]), "tensor")
    return parts.swapaxes(0, 1).reshape(parts.shape[1], -1)


def adamw(weight, grad, first, second, rate, decay):
    first = beta_one * first + (1.0 - beta_one) * grad
    second = beta_two * second + (1.0 - beta_two) * grad * grad
    step = first / (1.0 - beta_one**STEP) / (jnp.sqrt(second / (1.0 - beta_two**STEP)) + adam_eps)
    return (first, second, weight - rate * (step + decay * weight))


def adamw_kernel(rate, weight_ref, grad_ref, first_ref, second_ref, *out_refs):
    out = adamw(
        weight_ref[...], grad_ref[...].astype(f32), first_ref[...], second_ref[...], rate, decay_rate
    )
    for ref, value in zip(out_refs, out):
        ref[...] = value


def adamw_rows(weight, grad, first, second, rate):
    block = pl.BlockSpec((weight.shape[0] // 4, weight.shape[1]), lambda i: (i, 0))
    return pl.pallas_call(
        partial(adamw_kernel, rate),
        out_shape=[jax.ShapeDtypeStruct(weight.shape, f32)] * 3,
        grid=(4,),
        in_specs=[block] * 4,
        out_specs=[block] * 3,
        compiler_params=pltpu.CompilerParams(vmem_limit_bytes=16 << 20),
        cost_estimate=pl.CostEstimate(flops=1 << 20, bytes_accessed=1 << 20, transcendentals=0),
        name="adamw",
    )(weight, grad, first, second)


def on_device(
    tokens,
    cotangent,
    doc_lengths,
    expert_choices,
    gains,
    gain_moment,
    gain_square,
    router,
    router_moment,
    router_square,
    w_attention,
    attention_moment,
    attention_square,
    w_out,
    out_moment,
    out_square,
    w_gate_up,
    gate_up_moment,
    gate_up_square,
    w_down,
    down_moment,
    down_square,
):
    ranks = lax.axis_size("tensor")
    peers = lax.axis_size("expert")
    rows = tokens.shape[0]
    group_rows = rows * ranks
    experts = w_gate_up.shape[0]
    blocks = min(peers, 4)
    halves = 2 if experts % 2 == 0 else 1
    half = experts // halves
    hidden = w_down.shape[1]

    inputs = tokens.astype(f32)
    scale_one = lax.rsqrt(jnp.mean(inputs * inputs, axis=-1, keepdims=True) + norm_eps)
    normed = (inputs * scale_one * gains[0]).astype(bf16)
    gathered = lax.all_gather(normed, "tensor", axis=0, tiled=True)

    attention_low = w_attention.reshape(D, -1).astype(bf16)
    out_low = w_out.reshape(-1, D).astype(bf16)
    expert_low = jnp.concatenate(
        [w_gate_up.swapaxes(2, 3).astype(bf16), w_down.astype(bf16)[:, None]], axis=1
    )
    out_all = lax.all_gather(out_low, "tensor", axis=0, tiled=True)
    expert_all = [
        lax.all_gather(expert_low[part * half : (part + 1) * half], "tensor", axis=2, tiled=True)
        for part in range(halves)
    ]

    attention_all = lax.all_gather(attention_low.T, "tensor", axis=0, tiled=True)

    message = below(cotangent, expert_choices.T, 1)
    messages = [shift(message, "expert", d) for d in range(1, peers)]

    start, position = doc_table(doc_lengths[0], group_rows)
    cosine, sine = angles(position)
    lowest = start[::QT] // KT
    start = start[None, :]
    projected = jnp.einsum("dc,td->ct", attention_low, gathered, preferred_element_type=f32)
    turned = rotate(projected[: (G + 1) * HD], cosine, sine).astype(bf16)
    queries = turned[: G * HD] * bf16(HD ** (-0.5))
    keys_t = turned[G * HD :]
    values_t = projected[(G + 1) * HD :].astype(bf16)
    keys, values = keys_t.T, values_t.T
    heads, log_sums = attention_forward(lowest, start, queries, keys, values_t)

    heads_rows, values, messages = lax.optimization_barrier(
        (to_rows(heads, ranks), values, messages)
    )
    cot_in = [cotangent] + messages
    choices_in = [expert_choices.T] + [
        m[rows : rows + TOPK, :rows].astype(jnp.int32) for m in messages
    ]
    attended = jnp.einsum("ct,cd->td", heads_rows, out_all, preferred_element_type=f32)
    state = inputs + attended
    scale_two = lax.rsqrt(jnp.mean(state * state, axis=-1, keepdims=True) + norm_eps)
    unit = state * scale_two
    normed_two = unit * gains[1]

    logits = lax.dot_general(router, normed_two, (((0,), (1,)), ((), ())), precision=highest)
    named = jnp.arange(EXPERTS, dtype=jnp.int32)[:, None, None]
    chosen = jnp.any(expert_choices.T[None, :, :] == named, axis=1)
    top = jnp.max(jnp.where(chosen, logits, -jnp.inf), axis=0, keepdims=True)
    weight = jnp.where(chosen, jnp.exp(jnp.where(chosen, logits - top, 0.0)), 0.0)
    gates = weight / jnp.sum(weight, axis=0, keepdims=True)

    me = lax.axis_index("expert")
    moved = normed_two.astype(bf16)
    by_peer = gates.reshape(peers, experts, rows)
    gates_to = [
        lax.dynamic_index_in_dim(by_peer, (me + d) % peers, 0, keepdims=False) for d in range(peers)
    ]
    high = -(-experts // 8) * 8
    x_in = [below(moved, gates_to[0], 2)]
    for d in range(1, peers):
        x_in.append(shift(below(moved, gates_to[d], 2), "expert", d))
    rank, counts = rank_table(jnp.stack(choices_in), me * experts, experts)

    def by_step(values):
        return values.reshape((-1, blocks) + values.shape[1:]).swapaxes(1, 2)

    def lay(values, height):
        if len(values) == blocks:
            return values
        return [jnp.concatenate([v[:height] for v in values[b::blocks]]) for b in range(blocks)]

    def unlay(values):
        if len(values) == peers:
            return values
        height = values[0].shape[0] * blocks // peers
        return [values[d % blocks][d // blocks * height :][:height] for d in range(peers)]

    rank_steps, count_steps = by_step(rank), by_step(counts)
    x_laid, cot_laid = lay(x_in, rows + 2 * high), lay(cot_in, rows)
    before, expert_grad = [], []
    for part in range(halves):
        own = slice(part * half, (part + 1) * half)
        before, grad_out = expert_layer(
            part,
            halves,
            rank_steps[:, own].reshape(-1, 1, blocks * rows),
            count_steps[:, own].reshape(-1, blocks),
            x_laid,
            cot_laid,
            before,
            expert_all[part],
            rows,
            high,
        )
        expert_grad.append(lax.psum_scatter(grad_out, "tensor", scatter_dimension=2, tiled=True))
    mixed_out, slot_out = unlay(before[:blocks]), unlay(before[blocks:])
    slot_out, attention_all = lax.optimization_barrier((slot_out, attention_all))
    slot_back = [slot_out[0]] + [shift(slot_out[d], "expert", -d) for d in range(1, peers)]
    slot_back, mixed_out = lax.optimization_barrier((slot_back, mixed_out))
    mixed_back = [mixed_out[0]] + [shift(mixed_out[d], "expert", -d) for d in range(1, peers)]

    gate_grads = jnp.concatenate(
        [
            v[rows : rows + experts, :rows].astype(f32)
            + v[rows + high : rows + high + experts, :rows].astype(f32)
            for v in slot_back
        ]
    )
    near_gates = jnp.concatenate(gates_to)
    near_router = jnp.roll(router.T.reshape(peers, experts, D), -me, axis=0).reshape(EXPERTS, D)
    logit_grads = near_gates * (
        gate_grads - jnp.sum(near_gates * gate_grads, axis=0, keepdims=True)
    )
    normed_two_grad = sum(v[:rows].astype(f32) for v in slot_back) + lax.dot_general(
        logit_grads, near_router, (((0,), (0,)), ((), ())), precision=highest
    )
    gain_two_grad = jnp.sum(normed_two_grad * unit, axis=0)
    unit_grad = normed_two_grad * gains[1]
    state_grad = cotangent.astype(f32) + scale_two * (
        unit_grad - unit * jnp.mean(unit_grad * unit, axis=-1, keepdims=True)
    )

    branch = state_grad.astype(bf16)
    head_grads_rows = jnp.einsum(
        "cd,td->ct", out_all, branch, preferred_element_type=f32
    ).astype(bf16)
    head_grads, expert_grad[0] = lax.optimization_barrier(
        (to_heads(head_grads_rows, ranks), expert_grad[0])
    )
    out_grad = jnp.einsum("ct,td->cd", heads_rows, branch, preferred_element_type=f32)
    out_grad = spread(out_grad.astype(bf16).reshape(ranks, -1, D), "tensor")
    query_grad, key_grad, value_grad = attention_backward(
        lowest, start, queries, heads, head_grads, log_sums, keys, keys_t, values
    )
    value_grad, out_grad, logit_grads = lax.optimization_barrier(
        (value_grad, out_grad, logit_grads)
    )
    out_grad = jnp.sum(out_grad.astype(f32), axis=0)
    router_grad = lax.dot_general(
        logit_grads, normed_two, (((1,), (0,)), ((), ())), precision=highest
    )
    router_grad = jnp.roll(router_grad.reshape(peers, experts, D), me, axis=0).reshape(EXPERTS, D)
    early = jnp.concatenate([router_grad, gain_two_grad[None]], axis=0)
    early = jnp.pad(early, ((0, -early.shape[0] % ranks), (0, 0))).reshape(ranks, -1, D)
    turned_grad = rotate(jnp.concatenate([query_grad, key_grad], axis=0), cosine, -sine)
    projected_grad = jnp.concatenate([turned_grad, value_grad], axis=0).astype(bf16)
    attention_grad = jnp.einsum(
        "td,ct->dc", gathered, projected_grad, preferred_element_type=f32
    )
    gain_one_grad = (
        jnp.sum(attention_grad * attention_low.astype(f32), axis=1) / gains[0]
    )
    projected_late, mixed_back = lax.optimization_barrier((projected_grad, mixed_back))
    projected_rows = to_rows(projected_late, ranks)
    projected_rows, early, gain_one_grad, expert_grad = lax.optimization_barrier(
        (projected_rows, early, gain_one_grad, expert_grad)
    )
    mixed = state + sum(v.astype(f32) for v in mixed_back)
    normed_grad = jnp.einsum(
        "ct,cd->td", projected_rows, attention_all, preferred_element_type=f32
    )
    attention_grad, out_grad = lax.psum(
        (attention_grad.astype(bf16), out_grad.astype(bf16)), "expert"
    )
    unit_one = inputs * scale_one
    unit_one_grad = normed_grad * gains[0]
    input_grad = state_grad + scale_one * (
        unit_one_grad - unit_one * jnp.mean(unit_one_grad * unit_one, axis=-1, keepdims=True)
    )

    early = jnp.sum(spread(early, "tensor"), axis=0)
    early = total([early], "expert")[0]
    early, attention_grad, out_grad = lax.optimization_barrier((early, attention_grad, out_grad))
    early = spread(jnp.broadcast_to(early[None], (ranks,) + early.shape), "tensor").reshape(-1, D)
    router_grad, gain_two_grad = early[:EXPERTS].T, early[EXPERTS]
    out_grad = out_grad.astype(f32).reshape(w_out.shape)
    gain_one_grad = total(total([gain_one_grad[None]], "expert"), "tensor")[0][0]
    gain_grad = jnp.stack([gain_one_grad, gain_two_grad])
    expert_grad = jnp.concatenate(expert_grad, axis=0).astype(f32)
    gate_up_grad, down_grad = expert_grad[:, :2], expert_grad[:, 2]
    gain_first, gain_second, gain_new = adamw(gains, gain_grad, gain_moment, gain_square, 1.0, 0.0)
    router_first, router_second, router_new = adamw(
        router, router_grad, router_moment, router_square, D ** (-0.5), decay_rate
    )
    attention_first, attention_second, attention_new = (
        v.reshape(w_attention.shape)
        for v in adamw_rows(
            w_attention.reshape(-1, 128),
            attention_grad.reshape(-1, 128),
            attention_moment.reshape(-1, 128),
            attention_square.reshape(-1, 128),
            2.0 * D ** (-0.5),
        )
    )
    out_first, out_second, out_new = adamw(
        w_out, out_grad, out_moment, out_square, 16.0 * (H * HD) ** (-0.5), decay_rate
    )
    gate_up_first, gate_up_second, gate_up_new = adamw(
        w_gate_up,
        gate_up_grad.swapaxes(2, 3),
        gate_up_moment,
        gate_up_square,
        2.0 * D ** (-0.5),
        decay_rate,
    )
    down_first, down_second, down_new = adamw(
        w_down, down_grad, down_moment, down_square, 8.0 * FF ** (-0.5), decay_rate
    )
    return (
        mixed,
        input_grad,
        gain_first,
        gain_second,
        gain_new,
        router_first,
        router_second,
        router_new,
        attention_first,
        attention_second,
        attention_new,
        out_first,
        out_second,
        out_new,
        gate_up_first,
        gate_up_second,
        gate_up_new,
        down_first,
        down_second,
        down_new,
    )


def solution(mesh):
    placed = (
        P(("expert", "tensor"), None),
        P(("expert", "tensor"), None),
        P("expert", None),
        P(("expert", "tensor"), None),
        P(),
        P(),
        P(),
        P(),
        P(),
        P(),
        P(None, "tensor", None),
        P(None, "tensor", None),
        P(None, "tensor", None),
        P("tensor", None, None),
        P("tensor", None, None),
        P("tensor", None, None),
        P("expert", None, None, "tensor"),
        P("expert", None, None, "tensor"),
        P("expert", None, None, "tensor"),
        P("expert", "tensor", None),
        P("expert", "tensor", None),
        P("expert", "tensor", None),
    )
    return jax.shard_map(
        on_device,
        mesh=mesh,
        in_specs=placed,
        out_specs=(
            P(("expert", "tensor"), None),
            P(("expert", "tensor"), None),
            P(),
            P(),
            P(),
            P(),
            P(),
            P(),
            P(None, "tensor", None),
            P(None, "tensor", None),
            P(None, "tensor", None),
            P("tensor", None, None),
            P("tensor", None, None),
            P("tensor", None, None),
            P("expert", None, None, "tensor"),
            P("expert", None, None, "tensor"),
            P("expert", None, None, "tensor"),
            P("expert", "tensor", None),
            P("expert", "tensor", None),
            P("expert", "tensor", None),
        ),
        check_vma=False,
    )
```
